512 devices in a mesh: cuts: 4 (over z_hi), fsdp: 8 (over x, z_lo), tensor: 16 (over y, core).
Axes of the slice: x: 4, y: 8, z: 8 (z_hi: 4, z_lo: 2; z = z_hi * 2 + z_lo), core: 2. Of those that a mesh axis runs over, the one named last changes fastest.
Arguments:
- tokens: bfloat16 [6144, 2304], P(('cuts', 'fsdp', 'tensor')), may hold values from -50 to 50
- norm_gain: float32 [2304], replicated, may hold values from 0.1 to 1.9
- gate_weight: bfloat16 [2304, 18432], P('fsdp', 'tensor'), may hold values from -0.125 to 0.125
- up_weight: bfloat16 [2304, 18432], P('fsdp', 'tensor'), may hold values from -0.125 to 0.125
- hidden_grad: bfloat16 [6144, 18432], P(('cuts', 'fsdp'), 'tensor'), may hold values from -1 to 1
Outputs:
- hidden: bfloat16 [6144, 18432], P(('cuts', 'fsdp'), 'tensor')
- input_grad: bfloat16 [6144, 2304], P(('cuts', 'fsdp', 'tensor'))
- gate_grad: float32 [2304, 18432], P(('fsdp', 'cuts'), 'tensor')
- up_grad: float32 [2304, 18432], P(('fsdp', 'cuts'), 'tensor')
The draws below stay inside these ranges and needn't reach their ends.
All inputs are finite; a program needn't handle non-finite values.
Results may differ from the reference program's by a relative error of at most 0.02.
Values may be sent and summed in bfloat16 or wider, within the bound.
No kernel may reach another device: no remote copies, remote signals or barrier semaphores. Data moves between devices by JAX's collectives and lax.ppermute only.
A program may use at most 64 MiB of HBM per device.

```python
import math
import jax
import jax.numpy as jnp
from jax import lax

D = 2304
FF = 18432
TOK_DEV = 192
TOKENS = 6144
N_CUTS = 4
N_FSDP = 8


def draw_tokens(key, part):
    key = jax.random.fold_in(key, 11)
    key_values, key_rows, key_cols = jax.random.split(key, 3)
    row_factor = jnp.exp(jax.random.uniform(key_rows, (TOKENS, 1), jnp.float32, math.log(0.3), math.log(3.0)))
    col_factor = jnp.exp(jax.random.uniform(key_cols, (1, D), jnp.float32, math.log(0.3), math.log(3.0)))
    values = jnp.clip(jax.random.normal(key_values, (TOKENS, D), jnp.float32), -5.0, 5.0) * row_factor * col_factor
    return values.astype(jnp.bfloat16)


def steps_of(own_key, extent, pieces, smallest, high):
    gain, own = 1.0, jax.random.fold_in(own_key, 6)
    for dim, blocks in pieces:
        steps = jnp.exp(jax.random.uniform(jax.random.fold_in(own, dim), (blocks,), jnp.float32, smallest / len(pieces), high / len(pieces)))
        gain = gain * jnp.repeat(steps, extent[dim] // blocks).reshape([-1 if axis == dim else 1 for axis in range(len(extent))])
    return gain


def noise(rng, dims, scale, bound, shards=(), kind=jnp.bfloat16):
    entries = jax.random.normal(rng, dims, jnp.float32) * scale
    if len(shards) > 0:
        entries = steps_of(rng, dims, shards, -0.22, 0.18) * entries
    return jnp.clip(entries, min=-bound, max=bound).astype(kind)


def setup_inputs(seed: int = 0) -> dict:
    seeds = jax.random.split(jax.random.key(seed), 6)
    return {
        "tokens": draw_tokens(jax.random.fold_in(seeds[5], 71), 0),
        "norm_gain": jnp.clip(1.0 + 0.18 * jax.random.normal(seeds[1], (D,), jnp.float32), 0.1, 1.9),
        "gate_weight": noise(seeds[2], (D, FF), D ** -0.5, 0.125, ((0, 8), (1, 16))),
        "up_weight": noise(seeds[3], (D, FF), D ** -0.5, 0.125, ((0, 8), (1, 16))),
        "hidden_grad": noise(seeds[4], (TOKENS, FF), 0.125, 1.0, ((0, 32), (1, 16))),
    }


ROOT_TWO_PI = 0.7978845608028654
CUBIC = 0.044715

def gelu_value(values):
    inside = ROOT_TWO_PI * (values + CUBIC * values * values * values)
    return 0.5 * values * (1.0 + jnp.tanh(inside))

def gelu_slope(values):
    inside = ROOT_TWO_PI * (values + CUBIC * values * values * values)
    tangent = jnp.tanh(inside)
    return 0.5 * (1.0 + tangent) + 0.5 * values * (1.0 - tangent * tangent) * ROOT_TWO_PI * (1.0 + 3.0 * CUBIC * values * values)

def per_slice(tokens, norm_gain, gate_weight, up_weight, hidden_grad):
    token_vals = tokens.astype(jnp.float32)
    width = tokens.shape[1]
    row_scale = lax.optimization_barrier(lax.rsqrt(lax.optimization_barrier(jnp.mean(token_vals * token_vals, axis=1)) + 1e-06).astype(jnp.bfloat16))
    scale_col = row_scale.astype(jnp.float32)[:, None]
    scaled = lax.optimization_barrier((token_vals * norm_gain).astype(jnp.bfloat16))
    gate = jnp.dot(scaled, gate_weight, preferred_element_type=jnp.float32) * scale_col
    upward = jnp.dot(scaled, up_weight, preferred_element_type=jnp.float32) * scale_col
    active = gelu_value(gate)
    hidden = (active * upward).astype(jnp.bfloat16)
    cotangent = hidden_grad.astype(jnp.float32) * scale_col
    gate_cot = (cotangent * upward * gelu_slope(gate)).astype(jnp.bfloat16)
    up_cot = (cotangent * active).astype(jnp.bfloat16)
    gate_term = jnp.dot(scaled.T, gate_cot, preferred_element_type=jnp.float32).astype(jnp.bfloat16)
    up_term = jnp.dot(scaled.T, up_cot, preferred_element_type=jnp.float32).astype(jnp.bfloat16)
    inner_grad = jnp.dot(gate_cot, gate_weight.T, preferred_element_type=jnp.float32) + jnp.dot(up_cot, up_weight.T, preferred_element_type=jnp.float32)
    inner = lax.optimization_barrier(jnp.sum(scaled.astype(jnp.float32) * inner_grad, axis=1))
    square = scale_col[:, 0] * scale_col[:, 0] / width
    input_grad = (norm_gain * inner_grad - square[:, None] * token_vals * inner[:, None]).astype(jnp.bfloat16)
    return (hidden, input_grad, gate_term, up_term)

def reference(tokens, norm_gain, gate_weight, up_weight, hidden_grad):
    slice_rows = TOK_DEV * N_FSDP
    hidden_parts = []
    input_parts = []
    gate_grad = jnp.zeros((D, FF), jnp.float32)
    up_grad = jnp.zeros((D, FF), jnp.float32)
    for slice_index in range(N_CUTS):
        first_row = slice_index * slice_rows
        results = per_slice(tokens[first_row:first_row + slice_rows], norm_gain, gate_weight, up_weight, hidden_grad[first_row:first_row + slice_rows])
        hidden_parts.append(results[0])
        input_parts.append(results[1])
        gate_grad = gate_grad + lax.optimization_barrier(results[2]).astype(jnp.float32)
        up_grad = up_grad + lax.optimization_barrier(results[3]).astype(jnp.float32)
    return (jnp.concatenate(hidden_parts, axis=0), jnp.concatenate(input_parts, axis=0), gate_grad, up_grad)
```

```python
import jax
import jax.numpy as jnp
from jax import lax
from jax.sharding import Mesh
from jax.sharding import PartitionSpec as P

ROOT_TWO_PI = 0.7978845608028654
CUBIC = 0.044715
BF16 = jnp.bfloat16
F32 = jnp.float32


def split_fsdp(mesh):
    cuts, fsdp, tensor = mesh.devices.shape
    return Mesh(
        mesh.devices.reshape(cuts, fsdp // 2, 2, tensor // 2, 2), ("c", "x", "l", "y", "k")
    )


def ring(size, shift):
    return [(i, (i + shift) % size) for i in range(size)]


def exchange(value, axis):
    return lax.all_to_all(value, axis, split_axis=0, concat_axis=0, tiled=True)


def make_step(nc, nx, nl, ny, nk):
    def per_device(tokens, norm_gain, gate_weight, up_weight, hidden_grad):
        rows, width = tokens.shape
        feats, units = gate_weight.shape
        part = units // nx
        own_tokens = hidden_grad.shape[0]
        pool = nx * own_tokens
        lo = lax.axis_index("l")
        core = lax.axis_index("k")

        token_vals = tokens.astype(F32)
        row_scale = lax.rsqrt(jnp.mean(token_vals * token_vals, axis=1) + 1e-06).astype(BF16)
        scale_own = row_scale.astype(F32)
        scaled = (token_vals * norm_gain).astype(BF16).astype(F32)
        normed = (scaled * scale_own[:, None]).astype(BF16)
        near = exchange(jnp.broadcast_to(normed[None], (nx, rows, width)), "x")
        near = near.reshape(nx * rows, width)
        table = lax.all_gather(near, ("y", "k"), axis=0, tiled=True)

        packed = jnp.concatenate(
            [gate_weight.reshape(feats, nx, part), up_weight.reshape(feats, nx, part)], axis=2
        ).transpose(1, 0, 2)
        grads = hidden_grad.reshape(2, own_tokens // 2, nx, part).transpose(2, 1, 0, 3)
        grads = grads.reshape(nx, own_tokens // 2, 2 * part)
        mixed = exchange(jnp.concatenate([packed, grads], axis=1), "x")
        weights = mixed[:, :feats]
        grads = mixed[:, feats:].reshape(nx, own_tokens // 2, 2, part).transpose(0, 2, 1, 3)
        grads = grads.reshape(nx, ny * nk, rows, part).transpose(1, 0, 2, 3).reshape(pool, part)
        nz = nc * nl
        half = nx // 2
        ahead = lax.ppermute(weights[:half], ("c", "l"), ring(nz, 1))
        back = lax.ppermute(weights[half:], ("c", "l"), ring(nz, -1))
        other = jnp.concatenate([ahead, back], axis=0)
        first = jnp.where(lo == 0, weights, other)
        second = jnp.where(lo == 0, other, weights)
        matrix = jnp.stack([first, second], axis=1).reshape(width, 2 * part)

        both = jnp.dot(table, matrix, preferred_element_type=F32)
        gate, upward = both[:, :part], both[:, part:]
        square = gate * gate
        tangent = jnp.tanh(ROOT_TWO_PI * (gate + CUBIC * square * gate))
        active = 0.5 * gate * (1.0 + tangent)
        slope = 0.5 * (1.0 + tangent) + 0.5 * gate * (1.0 - tangent * tangent) * ROOT_TWO_PI * (
            1.0 + 3.0 * CUBIC * square
        )
        cotangent = grads.astype(F32)
        hidden = (active * upward).astype(BF16)
        cots = jnp.concatenate(
            [(cotangent * upward * slope).astype(BF16), (cotangent * active).astype(BF16)], axis=1
        )

        partial = lax.dot_general(
            cots, matrix, (((1,), (1,)), ((), ())), preferred_element_type=F32
        ).astype(BF16)
        partial = partial.reshape(ny, nk, nx * rows, width)
        keep = lax.dynamic_index_in_dim(partial, core, 1, keepdims=False)
        give = lax.dynamic_index_in_dim(partial, 1 - core, 1, keepdims=False)
        taken = lax.ppermute(give, "k", [(0, 1), (1, 0)])

        grad = lax.dot_general(
            table, cots, (((0,), (0,)), ((), ())), preferred_element_type=F32
        ).astype(BF16)
        grad = grad.reshape(nx, nl, nc, feats // nc, 2 * part).transpose(2, 1, 0, 3, 4)
        grad = grad.reshape(nz * nx * (feats // nc), 2 * part)
        grad = lax.psum_scatter(grad, ("c", "l"), scatter_dimension=0, tiled=True)
        grad = grad.reshape(nx, feats // nc, 2 * part)

        partial = (keep.astype(F32) + taken.astype(F32)).astype(BF16)
        partial = exchange(partial, "y")
        partial = jnp.sum(partial.astype(F32), axis=0).astype(BF16)
        partial = partial.reshape(nx, rows, width)

        spread = hidden.reshape(ny * nk, nx, rows, part).transpose(1, 0, 2, 3)
        spread = spread.reshape(nx, own_tokens, part)
        spread = exchange(spread, "x")
        hidden = spread.transpose(1, 0, 2).reshape(own_tokens, units)
        inner_grad = jnp.sum(exchange(partial, "x").astype(F32), axis=0) * scale_own[:, None]
        inner = jnp.sum(scaled * inner_grad, axis=1)
        factor = scale_own * scale_own / width
        input_grad = (
            norm_gain * inner_grad - factor[:, None] * token_vals * inner[:, None]
        ).astype(BF16)
        grad = exchange(grad, "x").transpose(1, 0, 2).astype(F32)
        gate_grad = grad[:, :, :part].reshape(feats // nc, units)
        up_grad = grad[:, :, part:].reshape(feats // nc, units)
        return (hidden, input_grad, gate_grad, up_grad)

    return per_device


def solution(mesh):
    fine = split_fsdp(mesh)
    return jax.shard_map(
        make_step(*fine.devices.shape),
        mesh=fine,
        in_specs=(
            P(("c", "x", "l", "y", "k"), None),
            P(),
            P(("x", "l"), ("y", "k")),
            P(("x", "l"), ("y", "k")),
            P(("c", "x", "l"), ("y", "k")),
        ),
        out_specs=(
            P(("c", "x", "l"), ("y", "k")),
            P(("c", "x", "l", "y", "k"), None),
            P(("x", "l", "c"), ("y", "k")),
            P(("x", "l", "c"), ("y", "k")),
        ),
        check_vma=False,
    )
```

```python
import functools

import jax
import jax.numpy as jnp
from jax import lax
from jax.experimental import pallas as pl
from jax.experimental.pallas import tpu as pltpu
from jax.sharding import Mesh
from jax.sharding import PartitionSpec as P

ROOT_TWO_PI = 0.7978845608028654
CUBIC = 0.044715
BF16 = jnp.bfloat16
F32 = jnp.float32
VMEM = pl.BlockSpec(memory_space=pltpu.VMEM)
SMEM = pl.BlockSpec(memory_space=pltpu.SMEM)
ANY = pl.BlockSpec(memory_space=pl.ANY)


def split_fsdp(mesh):
    cuts, fsdp, tensor = mesh.devices.shape
    return Mesh(
        mesh.devices.reshape(cuts, fsdp // 2, 2, tensor // 2, 2), ("c", "x", "l", "y", "k")
    )


def ring(size, shift):
    return [(i, (i + shift) % size) for i in range(size)]


def exchange(value, axis):
    return lax.all_to_all(value, axis, split_axis=0, concat_axis=0, tiled=True)


def params(mib):
    return pltpu.CompilerParams(vmem_limit_bytes=mib * 1024 * 1024)


def share_sizes(units, parts):
    part = units // parts
    main = part // 128 * 128
    return main, part - main


def put_pair(out_ref, q, rows, a, b, main, tail, parts):
    out_ref[q, rows, 0:main] = a[:, q * main : (q + 1) * main]
    out_ref[q, rows, main : 2 * main] = b[:, q * main : (q + 1) * main]
    start = parts * main + q * tail
    out_ref[q, rows, 2 * main : 2 * main + tail] = a[:, start : start + tail]
    out_ref[q, rows, 2 * main + tail : 2 * (main + tail)] = b[:, start : start + tail]


def pack_weights_kernel(main, tail, parts, gate_ref, up_ref, out_ref):
    feats = gate_ref.shape[0]
    for q in range(parts):
        put_pair(out_ref, q, slice(0, feats), gate_ref, up_ref, main, tail, parts)


def pack_all_kernel(main, tail, parts, gate_ref, up_ref, grad_ref, out_ref):
    feats = gate_ref.shape[0]
    half = grad_ref.shape[0] // 2
    for q in range(parts):
        put_pair(out_ref, q, slice(0, feats), gate_ref, up_ref, main, tail, parts)
        put_pair(
            out_ref, q, slice(feats, feats + half),
            grad_ref.at[0:half], grad_ref.at[half : 2 * half], main, tail, parts,
        )


def pack(parts, gate, up, grads=None):
    feats, units = gate.shape
    main, tail = share_sizes(units, parts)
    operands = (gate, up) if grads is None else (gate, up, grads)
    rows = feats if grads is None else feats + grads.shape[0] // 2
    kernel = pack_weights_kernel if grads is None else pack_all_kernel
    return pl.pallas_call(
        functools.partial(kernel, main, tail, parts),
        out_shape=jax.ShapeDtypeStruct((parts, rows, 2 * (main + tail)), BF16),
        in_specs=[VMEM] * len(operands),
        out_specs=VMEM,
        compiler_params=params(24),
        cost_estimate=pl.CostEstimate(flops=0, bytes_accessed=4 * parts * rows * (main + tail), transcendentals=0),
    )(*operands)


def activate(gate, upward, cotangent):
    square = gate * gate
    tangent = jnp.tanh(ROOT_TWO_PI * (gate + CUBIC * square * gate))
    active = 0.5 * gate * (1.0 + tangent)
    slope = 0.5 * (1.0 + tangent) + 0.5 * gate * (1.0 - tangent * tangent) * ROOT_TWO_PI * (
        1.0 + 3.0 * CUBIC * square
    )
    hidden = (active * upward).astype(BF16)
    return hidden, (cotangent * upward * slope).astype(BF16), (cotangent * active).astype(BF16)


def forward_kernel(
    chunk, main, tail, place_ref, table_ref, own_ref, other_ref, grads_ref,
    hidden_ref, cots_ref, keep_ref, give_ref, matrix, sems,
):
    blocks, feats, _ = other_ref.shape
    low, core = place_ref[0], place_ref[1]
    copies = []
    for x in range(blocks):
        for i, (src, at) in enumerate(((own_ref, low), (other_ref, 1 - low))):
            rows = pl.ds(pl.multiple_of((2 * x + at) * feats, 16), feats)
            copies.append(
                pltpu.make_async_copy(
                    src.at[x, pl.ds(0, feats)], matrix.at[rows], sems.at[2 * x + i]
                )
            )
    for copy in copies:
        copy.start()
    for copy in copies:
        copy.wait()
    step = keep_ref.shape[1]
    for first in range(0, table_ref.shape[0], chunk):
        rows = slice(first, first + chunk)
        both = jnp.dot(table_ref[rows, :], matrix[...], preferred_element_type=F32)
        grads = grads_ref[rows, :].astype(F32)
        hidden, gate_cot, up_cot = activate(
            both[:, :main], both[:, main : 2 * main], grads[:, :main]
        )
        hidden_ref[rows, :main] = hidden
        cots_ref[rows, :main] = gate_cot
        cots_ref[rows, main : 2 * main] = up_cot
        rest = both[:, 2 * main :]
        hidden, gate_cot, up_cot = activate(rest[:, :tail], rest[:, tail:], grads[:, main:])
        hidden_ref[rows, main:] = hidden
        cots_ref[rows, 2 * main : 2 * main + tail] = gate_cot
        cots_ref[rows, 2 * main + tail :] = up_cot
        partial = lax.dot_general(
            cots_ref[rows, :], matrix[...], (((1,), (1,)), ((), ())), preferred_element_type=F32
        )
        for j in range(chunk // (2 * step)):
            even = partial[2 * j * step : (2 * j + 1) * step]
            odd = partial[(2 * j + 1) * step : (2 * j + 2) * step]
            y = first // (2 * step) + j
            keep_ref[y] = jnp.where(core == 0, even, odd).astype(BF16)
            give_ref[y] = jnp.where(core == 0, odd, even).astype(BF16)


def forward(place, table, own, other, grads, ny, chunk):
    pool, width = table.shape
    pair = other.shape[2]
    part = pair // 2
    main = part // 128 * 128
    step = pool // (2 * ny)
    return pl.pallas_call(
        functools.partial(forward_kernel, chunk, main, part - main),
        out_shape=(
            jax.ShapeDtypeStruct((pool, part), BF16),
            jax.ShapeDtypeStruct((pool, pair), BF16),
            jax.ShapeDtypeStruct((ny, step, width), BF16),
            jax.ShapeDtypeStruct((ny, step, width), BF16),
        ),
        in_specs=[SMEM, VMEM, ANY, ANY, VMEM],
        out_specs=(VMEM, VMEM, VMEM, VMEM),
        scratch_shapes=[
            pltpu.VMEM((width, pair), BF16),
            pltpu.SemaphoreType.DMA((2 * other.shape[0],)),
        ],
        compiler_params=params(48),
        cost_estimate=pl.CostEstimate(
            flops=4 * pool * width * pair, bytes_accessed=2 * (2 * pool * width + width * pair), transcendentals=0
        ),
    )(place, table, own, other, grads)


def gradient_kernel(tile, nx, nl, nc, table_ref, cots_ref, out_ref, total):
    width = table_ref.shape[1]
    for first in range(0, width, tile):
        total[first : first + tile, :] = lax.dot_general(
            table_ref[:, first : first + tile], cots_ref[...], (((0,), (0,)), ((), ())),
            preferred_element_type=F32,
        )
    piece = width // (nx * nl * nc)
    block = nx * piece
    for c in range(nc):
        for l in range(nl):
            found = [
                total[((x * nl + l) * nc + c) * piece : ((x * nl + l) * nc + c + 1) * piece, :]
                for x in range(nx)
            ]
            z = c * nl + l
            out_ref[z * block : (z + 1) * block, :] = jnp.concatenate(found, axis=0).astype(BF16)


def gradient(table, cots, nx, nl, nc, tile):
    pool, width = table.shape
    pair = cots.shape[1]
    return pl.pallas_call(
        functools.partial(gradient_kernel, tile, nx, nl, nc),
        out_shape=jax.ShapeDtypeStruct((width, pair), BF16),
        in_specs=[VMEM, VMEM],
        out_specs=VMEM,
        scratch_shapes=[pltpu.VMEM((width, pair), F32)],
        compiler_params=params(48),
        cost_estimate=pl.CostEstimate(
            flops=2 * pool * width * pair, bytes_accessed=2 * (pool * width + width * pair), transcendentals=0
        ),
    )(table, cots)


def swap_over_x(pieces, nx):
    me = lax.axis_index("x")
    got = [lax.dynamic_index_in_dim(pieces, me, 0, keepdims=False)]
    for shift in range(1, nx):
        piece = lax.dynamic_index_in_dim(pieces, lax.rem(me + shift, nx), 0, keepdims=False)
        got.append(lax.ppermute(piece, "x", ring(nx, shift)))
    return got


def make_step(nc, nx, nl, ny, nk):
    def per_device(tokens, norm_gain, gate_weight, up_weight, hidden_grad):
        rows, width = tokens.shape
        feats, units = gate_weight.shape
        main, tail = share_sizes(units, nx)
        part = main + tail
        own_tokens = hidden_grad.shape[0]
        half = own_tokens // 2
        pool = nx * own_tokens
        nz = nc * nl
        place = jnp.stack([lax.axis_index("l"), lax.axis_index("k")]).astype(jnp.int32)

        token_vals = tokens.astype(F32)
        row_scale = lax.rsqrt(jnp.mean(token_vals * token_vals, axis=1) + 1e-06).astype(BF16)
        scale_own = row_scale.astype(F32)
        scaled = (token_vals * norm_gain).astype(BF16).astype(F32)
        normed = (scaled * scale_own[:, None]).astype(BF16)
        near = exchange(jnp.broadcast_to(normed[None], (nx, rows, width)), "x")
        near = near.reshape(nx * rows, width)
        table = lax.all_gather(near, ("y", "k"), axis=0, tiled=True)

        other_gate = lax.ppermute(gate_weight, ("c", "l"), ring(nz, 1))
        other_up = lax.ppermute(up_weight, ("c", "l"), ring(nz, -1))
        own = exchange(pack(nx, gate_weight, up_weight, hidden_grad), "x")
        other = exchange(pack(nx, other_gate, other_up), "x")
        grads = own[:, feats:]
        grads = jnp.stack(
            [
                jnp.concatenate(
                    [
                        grads[:, :, h * main : (h + 1) * main],
                        grads[:, :, 2 * main + h * tail : 2 * main + (h + 1) * tail],
                    ],
                    axis=2,
                )
                for h in range(2)
            ],
            axis=1,
        )
        grads = grads.reshape(nx, ny * nk, rows, part).transpose(1, 0, 2, 3).reshape(pool, part)

        hidden, cots, keep, give = forward(place, table, own, other, grads, ny, pool // 2)
        taken = lax.ppermute(give, "k", [(0, 1), (1, 0)])
        grad = gradient(table, cots, nx, nl, nc, width // 3)
        grad = lax.psum_scatter(grad, ("c", "l"), scatter_dimension=0, tiled=True)
        grad = grad.reshape(nx, feats // nc, 2 * part)

        partial = (keep.astype(F32) + taken.astype(F32)).astype(BF16)
        partial = exchange(partial, "y")
        partial = jnp.sum(partial.astype(F32), axis=0).astype(BF16).reshape(nx, rows, width)
        inner_grad = sum(piece.astype(F32) for piece in swap_over_x(partial, nx))
        inner_grad = inner_grad * scale_own[:, None]
        inner = jnp.sum(scaled * inner_grad, axis=1)
        factor = scale_own * scale_own / width
        input_grad = (
            norm_gain * inner_grad - factor[:, None] * token_vals * inner[:, None]
        ).astype(BF16)

        def ordered(pieces):
            me = lax.axis_index("x")
            stacked = jnp.stack(pieces)
            return [
                lax.dynamic_index_in_dim(stacked, lax.rem(me - q + nx, nx), 0, keepdims=False)
                for q in range(nx)
            ]

        spread = hidden.reshape(ny * nk, nx, rows, part).transpose(1, 0, 2, 3)
        spread = ordered(swap_over_x(spread.reshape(nx, own_tokens, part), nx))
        hidden = jnp.concatenate(
            [p[:, :main] for p in spread] + [p[:, main:] for p in spread], axis=1
        )
        grad = [p.astype(F32) for p in ordered(swap_over_x(grad, nx))]
        gate_grad = jnp.concatenate(
            [p[:, :main] for p in grad] + [p[:, 2 * main : 2 * main + tail] for p in grad], axis=1
        )
        up_grad = jnp.concatenate(
            [p[:, main : 2 * main] for p in grad] + [p[:, 2 * main + tail :] for p in grad], axis=1
        )
        return (hidden, input_grad, gate_grad, up_grad)

    return per_device


def solution(mesh):
    fine = split_fsdp(mesh)
    return jax.shard_map(
        make_step(*fine.devices.shape),
        mesh=fine,
        in_specs=(
            P(("c", "x", "l", "y", "k"), None),
            P(),
            P(("x", "l"), ("y", "k")),
            P(("x", "l"), ("y", "k")),
            P(("c", "x", "l"), ("y", "k")),
        ),
        out_specs=(
            P(("c", "x", "l"), ("y", "k")),
            P(("c", "x", "l", "y", "k"), None),
            P(("x", "l", "c"), ("y", "k")),
            P(("x", "l", "c"), ("y", "k")),
        ),
        check_vma=False,
    )
```

```python
import functools

import jax
import jax.numpy as jnp
from jax import lax
from jax.experimental import pallas as pl
from jax.experimental.pallas import tpu as pltpu
from jax.sharding import Mesh
from jax.sharding import PartitionSpec as P

ROOT_TWO_PI = 0.7978845608028654
CUBIC = 0.044715
BF16 = jnp.bfloat16
F32 = jnp.float32
VMEM = pl.BlockSpec(memory_space=pltpu.VMEM)
SMEM = pl.BlockSpec(memory_space=pltpu.SMEM)
ANY = pl.BlockSpec(memory_space=pl.ANY)


def split_fsdp(mesh):
    cuts, fsdp, tensor = mesh.devices.shape
    return Mesh(
        mesh.devices.reshape(cuts, fsdp // 2, 2, tensor // 2, 2), ("c", "x", "l", "y", "k")
    )


def ring(size, shift):
    return [(i, (i + shift) % size) for i in range(size)]


def exchange(value, axis):
    return lax.all_to_all(value, axis, split_axis=0, concat_axis=0, tiled=True)


def params(mib):
    return pltpu.CompilerParams(vmem_limit_bytes=mib * 1024 * 1024)


def share_sizes(units, parts):
    part = units // parts
    main = part // 128 * 128
    return main, part - main


def put_pair(out_ref, q, rows, a, b, main, tail, parts):
    out_ref[q, rows, 0:main] = a[:, q * main : (q + 1) * main]
    out_ref[q, rows, main : 2 * main] = b[:, q * main : (q + 1) * main]
    start = parts * main + q * tail
    out_ref[q, rows, 2 * main : 2 * main + tail] = a[:, start : start + tail]
    out_ref[q, rows, 2 * main + tail : 2 * (main + tail)] = b[:, start : start + tail]


def pack_weights_kernel(main, tail, parts, gate_ref, up_ref, out_ref):
    feats = gate_ref.shape[0]
    for q in range(parts):
        put_pair(out_ref, q, slice(0, feats), gate_ref, up_ref, main, tail, parts)


def pack_all_kernel(main, tail, parts, gate_ref, up_ref, grad_ref, out_ref):
    feats = gate_ref.shape[0]
    half = grad_ref.shape[0] // 2
    for q in range(parts):
        put_pair(out_ref, q, slice(0, feats), gate_ref, up_ref, main, tail, parts)
        put_pair(
            out_ref, q, slice(feats, feats + half),
            grad_ref.at[0:half], grad_ref.at[half : 2 * half], main, tail, parts,
        )


def pack(parts, gate, up, grads=None):
    feats, units = gate.shape
    main, tail = share_sizes(units, parts)
    operands = (gate, up) if grads is None else (gate, up, grads)
    rows = feats if grads is None else feats + grads.shape[0] // 2
    kernel = pack_weights_kernel if grads is None else pack_all_kernel
    return pl.pallas_call(
        functools.partial(kernel, main, tail, parts),
        out_shape=jax.ShapeDtypeStruct((parts, rows, 2 * (main + tail)), BF16),
        in_specs=[VMEM] * len(operands),
        out_specs=VMEM,
        compiler_params=params(24),
        cost_estimate=pl.CostEstimate(flops=0, bytes_accessed=4 * parts * rows * (main + tail), transcendentals=0),
    )(*operands)


def activate(gate, upward, cotangent):
    square = gate * gate
    tangent = jnp.tanh(ROOT_TWO_PI * (gate + CUBIC * square * gate))
    active = 0.5 * gate * (1.0 + tangent)
    slope = 0.5 * (1.0 + tangent) + 0.5 * gate * (1.0 - tangent * tangent) * ROOT_TWO_PI * (
        1.0 + 3.0 * CUBIC * square
    )
    hidden = (active * upward).astype(BF16)
    return hidden, (cotangent * upward * slope).astype(BF16), (cotangent * active).astype(BF16)


def split_index(value, size, top):
    factor = (1 << 20) // size + 1
    assert all(i * factor >> 20 == i // size for i in range(top))
    high = (value * factor) >> 20
    return high, value - high * size


def shuffle(pool, outer, inner, rows):
    index = lax.broadcasted_iota(jnp.int32, (pool, 1), 0)
    high, rest = split_index(index, inner * rows, pool)
    mid, low = split_index(rest, rows, inner * rows)
    source = mid * (outer * rows) + high * rows + low
    columns = lax.broadcasted_iota(jnp.int32, (pool, pool), 1)
    return (columns == source).astype(F32).astype(BF16)


def forward_kernel(
    chunk, main, tail, rows_each, place_ref, table_any, own_ref, other_ref,
    hidden_ref, cots_ref, keep_ref, give_ref, table_ref, matrix, raw, grads_ref, found, sems,
):
    blocks, feats, _ = other_ref.shape
    pool = table_ref.shape[0]
    half = raw.shape[1]
    low, core = place_ref[0], place_ref[1]
    grads_copy = pltpu.make_async_copy(own_ref.at[:, pl.ds(feats, half)], raw, sems.at[2 * blocks])
    grads_copy.start()
    copies = []
    for x in range(blocks):
        for i, (src, at) in enumerate(((own_ref, low), (other_ref, 1 - low))):
            rows = pl.ds(pl.multiple_of((2 * x + at) * feats, 16), feats)
            copies.append(
                pltpu.make_async_copy(
                    src.at[x, pl.ds(0, feats)], matrix.at[rows], sems.at[2 * x + i]
                )
            )
    tables = [
        pltpu.make_async_copy(
            table_any.at[pl.ds(first, chunk)], table_ref.at[pl.ds(first, chunk)],
            sems.at[2 * blocks + 1 + first // chunk],
        )
        for first in range(0, pool, chunk)
    ]
    tables[0].start()
    for copy in copies:
        copy.start()
    for copy in tables[1:]:
        copy.start()
    groups = pool // (blocks * rows_each)
    forth = shuffle(pool, groups, blocks, rows_each)
    back = shuffle(pool, blocks, groups, rows_each)
    grads_copy.wait()
    for x in range(blocks):
        for h in range(2):
            rows = slice((2 * x + h) * half, (2 * x + h + 1) * half)
            grads_ref[rows, :main] = raw[x, :, h * main : (h + 1) * main]
            grads_ref[rows, main:] = raw[x, :, 2 * main + h * tail : 2 * main + (h + 1) * tail]
    for copy in copies:
        copy.wait()
    step = keep_ref.shape[1]
    for first in range(0, pool, chunk):
        rows = slice(first, first + chunk)
        tables[first // chunk].wait()
        both = jnp.dot(table_ref[rows, :], matrix[...], preferred_element_type=F32)
        grads = jnp.dot(forth[rows, :], grads_ref[...], preferred_element_type=F32)
        hidden, gate_cot, up_cot = activate(
            both[:, :main], both[:, main : 2 * main], grads[:, :main]
        )
        found[rows, :main] = hidden
        cots_ref[rows, :main] = gate_cot
        cots_ref[rows, main : 2 * main] = up_cot
        rest = both[:, 2 * main :]
        hidden, gate_cot, up_cot = activate(rest[:, :tail], rest[:, tail:], grads[:, main:])
        found[rows, main:] = hidden
        cots_ref[rows, 2 * main : 2 * main + tail] = gate_cot
        cots_ref[rows, 2 * main + tail :] = up_cot
        partial = lax.dot_general(
            cots_ref[rows, :], matrix[...], (((1,), (1,)), ((), ())), preferred_element_type=F32
        )
        for j in range(chunk // (2 * step)):
            even = partial[2 * j * step : (2 * j + 1) * step]
            odd = partial[(2 * j + 1) * step : (2 * j + 2) * step]
            y = first // (2 * step) + j
            keep_ref[y] = jnp.where(core == 0, even, odd).astype(BF16)
            give_ref[y] = jnp.where(core == 0, odd, even).astype(BF16)
    spread = jnp.dot(back, found[...], preferred_element_type=F32).astype(BF16)
    for x in range(blocks):
        for h in range(2):
            rows = slice((2 * x + h) * half, (2 * x + h + 1) * half)
            hidden_ref[x, :, h * main : (h + 1) * main] = spread[rows, :main]
            hidden_ref[x, :, 2 * main + h * tail : 2 * main + (h + 1) * tail] = spread[rows, main:]


def forward(place, table, own, other, ny, rows_each, chunk):
    pool, width = table.shape
    blocks, feats, pair = other.shape
    part = pair // 2
    main = part // 128 * 128
    step = pool // (2 * ny)
    half = own.shape[1] - feats
    return pl.pallas_call(
        functools.partial(forward_kernel, chunk, main, part - main, rows_each),
        out_shape=(
            jax.ShapeDtypeStruct((blocks, half, pair), BF16),
            jax.ShapeDtypeStruct((pool, pair), BF16),
            jax.ShapeDtypeStruct((ny, step, width), BF16),
            jax.ShapeDtypeStruct((ny, step, width), BF16),
        ),
        in_specs=[SMEM, ANY, ANY, ANY],
        out_specs=(VMEM, VMEM, VMEM, VMEM),
        scratch_shapes=[
            pltpu.VMEM((pool, width), BF16),
            pltpu.VMEM((width, pair), BF16),
            pltpu.VMEM((blocks, half, pair), BF16),
            pltpu.VMEM((pool, part), BF16),
            pltpu.VMEM((pool, part), BF16),
            pltpu.SemaphoreType.DMA((2 * blocks + 1 + pool // chunk,)),
        ],
        compiler_params=params(48),
        cost_estimate=pl.CostEstimate(
            flops=4 * pool * width * pair, bytes_accessed=2 * (2 * pool * width + width * pair), transcendentals=0
        ),
    )(place, table, own, other)


def gradient_kernel(tile, nx, nl, nc, table_ref, cots_ref, out_ref, total):
    width = table_ref.shape[1]
    for first in range(0, width, tile):
        total[first : first + tile, :] = lax.dot_general(
            table_ref[:, first : first + tile], cots_ref[...], (((0,), (0,)), ((), ())),
            preferred_element_type=F32,
        )
    piece = width // (nx * nl * nc)
    block = nx * piece
    for c in range(nc):
        for l in range(nl):
            found = [
                total[((x * nl + l) * nc + c) * piece : ((x * nl + l) * nc + c + 1) * piece, :]
                for x in range(nx)
            ]
            z = c * nl + l
            out_ref[z * block : (z + 1) * block, :] = jnp.concatenate(found, axis=0).astype(BF16)


def gradient(table, cots, nx, nl, nc, tile):
    pool, width = table.shape
    pair = cots.shape[1]
    return pl.pallas_call(
        functools.partial(gradient_kernel, tile, nx, nl, nc),
        out_shape=jax.ShapeDtypeStruct((width, pair), BF16),
        in_specs=[VMEM, VMEM],
        out_specs=VMEM,
        scratch_shapes=[pltpu.VMEM((width, pair), F32)],
        compiler_params=params(48),
        cost_estimate=pl.CostEstimate(
            flops=2 * pool * width * pair, bytes_accessed=2 * (pool * width + width * pair), transcendentals=0
        ),
    )(table, cots)


def swap_over_x(pieces, nx):
    me = lax.axis_index("x")
    got = [lax.dynamic_index_in_dim(pieces, me, 0, keepdims=False)]
    for shift in range(1, nx):
        piece = lax.dynamic_index_in_dim(pieces, lax.rem(me + shift, nx), 0, keepdims=False)
        got.append(lax.ppermute(piece, "x", ring(nx, shift)))
    return got


def row_scale_of(token_vals):
    mean = jnp.mean(token_vals * token_vals, axis=1, keepdims=True)
    return lax.rsqrt(mean + 1e-06).astype(BF16).astype(F32)


def normalise_kernel(tokens_ref, gain_ref, out_ref):
    token_vals = tokens_ref[...].astype(F32)
    scaled = (token_vals * gain_ref[...]).astype(BF16).astype(F32)
    normed = (scaled * row_scale_of(token_vals)).astype(BF16)
    for i in range(out_ref.shape[0]):
        out_ref[i] = normed


def normalise(tokens, gain, copies):
    return pl.pallas_call(
        normalise_kernel,
        out_shape=jax.ShapeDtypeStruct((copies, *tokens.shape), BF16),
        in_specs=[VMEM, VMEM],
        out_specs=VMEM,
        compiler_params=params(8),
    )(tokens, gain)


def gather_kernel(nx, rows, wide, thin, sums_ref, grad_ref, out_ref):
    total = sums_ref[0].astype(F32)
    for i in range(1, sums_ref.shape[0]):
        total = total + sums_ref[i].astype(F32)
    grad = grad_ref[...].astype(F32)
    piece = grad.shape[0] // nx
    pad = jnp.zeros((16 - rows, wide + thin), F32)
    for x in range(nx):
        mine = total[x * rows : (x + 1) * rows]
        for j in range(nx):
            start = nx * wide + j * thin
            both = jnp.concatenate(
                [mine[:, j * wide : (j + 1) * wide], mine[:, start : start + thin]], axis=1
            )
            out_ref[x, 16 * j : 16 * j + 16, :] = jnp.concatenate([both, pad], axis=0).astype(BF16)
        out_ref[x, 16 * nx :, :] = grad[x * piece : (x + 1) * piece].astype(BF16)


def finish_kernel(main, tail, wide, thin, got_ref, tokens_ref, gain_ref, input_ref, gate_ref, up_ref):
    nx = got_ref.shape[0]
    rows, width = tokens_ref.shape
    found = [
        sum(got_ref[x, 16 * j : 16 * j + 16, :].astype(F32) for x in range(nx))[:rows]
        for j in range(nx)
    ]
    token_vals = tokens_ref[...].astype(F32)
    scale = row_scale_of(token_vals)
    gain = gain_ref[...]
    scaled = (token_vals * gain).astype(BF16).astype(F32)
    inner_grad = (
        jnp.concatenate([f[:, :wide] for f in found] + [f[:, wide:] for f in found], axis=1) * scale
    )
    inner = jnp.sum(scaled * inner_grad, axis=1, keepdims=True)
    factor = scale * scale / width
    input_ref[...] = (gain * inner_grad - factor * token_vals * inner).astype(BF16)
    for q in range(nx):
        grad = got_ref[q, 16 * nx :, :].astype(F32)
        start = nx * main + q * tail
        gate_ref[:, q * main : (q + 1) * main] = grad[:, :main]
        gate_ref[:, start : start + tail] = grad[:, 2 * main : 2 * main + tail]
        up_ref[:, q * main : (q + 1) * main] = grad[:, main : 2 * main]
        up_ref[:, start : start + tail] = grad[:, 2 * main + tail :]


def spread_kernel(main, tail, place_ref, got_ref, out_ref):
    nx, half, _ = got_ref.shape
    me = place_ref[2]
    for q in range(nx):
        source = lax.rem(me - q + nx, nx)
        start = nx * main + q * tail
        for h in range(2):
            rows = slice(h * half, (h + 1) * half)
            out_ref[rows, q * main : (q + 1) * main] = got_ref[source, :, h * main : (h + 1) * main]
            out_ref[rows, start : start + tail] = got_ref[
                source, :, 2 * main + h * tail : 2 * main + (h + 1) * tail
            ]


def make_step(nc, nx, nl, ny, nk):
    def per_device(tokens, norm_gain, gate_weight, up_weight, hidden_grad):
        rows, width = tokens.shape
        feats, units = gate_weight.shape
        main, tail = share_sizes(units, nx)
        wide, thin = share_sizes(width, nx)
        pair = 2 * (main + tail)
        own_tokens = hidden_grad.shape[0]
        pool = nx * own_tokens
        nz = nc * nl
        place = jnp.stack([lax.axis_index("l"), lax.axis_index("k"), lax.axis_index("x")])
        place = place.astype(jnp.int32)
        gain = norm_gain.reshape(1, width)

        other_gate = lax.ppermute(gate_weight, ("c", "l"), ring(nz, 1))
        other_up = lax.ppermute(up_weight, ("c", "l"), ring(nz, -1))

        near = exchange(normalise(tokens, gain, nx), "x").reshape(nx * rows, width)
        table = lax.all_gather(near, ("y", "k"), axis=0, tiled=True)

        gate_weight, up_weight, hidden_grad, other_gate, other_up = lax.optimization_barrier(
            (gate_weight, up_weight, hidden_grad, other_gate, other_up)
        )
        own = exchange(pack(nx, gate_weight, up_weight, hidden_grad), "x")
        other = exchange(pack(nx, other_gate, other_up), "x")

        hidden, cots, keep, give = forward(place, table, own, other, ny, rows, pool // 2)
        taken = lax.ppermute(give, "k", [(0, 1), (1, 0)])
        grad = gradient(table, cots, nx, nl, nc, width // 3)
        grad = lax.psum_scatter(grad, ("c", "l"), scatter_dimension=0, tiled=True)

        partial = (keep.astype(F32) + taken.astype(F32)).astype(BF16)
        partial = exchange(partial, "y")

        hidden = jnp.stack(swap_over_x(hidden, nx))
        hidden = pl.pallas_call(
            functools.partial(spread_kernel, main, tail),
            out_shape=jax.ShapeDtypeStruct((own_tokens, units), BF16),
            in_specs=[SMEM, VMEM],
            out_specs=VMEM,
            compiler_params=params(8),
        )(place, hidden)
        last = pl.pallas_call(
            functools.partial(gather_kernel, nx, rows, wide, thin),
            out_shape=jax.ShapeDtypeStruct((nx, 16 * nx + feats // nc, pair), BF16),
            in_specs=[VMEM, VMEM],
            out_specs=VMEM,
            compiler_params=params(24),
        )(partial, grad)
        last = exchange(last, "x")
        input_grad, gate_grad, up_grad = pl.pallas_call(
            functools.partial(finish_kernel, main, tail, wide, thin),
            out_shape=(
                jax.ShapeDtypeStruct((rows, width), BF16),
                jax.ShapeDtypeStruct((feats // nc, units), F32),
                jax.ShapeDtypeStruct((feats // nc, units), F32),
            ),
            in_specs=[VMEM, VMEM, VMEM],
            out_specs=(VMEM, VMEM, VMEM),
            compiler_params=params(16),
        )(last, tokens, gain)
        return (hidden, input_grad, gate_grad, up_grad)

    return per_device


def solution(mesh):
    fine = split_fsdp(mesh)
    return jax.shard_map(
        make_step(*fine.devices.shape),
        mesh=fine,
        in_specs=(
            P(("c", "x", "l", "y", "k"), None),
            P(),
            P(("x", "l"), ("y", "k")),
            P(("x", "l"), ("y", "k")),
            P(("c", "x", "l"), ("y", "k")),
        ),
        out_specs=(
            P(("c", "x", "l"), ("y", "k")),
            P(("c", "x", "l", "y", "k"), None),
            P(("x", "l", "c"), ("y", "k")),
            P(("x", "l", "c"), ("y", "k")),
        ),
        check_vma=False,
    )
```

```python
import functools

import jax
import jax.numpy as jnp
from jax import lax
from jax.experimental import pallas as pl
from jax.experimental.pallas import tpu as pltpu
from jax.sharding import Mesh
from jax.sharding import PartitionSpec as P

ROOT_TWO_PI = 0.7978845608028654
CUBIC = 0.044715
BF16 = jnp.bfloat16
F32 = jnp.float32
VMEM = pl.BlockSpec(memory_space=pltpu.VMEM)
SMEM = pl.BlockSpec(memory_space=pltpu.SMEM)
ANY = pl.BlockSpec(memory_space=pl.ANY)


def split_fsdp(mesh):
    cuts, fsdp, tensor = mesh.devices.shape
    return Mesh(
        mesh.devices.reshape(cuts, fsdp // 2, 2, tensor // 2, 2), ("c", "x", "l", "y", "k")
    )


def ring(size, shift):
    return [(i, (i + shift) % size) for i in range(size)]


def both_ways(size):
    return [(2 * i, 2 * ((i + 1) % size)) for i in range(size)] + [
        (2 * i + 1, 2 * ((i - 1) % size) + 1) for i in range(size)
    ]


def exchange(value, axis):
    return lax.all_to_all(value, axis, split_axis=0, concat_axis=0, tiled=True)


def params(mib):
    return pltpu.CompilerParams(vmem_limit_bytes=mib * 1024 * 1024)


def share_sizes(units, parts):
    part = units // parts
    main = part // 128 * 128
    return main, part - main


def put_pair(out_ref, q, rows, a, b, main, tail, parts):
    out_ref[q, rows, 0:main] = a[:, q * main : (q + 1) * main]
    out_ref[q, rows, main : 2 * main] = b[:, q * main : (q + 1) * main]
    start = parts * main + q * tail
    out_ref[q, rows, 2 * main : 2 * main + tail] = a[:, start : start + tail]
    out_ref[q, rows, 2 * main + tail : 2 * (main + tail)] = b[:, start : start + tail]


def pack_weights_kernel(main, tail, parts, gate_ref, up_ref, out_ref):
    feats = gate_ref.shape[0]
    for q in range(parts):
        put_pair(out_ref, q, slice(0, feats), gate_ref, up_ref, main, tail, parts)


def pack_all_kernel(main, tail, parts, gate_ref, up_ref, grad_ref, out_ref):
    feats = gate_ref.shape[0]
    half = grad_ref.shape[0] // 2
    for q in range(parts):
        put_pair(out_ref, q, slice(0, feats), gate_ref, up_ref, main, tail, parts)
        put_pair(
            out_ref, q, slice(feats, feats + half),
            grad_ref.at[0:half], grad_ref.at[half : 2 * half], main, tail, parts,
        )


def pack(parts, gate, up, grads=None):
    feats, units = gate.shape
    main, tail = share_sizes(units, parts)
    operands = (gate, up) if grads is None else (gate, up, grads)
    rows = feats if grads is None else feats + grads.shape[0] // 2 + 16
    kernel = pack_weights_kernel if grads is None else pack_all_kernel
    return pl.pallas_call(
        functools.partial(kernel, main, tail, parts),
        out_shape=jax.ShapeDtypeStruct((parts, rows, 2 * (main + tail)), BF16),
        in_specs=[VMEM] * len(operands),
        out_specs=VMEM,
        compiler_params=params(24),
        cost_estimate=pl.CostEstimate(flops=0, bytes_accessed=4 * parts * rows * (main + tail), transcendentals=0),
    )(*operands)


def activate(gate, upward, cotangent):
    square = gate * gate
    tangent = jnp.tanh(ROOT_TWO_PI * (gate + CUBIC * square * gate))
    active = 0.5 * gate * (1.0 + tangent)
    slope = 0.5 * (1.0 + tangent) + 0.5 * gate * (1.0 - tangent * tangent) * ROOT_TWO_PI * (
        1.0 + 3.0 * CUBIC * square
    )
    hidden = (active * upward).astype(BF16)
    return hidden, (cotangent * upward * slope).astype(BF16), (cotangent * active).astype(BF16)


def split_index(value, size, top):
    factor = (1 << 20) // size + 1
    assert all(i * factor >> 20 == i // size for i in range(top))
    high = (value * factor) >> 20
    return high, value - high * size


def shuffle(pool, outer, inner, rows):
    index = lax.broadcasted_iota(jnp.int32, (pool, 1), 0)
    high, rest = split_index(index, inner * rows, pool)
    mid, low = split_index(rest, rows, inner * rows)
    source = mid * (outer * rows) + high * rows + low
    columns = lax.broadcasted_iota(jnp.int32, (pool, pool), 1)
    return (columns == source).astype(F32).astype(BF16)


def forward_kernel(
    chunk, main, tail, rows_each, place_ref, table_any, own_ref, other_ref,
    hidden_ref, cots_ref, keep_ref, give_ref, table_ref, matrix, raw, grads_ref, found, sems,
):
    blocks, feats, _ = other_ref.shape
    pool = table_ref.shape[0]
    half = raw.shape[1]
    low, core, me = place_ref[0], place_ref[1], place_ref[3]
    chain = keep_ref.shape[0]
    grads_copy = pltpu.make_async_copy(own_ref.at[:, pl.ds(feats, half)], raw, sems.at[2 * blocks])
    grads_copy.start()
    copies = []
    for x in range(blocks):
        for i, (src, at) in enumerate(((own_ref, low), (other_ref, 1 - low))):
            rows = pl.ds(pl.multiple_of((2 * x + at) * feats, 16), feats)
            copies.append(
                pltpu.make_async_copy(
                    src.at[x, pl.ds(0, feats)], matrix.at[rows], sems.at[2 * x + i]
                )
            )
    tables = [
        pltpu.make_async_copy(
            table_any.at[pl.ds(first, chunk)], table_ref.at[pl.ds(first, chunk)],
            sems.at[2 * blocks + 1 + first // chunk],
        )
        for first in range(0, pool, chunk)
    ]
    tables[0].start()
    for copy in copies:
        copy.start()
    for copy in tables[1:]:
        copy.start()
    groups = pool // (blocks * rows_each)
    forth = shuffle(pool, groups, blocks, rows_each)
    back = shuffle(pool, blocks, groups, rows_each)
    grads_copy.wait()
    for x in range(blocks):
        for h in range(2):
            rows = slice((2 * x + h) * half, (2 * x + h + 1) * half)
            grads_ref[rows, :main] = raw[x, :, h * main : (h + 1) * main]
            grads_ref[rows, main:] = raw[x, :, 2 * main + h * tail : 2 * main + (h + 1) * tail]
    for copy in copies:
        copy.wait()
    step = keep_ref.shape[1]
    for first in range(0, pool, chunk):
        rows = slice(first, first + chunk)
        tables[first // chunk].wait()
        both = jnp.dot(table_ref[rows, :], matrix[...], preferred_element_type=F32)
        grads = jnp.dot(forth[rows, :], grads_ref[...], preferred_element_type=F32)
        hidden, gate_cot, up_cot = activate(
            both[:, :main], both[:, main : 2 * main], grads[:, :main]
        )
        found[rows, :main] = hidden
        cots_ref[rows, :main] = gate_cot
        cots_ref[rows, main : 2 * main] = up_cot
        rest = both[:, 2 * main :]
        hidden, gate_cot, up_cot = activate(rest[:, :tail], rest[:, tail:], grads[:, main:])
        found[rows, main:] = hidden
        cots_ref[rows, 2 * main : 2 * main + tail] = gate_cot
        cots_ref[rows, 2 * main + tail :] = up_cot
        partial = lax.dot_general(
            cots_ref[rows, :], matrix[...], (((1,), (1,)), ((), ())), preferred_element_type=F32
        )
        for j in range(chunk // step):
            block = partial[j * step : (j + 1) * step].astype(BF16)
            ahead = lax.rem(first // step + j - me + 2 * chain, 2 * chain)
            right = ahead < chain
            slot = jnp.where(right, chain - 1 - ahead, ahead - chain)
            kept = right == (core == 0)

            @pl.when(kept)
            def _():
                keep_ref[slot] = block

            @pl.when(jnp.logical_not(kept))
            def _():
                give_ref[slot] = block

    spread = jnp.dot(back, found[...], preferred_element_type=F32).astype(BF16)
    for x in range(blocks):
        for h in range(2):
            rows = slice((2 * x + h) * half, (2 * x + h + 1) * half)
            hidden_ref[x, :, h * main : (h + 1) * main] = spread[rows, :main]
            hidden_ref[x, :, 2 * main + h * tail : 2 * main + (h + 1) * tail] = spread[rows, main:]


def forward(place, table, own, other, ny, rows_each, half, chunk):
    pool, width = table.shape
    blocks, feats, pair = other.shape
    part = pair // 2
    main = part // 128 * 128
    step = pool // ny
    return pl.pallas_call(
        functools.partial(forward_kernel, chunk, main, part - main, rows_each),
        out_shape=(
            jax.ShapeDtypeStruct((blocks, half, pair), BF16),
            jax.ShapeDtypeStruct((pool, pair), BF16),
            jax.ShapeDtypeStruct((ny // 2, step, width), BF16),
            jax.ShapeDtypeStruct((ny // 2, step, width), BF16),
        ),
        in_specs=[SMEM, ANY, ANY, ANY],
        out_specs=(VMEM, VMEM, VMEM, VMEM),
        scratch_shapes=[
            pltpu.VMEM((pool, width), BF16),
            pltpu.VMEM((width, pair), BF16),
            pltpu.VMEM((blocks, half, pair), BF16),
            pltpu.VMEM((pool, part), BF16),
            pltpu.VMEM((pool, part), BF16),
            pltpu.SemaphoreType.DMA((2 * blocks + 1 + pool // chunk,)),
        ],
        compiler_params=params(48),
        cost_estimate=pl.CostEstimate(
            flops=4 * pool * width * pair, bytes_accessed=2 * (2 * pool * width + width * pair), transcendentals=0
        ),
    )(place, table, own, other)


def gradient_kernel(tile, nx, nl, nc, table_ref, cots_ref, out_ref, total):
    width = table_ref.shape[1]
    for first in range(0, width, tile):
        total[first : first + tile, :] = lax.dot_general(
            table_ref[:, first : first + tile], cots_ref[...], (((0,), (0,)), ((), ())),
            preferred_element_type=F32,
        )
    piece = width // (nx * nl * nc)
    block = nx * piece
    for c in range(nc):
        for l in range(nl):
            found = [
                total[((x * nl + l) * nc + c) * piece : ((x * nl + l) * nc + c + 1) * piece, :]
                for x in range(nx)
            ]
            z = c * nl + l
            out_ref[z * block : (z + 1) * block, :] = jnp.concatenate(found, axis=0).astype(BF16)


def gradient(table, cots, nx, nl, nc, tile):
    pool, width = table.shape
    pair = cots.shape[1]
    return pl.pallas_call(
        functools.partial(gradient_kernel, tile, nx, nl, nc),
        out_shape=jax.ShapeDtypeStruct((width, pair), BF16),
        in_specs=[VMEM, VMEM],
        out_specs=VMEM,
        scratch_shapes=[pltpu.VMEM((width, pair), F32)],
        compiler_params=params(48),
        cost_estimate=pl.CostEstimate(
            flops=2 * pool * width * pair, bytes_accessed=2 * (pool * width + width * pair), transcendentals=0
        ),
    )(table, cots)


def swap_over_x(pieces, nx):
    me = lax.axis_index("x")
    got = [lax.dynamic_index_in_dim(pieces, me, 0, keepdims=False)]
    for shift in range(1, nx):
        piece = lax.dynamic_index_in_dim(pieces, lax.rem(me + shift, nx), 0, keepdims=False)
        got.append(lax.ppermute(piece, "x", ring(nx, shift)))
    return got


def row_scale_of(token_vals):
    mean = jnp.mean(token_vals * token_vals, axis=1, keepdims=True)
    return lax.rsqrt(mean + 1e-06).astype(BF16).astype(F32)


def normalise_kernel(tokens_ref, gain_ref, out_ref):
    token_vals = tokens_ref[...].astype(F32)
    scaled = (token_vals * gain_ref[...]).astype(BF16).astype(F32)
    normed = (scaled * row_scale_of(token_vals)).astype(BF16)
    for i in range(out_ref.shape[0]):
        out_ref[i] = normed


def normalise(tokens, gain, copies):
    return pl.pallas_call(
        normalise_kernel,
        out_shape=jax.ShapeDtypeStruct((copies, *tokens.shape), BF16),
        in_specs=[VMEM, VMEM],
        out_specs=VMEM,
        compiler_params=params(8),
    )(tokens, gain)


def gather_kernel(nx, rows, wide, thin, place_ref, near_ref, far_ref, sums_ref, grad_ref, out_ref):
    mine = sums_ref[0 : near_ref.shape[0], :].astype(F32)
    total = near_ref[...].astype(F32) + jnp.where(place_ref[1] == 0, mine, far_ref[...].astype(F32))
    grad = grad_ref[...].astype(F32)
    piece = grad.shape[0] // nx
    pad = jnp.zeros((16 - rows, wide + thin), F32)
    for x in range(nx):
        mine = total[x * rows : (x + 1) * rows]
        for j in range(nx):
            start = nx * wide + j * thin
            both = jnp.concatenate(
                [mine[:, j * wide : (j + 1) * wide], mine[:, start : start + thin]], axis=1
            )
            out_ref[x, 16 * j : 16 * j + 16, :] = jnp.concatenate([both, pad], axis=0).astype(BF16)
        out_ref[x, 16 * nx :, :] = grad[x * piece : (x + 1) * piece].astype(BF16)


def finish_kernel(main, tail, wide, thin, got_ref, tokens_ref, gain_ref, input_ref, gate_ref, up_ref):
    nx = got_ref.shape[0]
    rows, width = tokens_ref.shape
    found = [
        sum(got_ref[x, 16 * j : 16 * j + 16, :].astype(F32) for x in range(nx))[:rows]
        for j in range(nx)
    ]
    token_vals = tokens_ref[...].astype(F32)
    scale = row_scale_of(token_vals)
    gain = gain_ref[...]
    scaled = (token_vals * gain).astype(BF16).astype(F32)
    inner_grad = (
        jnp.concatenate([f[:, :wide] for f in found] + [f[:, wide:] for f in found], axis=1) * scale
    )
    inner = jnp.sum(scaled * inner_grad, axis=1, keepdims=True)
    factor = scale * scale / width
    input_ref[...] = (gain * inner_grad - factor * token_vals * inner).astype(BF16)
    for q in range(nx):
        grad = got_ref[q, 16 * nx :, :].astype(F32)
        start = nx * main + q * tail
        gate_ref[:, q * main : (q + 1) * main] = grad[:, :main]
        gate_ref[:, start : start + tail] = grad[:, 2 * main : 2 * main + tail]
        up_ref[:, q * main : (q + 1) * main] = grad[:, main : 2 * main]
        up_ref[:, start : start + tail] = grad[:, 2 * main + tail :]


def spread_kernel(main, tail, place_ref, got_ref, out_ref):
    nx, half, _ = got_ref.shape
    me = place_ref[2]
    for q in range(nx):
        source = lax.rem(me - q + nx, nx)
        start = nx * main + q * tail
        for h in range(2):
            rows = slice(h * half, (h + 1) * half)
            out_ref[rows, q * main : (q + 1) * main] = got_ref[source, :, h * main : (h + 1) * main]
            out_ref[rows, start : start + tail] = got_ref[
                source, :, 2 * main + h * tail : 2 * main + (h + 1) * tail
            ]


def make_step(nc, nx, nl, ny, nk):
    def per_device(tokens, norm_gain, gate_weight, up_weight, hidden_grad):
        rows, width = tokens.shape
        feats, units = gate_weight.shape
        main, tail = share_sizes(units, nx)
        wide, thin = share_sizes(width, nx)
        pair = 2 * (main + tail)
        own_tokens = hidden_grad.shape[0]
        pool = nx * own_tokens
        nz = nc * nl
        place = jnp.stack([lax.axis_index(name) for name in ("l", "k", "x", "y")]).astype(jnp.int32)
        gain = norm_gain.reshape(1, width)

        near = exchange(normalise(tokens, gain, nx), "x").reshape(nx * rows, width)
        table = lax.all_gather(near, ("y", "k"), axis=0, tiled=True)

        other = exchange(
            lax.ppermute(pack(nx, gate_weight, up_weight), ("c", "l", "k"), both_ways(nz)), "x"
        )
        own = exchange(pack(nx, gate_weight, up_weight, hidden_grad), "x")

        hidden, cots, keep, give = forward(
            place, table, own, other, ny, rows, own_tokens // 2, pool // 2
        )
        taken = lax.ppermute(give, "k", [(0, 1), (1, 0)])
        grad = gradient(table, cots, nx, nl, nc, width // 3)
        taken, grad = lax.optimization_barrier((taken, grad))
        grad = lax.psum_scatter(grad, ("c", "l"), scatter_dimension=0, tiled=True)

        def term(i):
            return keep[i].astype(F32) + taken[i].astype(F32)

        partial = term(0).astype(BF16)
        for i in range(1, ny // 2):
            partial = lax.ppermute(partial, ("y", "k"), both_ways(ny))
            partial = (partial.astype(F32) + term(i)).astype(BF16)
        step = partial.shape[0] // 2
        lower, upper = partial[:step], partial[step:]
        core = lax.axis_index("k")
        near = lax.ppermute(
            jnp.where(core == 0, upper, lower), ("y", "k"),
            [(2 * y, 2 * y + 1) for y in range(ny)]
            + [(2 * y + 1, 2 * ((y - 1) % ny)) for y in range(ny)],
        )
        far = lax.ppermute(
            upper, ("y", "k"), [(2 * y + 1, 2 * ((y - 1) % ny) + 1) for y in range(ny)]
        )

        hidden = jnp.stack(swap_over_x(hidden, nx))
        hidden = pl.pallas_call(
            functools.partial(spread_kernel, main, tail),
            out_shape=jax.ShapeDtypeStruct((own_tokens, units), BF16),
            in_specs=[SMEM, VMEM],
            out_specs=VMEM,
            compiler_params=params(8),
        )(place, hidden)
        last = pl.pallas_call(
            functools.partial(gather_kernel, nx, rows, wide, thin),
            out_shape=jax.ShapeDtypeStruct((nx, 16 * nx + feats // nc, pair), BF16),
            in_specs=[SMEM, VMEM, VMEM, VMEM, VMEM],
            out_specs=VMEM,
            compiler_params=params(24),
        )(place, near, far, partial, grad)
        last = exchange(last, "x")
        input_grad, gate_grad, up_grad = pl.pallas_call(
            functools.partial(finish_kernel, main, tail, wide, thin),
            out_shape=(
                jax.ShapeDtypeStruct((rows, width), BF16),
                jax.ShapeDtypeStruct((feats // nc, units), F32),
                jax.ShapeDtypeStruct((feats // nc, units), F32),
            ),
            in_specs=[VMEM, VMEM, VMEM],
            out_specs=(VMEM, VMEM, VMEM),
            compiler_params=params(16),
        )(last, tokens, gain)
        return (hidden, input_grad, gate_grad, up_grad)

    return per_device


def solution(mesh):
    fine = split_fsdp(mesh)
    return jax.shard_map(
        make_step(*fine.devices.shape),
        mesh=fine,
        in_specs=(
            P(("c", "x", "l", "y", "k"), None),
            P(),
            P(("x", "l"), ("y", "k")),
            P(("x", "l"), ("y", "k")),
            P(("c", "x", "l"), ("y", "k")),
        ),
        out_specs=(
            P(("c", "x", "l"), ("y", "k")),
            P(("c", "x", "l", "y", "k"), None),
            P(("x", "l", "c"), ("y", "k")),
            P(("x", "l", "c"), ("y", "k")),
        ),
        check_vma=False,
    )
```

```python
import functools

import jax
import jax.numpy as jnp
from jax import lax
from jax.experimental import pallas as pl
from jax.experimental.pallas import tpu as pltpu
from jax.sharding import Mesh
from jax.sharding import PartitionSpec as P

ROOT_TWO_PI = 0.7978845608028654
CUBIC = 0.044715
BF16 = jnp.bfloat16
F32 = jnp.float32
VMEM = pl.BlockSpec(memory_space=pltpu.VMEM)
SMEM = pl.BlockSpec(memory_space=pltpu.SMEM)
ANY = pl.BlockSpec(memory_space=pl.ANY)


def split_fsdp(mesh):
    cuts, fsdp, tensor = mesh.devices.shape
    return Mesh(
        mesh.devices.reshape(cuts, fsdp // 2, 2, tensor // 2, 2), ("c", "x", "l", "y", "k")
    )


def ring(size, shift):
    return [(i, (i + shift) % size) for i in range(size)]


def both_ways(size):
    return [(2 * i, 2 * ((i + 1) % size)) for i in range(size)] + [
        (2 * i + 1, 2 * ((i - 1) % size) + 1) for i in range(size)
    ]


def exchange(value, axis):
    return lax.all_to_all(value, axis, split_axis=0, concat_axis=0, tiled=True)


def params(mib):
    return pltpu.CompilerParams(vmem_limit_bytes=mib * 1024 * 1024)


def share_sizes(units, parts):
    part = units // parts
    main = part // 128 * 128
    return main, part - main


def put_pair(out_ref, q, rows, a, b, main, tail, parts):
    out_ref[q, rows, 0:main] = a[:, q * main : (q + 1) * main]
    out_ref[q, rows, main : 2 * main] = b[:, q * main : (q + 1) * main]
    start = parts * main + q * tail
    out_ref[q, rows, 2 * main : 2 * main + tail] = a[:, start : start + tail]
    out_ref[q, rows, 2 * main + tail : 2 * (main + tail)] = b[:, start : start + tail]


def pack_weights_kernel(main, tail, parts, gate_ref, up_ref, out_ref):
    rows = slice(0, out_ref.shape[1])
    for q in range(parts):
        put_pair(out_ref, q, rows, gate_ref.at[rows], up_ref.at[rows], main, tail, parts)


def pack_all_kernel(main, tail, parts, gate_ref, up_ref, grad_ref, out_ref):
    feats = gate_ref.shape[0]
    half = grad_ref.shape[0] // 2
    for q in range(parts):
        put_pair(out_ref, q, slice(0, feats), gate_ref, up_ref, main, tail, parts)
        put_pair(
            out_ref, q, slice(feats, feats + half),
            grad_ref.at[0:half], grad_ref.at[half : 2 * half], main, tail, parts,
        )


def pack(parts, gate, up, grads=None):
    feats, units = gate.shape
    main, tail = share_sizes(units, parts)
    operands = (gate, up) if grads is None else (gate, up, grads)
    rows = feats // 2 if grads is None else feats + grads.shape[0] // 2 + 16
    kernel = pack_weights_kernel if grads is None else pack_all_kernel
    return pl.pallas_call(
        functools.partial(kernel, main, tail, parts),
        out_shape=jax.ShapeDtypeStruct((parts, rows, 2 * (main + tail)), BF16),
        in_specs=[VMEM] * len(operands),
        out_specs=VMEM,
        compiler_params=params(24),
        cost_estimate=pl.CostEstimate(flops=0, bytes_accessed=4 * parts * rows * (main + tail), transcendentals=0),
    )(*operands)


def activate(gate, upward, cotangent):
    square = gate * gate
    tangent = jnp.tanh(ROOT_TWO_PI * (gate + CUBIC * square * gate))
    active = 0.5 * gate * (1.0 + tangent)
    slope = 0.5 * (1.0 + tangent) + 0.5 * gate * (1.0 - tangent * tangent) * ROOT_TWO_PI * (
        1.0 + 3.0 * CUBIC * square
    )
    hidden = (active * upward).astype(BF16)
    return hidden, (cotangent * upward * slope).astype(BF16), (cotangent * active).astype(BF16)


def split_index(value, size, top):
    factor = (1 << 20) // size + 1
    assert all(i * factor >> 20 == i // size for i in range(top))
    high = (value * factor) >> 20
    return high, value - high * size


def shuffle(pool, outer, inner, rows):
    index = lax.broadcasted_iota(jnp.int32, (pool, 1), 0)
    high, rest = split_index(index, inner * rows, pool)
    mid, low = split_index(rest, rows, inner * rows)
    source = mid * (outer * rows) + high * rows + low
    columns = lax.broadcasted_iota(jnp.int32, (pool, pool), 1)
    return (columns == source).astype(F32).astype(BF16)


def forward_kernel(
    chunk, main, tail, rows_each, place_ref, table_any, own_ref, early_ref, late_ref,
    hidden_ref, cots_ref, keep_ref, give_ref, table_ref, mine, theirs, raw, grads_ref, found, sems,
):
    blocks, cut, _ = early_ref.shape
    feats = cut + late_ref.shape[1]
    pool, width = table_ref.shape
    half = raw.shape[1]
    low, core, me = place_ref[0], place_ref[1], place_ref[3]
    chain = keep_ref.shape[0]
    near_cols = pl.ds(pl.multiple_of(low * (width // 2), 128), width // 2)
    far_cols = pl.ds(pl.multiple_of((1 - low) * (width // 2), 128), width // 2)
    grads_copy = pltpu.make_async_copy(own_ref.at[:, pl.ds(feats, half)], raw, sems.at[3 * blocks])
    grads_copy.start()
    copies = []
    for x in range(blocks):
        for i, (src, dst, first, size) in enumerate((
            (own_ref, mine, 0, feats), (early_ref, theirs, 0, cut), (late_ref, theirs, cut, feats - cut)
        )):
            copies.append(
                pltpu.make_async_copy(
                    src.at[x, pl.ds(0, size)], dst.at[pl.ds(x * feats + first, size)], sems.at[3 * x + i]
                )
            )
    tables = [
        pltpu.make_async_copy(
            table_any.at[pl.ds(first, chunk)], table_ref.at[pl.ds(first, chunk)],
            sems.at[3 * blocks + 1 + first // chunk],
        )
        for first in range(0, pool, chunk)
    ]
    tables[0].start()
    for copy in copies:
        copy.start()
    for copy in tables[1:]:
        copy.start()
    groups = pool // (blocks * rows_each)
    forth = shuffle(pool, groups, blocks, rows_each)
    back = shuffle(pool, blocks, groups, rows_each)
    grads_copy.wait()
    for x in range(blocks):
        for h in range(2):
            rows = slice((2 * x + h) * half, (2 * x + h + 1) * half)
            grads_ref[rows, :main] = raw[x, :, h * main : (h + 1) * main]
            grads_ref[rows, main:] = raw[x, :, 2 * main + h * tail : 2 * main + (h + 1) * tail]
    for copy in copies:
        copy.wait()
    step = keep_ref.shape[1]
    for first in range(0, pool, chunk):
        rows = slice(first, first + chunk)
        tables[first // chunk].wait()
        both = jnp.dot(table_ref[rows, near_cols], mine[...], preferred_element_type=F32)
        both = both + jnp.dot(table_ref[rows, far_cols], theirs[...], preferred_element_type=F32)
        grads = jnp.dot(forth[rows, :], grads_ref[...], preferred_element_type=F32)
        hidden, gate_cot, up_cot = activate(
            both[:, :main], both[:, main : 2 * main], grads[:, :main]
        )
        found[rows, :main] = hidden
        cots_ref[rows, :main] = gate_cot
        cots_ref[rows, main : 2 * main] = up_cot
        rest = both[:, 2 * main :]
        hidden, gate_cot, up_cot = activate(rest[:, :tail], rest[:, tail:], grads[:, main:])
        found[rows, main:] = hidden
        cots_ref[rows, 2 * main : 2 * main + tail] = gate_cot
        cots_ref[rows, 2 * main + tail :] = up_cot
        for weights, cols in ((mine, near_cols), (theirs, far_cols)):
            partial = lax.dot_general(
                cots_ref[rows, :], weights[...], (((1,), (1,)), ((), ())), preferred_element_type=F32
            )
            for j in range(chunk // step):
                block = partial[j * step : (j + 1) * step].astype(BF16)
                ahead = lax.rem(first // step + j - me + 2 * chain, 2 * chain)
                right = ahead < chain
                slot = jnp.where(right, chain - 1 - ahead, ahead - chain)
                kept = right == (core == 0)

                @pl.when(kept)
                def _():
                    keep_ref[slot, :, cols] = block

                @pl.when(jnp.logical_not(kept))
                def _():
                    give_ref[slot, :, cols] = block

    spread = jnp.dot(back, found[...], preferred_element_type=F32).astype(BF16)
    for x in range(blocks):
        for h in range(2):
            rows = slice((2 * x + h) * half, (2 * x + h + 1) * half)
            hidden_ref[x, :, h * main : (h + 1) * main] = spread[rows, :main]
            hidden_ref[x, :, 2 * main + h * tail : 2 * main + (h + 1) * tail] = spread[rows, main:]


def forward(place, table, own, early, late, ny, rows_each, half, chunk):
    pool, width = table.shape
    blocks, _, pair = early.shape
    part = pair // 2
    main = part // 128 * 128
    step = pool // ny
    return pl.pallas_call(
        functools.partial(forward_kernel, chunk, main, part - main, rows_each),
        out_shape=(
            jax.ShapeDtypeStruct((blocks, half, pair), BF16),
            jax.ShapeDtypeStruct((pool, pair), BF16),
            jax.ShapeDtypeStruct((ny // 2, step, width), BF16),
            jax.ShapeDtypeStruct((ny // 2, step, width), BF16),
        ),
        in_specs=[SMEM, ANY, ANY, ANY, ANY],
        out_specs=(VMEM, VMEM, VMEM, VMEM),
        scratch_shapes=[
            pltpu.VMEM((pool, width), BF16),
            pltpu.VMEM((width // 2, pair), BF16),
            pltpu.VMEM((width // 2, pair), BF16),
            pltpu.VMEM((blocks, half, pair), BF16),
            pltpu.VMEM((pool, part), BF16),
            pltpu.VMEM((pool, part), BF16),
            pltpu.SemaphoreType.DMA((3 * blocks + 1 + pool // chunk,)),
        ],
        compiler_params=params(60),
        cost_estimate=pl.CostEstimate(
            flops=4 * pool * width * pair, bytes_accessed=2 * (2 * pool * width + width * pair), transcendentals=0
        ),
    )(place, table, own, early, late)


def gradient_kernel(tile, nx, nl, nc, table_ref, cots_ref, out_ref, total):
    width = table_ref.shape[1]
    for first in range(0, width, tile):
        total[first : first + tile, :] = lax.dot_general(
            table_ref[:, first : first + tile], cots_ref[...], (((0,), (0,)), ((), ())),
            preferred_element_type=F32,
        )
    piece = width // (nx * nl * nc)
    block = nx * piece
    for c in range(nc):
        for l in range(nl):
            found = [
                total[((l * nx + x) * nc + c) * piece : ((l * nx + x) * nc + c + 1) * piece, :]
                for x in range(nx)
            ]
            z = c * nl + l
            out_ref[z * block : (z + 1) * block, :] = jnp.concatenate(found, axis=0).astype(BF16)


def gradient(table, cots, nx, nl, nc, tile):
    pool, width = table.shape
    pair = cots.shape[1]
    return pl.pallas_call(
        functools.partial(gradient_kernel, tile, nx, nl, nc),
        out_shape=jax.ShapeDtypeStruct((width, pair), BF16),
        in_specs=[VMEM, VMEM],
        out_specs=VMEM,
        scratch_shapes=[pltpu.VMEM((width, pair), F32)],
        compiler_params=params(48),
        cost_estimate=pl.CostEstimate(
            flops=2 * pool * width * pair, bytes_accessed=2 * (pool * width + width * pair), transcendentals=0
        ),
    )(table, cots)


def swap_over_x(pieces, nx):
    me = lax.axis_index("x")
    got = [lax.dynamic_index_in_dim(pieces, me, 0, keepdims=False)]
    for shift in range(1, nx):
        piece = lax.dynamic_index_in_dim(pieces, lax.rem(me + shift, nx), 0, keepdims=False)
        got.append(lax.ppermute(piece, "x", ring(nx, shift)))
    return got


def row_scale_of(token_vals):
    mean = jnp.mean(token_vals * token_vals, axis=1, keepdims=True)
    return lax.rsqrt(mean + 1e-06).astype(BF16).astype(F32)


def turned(value, outer, inner):
    size = value.shape[1] // (outer * inner)
    blocks = [(o * inner + i) * size for i in range(inner) for o in range(outer)]
    return jnp.concatenate([value[:, at : at + size] for at in blocks], axis=1)


def normalise_kernel(tokens_ref, gain_ref, out_ref):
    token_vals = tokens_ref[...].astype(F32)
    scaled = (token_vals * gain_ref[...]).astype(BF16).astype(F32)
    normed = turned(scaled * row_scale_of(token_vals), out_ref.shape[0], 2).astype(BF16)
    for i in range(out_ref.shape[0]):
        out_ref[i] = normed


def normalise(tokens, gain, copies):
    return pl.pallas_call(
        normalise_kernel,
        out_shape=jax.ShapeDtypeStruct((copies, *tokens.shape), BF16),
        in_specs=[VMEM, VMEM],
        out_specs=VMEM,
        compiler_params=params(8),
    )(tokens, gain)


def gather_kernel(nx, rows, wide, thin, place_ref, near_ref, far_ref, sums_ref, grad_ref, out_ref):
    mine = sums_ref[0 : near_ref.shape[0], :].astype(F32)
    total = near_ref[...].astype(F32) + jnp.where(place_ref[1] == 0, mine, far_ref[...].astype(F32))
    grad = grad_ref[...].astype(F32)
    piece = grad.shape[0] // nx
    pad = jnp.zeros((16 - rows, wide + thin), F32)
    for x in range(nx):
        mine = total[x * rows : (x + 1) * rows]
        for j in range(nx):
            start = nx * wide + j * thin
            both = jnp.concatenate(
                [mine[:, j * wide : (j + 1) * wide], mine[:, start : start + thin]], axis=1
            )
            out_ref[x, 16 * j : 16 * j + 16, :] = jnp.concatenate([both, pad], axis=0).astype(BF16)
        out_ref[x, 16 * nx :, :] = grad[x * piece : (x + 1) * piece].astype(BF16)


def finish_kernel(main, tail, wide, thin, got_ref, tokens_ref, gain_ref, input_ref, gate_ref, up_ref):
    nx = got_ref.shape[0]
    rows, width = tokens_ref.shape
    found = [
        sum(got_ref[x, 16 * j : 16 * j + 16, :].astype(F32) for x in range(nx))[:rows]
        for j in range(nx)
    ]
    token_vals = tokens_ref[...].astype(F32)
    scale = row_scale_of(token_vals)
    gain = gain_ref[...]
    scaled = (token_vals * gain).astype(BF16).astype(F32)
    inner_grad = jnp.concatenate([f[:, :wide] for f in found] + [f[:, wide:] for f in found], axis=1)
    inner_grad = turned(inner_grad, 2, nx) * scale
    inner = jnp.sum(scaled * inner_grad, axis=1, keepdims=True)
    factor = scale * scale / width
    input_ref[...] = (gain * inner_grad - factor * token_vals * inner).astype(BF16)
    for q in range(nx):
        grad = got_ref[q, 16 * nx :, :].astype(F32)
        start = nx * main + q * tail
        gate_ref[:, q * main : (q + 1) * main] = grad[:, :main]
        gate_ref[:, start : start + tail] = grad[:, 2 * main : 2 * main + tail]
        up_ref[:, q * main : (q + 1) * main] = grad[:, main : 2 * main]
        up_ref[:, start : start + tail] = grad[:, 2 * main + tail :]


def spread_kernel(main, tail, place_ref, got_ref, out_ref):
    nx, half, _ = got_ref.shape
    me = place_ref[2]
    for q in range(nx):
        source = lax.rem(me - q + nx, nx)
        start = nx * main + q * tail
        for h in range(2):
            rows = slice(h * half, (h + 1) * half)
            out_ref[rows, q * main : (q + 1) * main] = got_ref[source, :, h * main : (h + 1) * main]
            out_ref[rows, start : start + tail] = got_ref[
                source, :, 2 * main + h * tail : 2 * main + (h + 1) * tail
            ]


def make_step(nc, nx, nl, ny, nk):
    def per_device(tokens, norm_gain, gate_weight, up_weight, hidden_grad):
        rows, width = tokens.shape
        feats, units = gate_weight.shape
        main, tail = share_sizes(units, nx)
        wide, thin = share_sizes(width, nx)
        pair = 2 * (main + tail)
        own_tokens = hidden_grad.shape[0]
        pool = nx * own_tokens
        nz = nc * nl
        place = jnp.stack([lax.axis_index(name) for name in ("l", "k", "x", "y")]).astype(jnp.int32)
        gain = norm_gain.reshape(1, width)

        near = exchange(normalise(tokens, gain, nx), "x").reshape(nx * rows, width)
        table = lax.all_gather(near, ("y", "k"), axis=0, tiled=True)

        early = lax.ppermute(pack(nx, gate_weight, up_weight), ("c", "l", "k"), both_ways(nz))
        own = exchange(pack(nx, gate_weight, up_weight, hidden_grad), "x")
        early = exchange(early, "x")
        late = lax.ppermute(own[:, feats // 2 : feats], ("c", "l", "k"), both_ways(nz))

        hidden, cots, keep, give = forward(
            place, table, own, early, late, ny, rows, own_tokens // 2, pool // 2
        )
        taken = lax.ppermute(give, "k", [(0, 1), (1, 0)])
        grad = gradient(table, cots, nx, nl, nc, width // 3)
        taken, grad = lax.optimization_barrier((taken, grad))
        grad = lax.psum_scatter(grad, ("c", "l"), scatter_dimension=0, tiled=True)

        def term(i):
            return keep[i].astype(F32) + taken[i].astype(F32)

        partial = term(0).astype(BF16)
        for i in range(1, ny // 2):
            partial = lax.ppermute(partial, ("y", "k"), both_ways(ny))
            partial = (partial.astype(F32) + term(i)).astype(BF16)
        step = partial.shape[0] // 2
        lower, upper = partial[:step], partial[step:]
        core = lax.axis_index("k")
        near = lax.ppermute(
            jnp.where(core == 0, upper, lower), ("y", "k"),
            [(2 * y, 2 * y + 1) for y in range(ny)]
            + [(2 * y + 1, 2 * ((y - 1) % ny)) for y in range(ny)],
        )
        far = lax.ppermute(
            upper, ("y", "k"), [(2 * y + 1, 2 * ((y - 1) % ny) + 1) for y in range(ny)]
        )

        hidden = jnp.stack(swap_over_x(hidden, nx))
        hidden = pl.pallas_call(
            functools.partial(spread_kernel, main, tail),
            out_shape=jax.ShapeDtypeStruct((own_tokens, units), BF16),
            in_specs=[SMEM, VMEM],
            out_specs=VMEM,
            compiler_params=params(8),
        )(place, hidden)
        hidden, near, far = lax.optimization_barrier((hidden, near, far))
        last = pl.pallas_call(
            functools.partial(gather_kernel, nx, rows, wide, thin),
            out_shape=jax.ShapeDtypeStruct((nx, 16 * nx + feats // nc, pair), BF16),
            in_specs=[SMEM, VMEM, VMEM, VMEM, VMEM],
            out_specs=VMEM,
            compiler_params=params(24),
        )(place, near, far, partial, grad)
        last = exchange(last, "x")
        input_grad, gate_grad, up_grad = pl.pallas_call(
            functools.partial(finish_kernel, main, tail, wide, thin),
            out_shape=(
                jax.ShapeDtypeStruct((rows, width), BF16),
                jax.ShapeDtypeStruct((feats // nc, units), F32),
                jax.ShapeDtypeStruct((feats // nc, units), F32),
            ),
            in_specs=[VMEM, VMEM, VMEM],
            out_specs=(VMEM, VMEM, VMEM),
            compiler_params=params(16),
        )(last, tokens, gain)
        return (hidden, input_grad, gate_grad, up_grad)

    return per_device


def solution(mesh):
    fine = split_fsdp(mesh)
    return jax.shard_map(
        make_step(*fine.devices.shape),
        mesh=fine,
        in_specs=(
            P(("c", "x", "l", "y", "k"), None),
            P(),
            P(("x", "l"), ("y", "k")),
            P(("x", "l"), ("y", "k")),
            P(("c", "x", "l"), ("y", "k")),
        ),
        out_specs=(
            P(("c", "x", "l"), ("y", "k")),
            P(("c", "x", "l", "y", "k"), None),
            P(("x", "l", "c"), ("y", "k")),
            P(("x", "l", "c"), ("y", "k")),
        ),
        check_vma=False,
    )
```

```python
import functools

import jax
import jax.numpy as jnp
from jax import lax
from jax.experimental import pallas as pl
from jax.experimental.pallas import tpu as pltpu
from jax.sharding import Mesh
from jax.sharding import PartitionSpec as P

ROOT_TWO_PI = 0.7978845608028654
CUBIC = 0.044715
BF16 = jnp.bfloat16
F32 = jnp.float32
VMEM = pl.BlockSpec(memory_space=pltpu.VMEM)
SMEM = pl.BlockSpec(memory_space=pltpu.SMEM)
ANY = pl.BlockSpec(memory_space=pl.ANY)


def split_fsdp(mesh):
    cuts, fsdp, tensor = mesh.devices.shape
    return Mesh(
        mesh.devices.reshape(cuts, fsdp // 2, 2, tensor // 2, 2), ("c", "x", "l", "y", "k")
    )


def ring(size, shift):
    return [(i, (i + shift) % size) for i in range(size)]


def both_ways(size):
    return [(2 * i, 2 * ((i + 1) % size)) for i in range(size)] + [
        (2 * i + 1, 2 * ((i - 1) % size) + 1) for i in range(size)
    ]


def exchange(value, axis):
    return lax.all_to_all(value, axis, split_axis=0, concat_axis=0, tiled=True)


def params(mib):
    return pltpu.CompilerParams(vmem_limit_bytes=mib * 1024 * 1024)


def share_sizes(units, parts):
    part = units // parts
    main = part // 128 * 128
    return main, part - main


def put_pair(out_ref, q, rows, a, b, main, tail, parts):
    out_ref[q, rows, 0:main] = a[:, q * main : (q + 1) * main]
    out_ref[q, rows, main : 2 * main] = b[:, q * main : (q + 1) * main]
    start = parts * main + q * tail
    out_ref[q, rows, 2 * main : 2 * main + tail] = a[:, start : start + tail]
    out_ref[q, rows, 2 * main + tail : 2 * (main + tail)] = b[:, start : start + tail]


def pack_weights_kernel(main, tail, parts, gate_ref, up_ref, out_ref):
    rows = slice(0, out_ref.shape[1])
    for q in range(parts):
        put_pair(out_ref, q, rows, gate_ref.at[rows], up_ref.at[rows], main, tail, parts)


def pack_weights(parts, gate, up, rows):
    main, tail = share_sizes(gate.shape[1], parts)
    return pl.pallas_call(
        functools.partial(pack_weights_kernel, main, tail, parts),
        out_shape=jax.ShapeDtypeStruct((parts, rows, 2 * (main + tail)), BF16),
        in_specs=[VMEM, VMEM],
        out_specs=VMEM,
        compiler_params=params(16),
    )(gate, up)


def pack_grads_kernel(main, tail, parts, weights_ref, grad_ref, out_ref):
    cut = weights_ref.shape[1]
    half = grad_ref.shape[0] // 2
    out_ref[:, 0:cut, :] = weights_ref[...]
    for q in range(parts):
        put_pair(
            out_ref, q, slice(cut, cut + half),
            grad_ref.at[0:half], grad_ref.at[half : 2 * half], main, tail, parts,
        )


def pack_grads(parts, weights, grads):
    main, tail = share_sizes(grads.shape[1], parts)
    rows = weights.shape[1] + grads.shape[0] // 2 + 32
    return pl.pallas_call(
        functools.partial(pack_grads_kernel, main, tail, parts),
        out_shape=jax.ShapeDtypeStruct((parts, rows, 2 * (main + tail)), BF16),
        in_specs=[VMEM, VMEM],
        out_specs=VMEM,
        compiler_params=params(16),
    )(weights, grads)


def activate(gate, upward, cotangent):
    square = gate * gate
    tangent = jnp.tanh(ROOT_TWO_PI * (gate + CUBIC * square * gate))
    active = 0.5 * gate * (1.0 + tangent)
    slope = 0.5 * (1.0 + tangent) + 0.5 * gate * (1.0 - tangent * tangent) * ROOT_TWO_PI * (
        1.0 + 3.0 * CUBIC * square
    )
    hidden = (active * upward).astype(BF16)
    return hidden, (cotangent * upward * slope).astype(BF16), (cotangent * active).astype(BF16)


def split_index(value, size, top):
    factor = (1 << 20) // size + 1
    assert all(i * factor >> 20 == i // size for i in range(top))
    high = (value * factor) >> 20
    return high, value - high * size


def shuffle(pool, outer, inner, rows):
    index = lax.broadcasted_iota(jnp.int32, (pool, 1), 0)
    high, rest = split_index(index, inner * rows, pool)
    mid, low = split_index(rest, rows, inner * rows)
    source = mid * (outer * rows) + high * rows + low
    columns = lax.broadcasted_iota(jnp.int32, (pool, pool), 1)
    return (columns == source).astype(F32).astype(BF16)


SORTED = 4


def sort_grads_kernel(main, tail, cut, rows_each, raw_ref, out_ref):
    blocks = raw_ref.shape[0]
    size = SORTED * rows_each
    half = out_ref.shape[0] // (2 * blocks)
    order = shuffle(blocks * size, SORTED, blocks, rows_each)
    for g in range(2 * half // size):
        h, at = g * size // half, cut + g * size % half
        found = [raw_ref[x, at : at + size, :] for x in range(blocks)]
        found = jnp.concatenate(found, axis=0)
        rows = slice(g * blocks * size, (g + 1) * blocks * size)
        for lanes, first, width in (
            (slice(0, main), h * main, main), (slice(main, main + tail), 2 * main + h * tail, tail)
        ):
            out_ref[rows, lanes] = jnp.dot(
                order, found[:, first : first + width], preferred_element_type=F32
            ).astype(BF16)


def sort_grads(raw, cut, own_tokens, rows_each):
    blocks, _, pair = raw.shape
    main = pair // 2 // 128 * 128
    return pl.pallas_call(
        functools.partial(sort_grads_kernel, main, pair // 2 - main, cut, rows_each),
        out_shape=jax.ShapeDtypeStruct((blocks * own_tokens, pair // 2), BF16),
        in_specs=[VMEM],
        out_specs=VMEM,
        compiler_params=params(16),
    )(raw)


def sort_hidden_kernel(main, tail, rows_each, found_ref, out_ref):
    blocks, half, _ = out_ref.shape
    size = SORTED * rows_each
    order = shuffle(blocks * size, blocks, SORTED, rows_each)
    for g in range(2 * half // size):
        h, at = g * size // half, g * size % half
        rows = slice(g * blocks * size, (g + 1) * blocks * size)
        for lanes, first, width in (
            (slice(0, main), h * main, main), (slice(main, main + tail), 2 * main + h * tail, tail)
        ):
            got = jnp.dot(order, found_ref[rows, lanes], preferred_element_type=F32).astype(BF16)
            for x in range(blocks):
                out_ref[x, at : at + size, first : first + width] = got[x * size : (x + 1) * size]


def sort_hidden(found, blocks, rows_each):
    pool, part = found.shape
    main = part // 128 * 128
    return pl.pallas_call(
        functools.partial(sort_hidden_kernel, main, part - main, rows_each),
        out_shape=jax.ShapeDtypeStruct((blocks, pool // blocks // 2, 2 * part), BF16),
        in_specs=[VMEM],
        out_specs=VMEM,
        compiler_params=params(16),
    )(found)


def forward_kernel(
    chunk, main, tail, place_ref, table_any, own_ref, early_ref, late_ref, grads_ref,
    found_ref, cots_ref, keep_ref, give_ref, table_ref, theirs, sems,
):
    blocks, feats, pair = own_ref.shape
    cut = feats - late_ref.shape[1]
    pool, width = table_ref.shape
    low, core, me = place_ref[0], place_ref[1], place_ref[3]
    chain, step, _ = keep_ref.shape
    tables = [
        pltpu.make_async_copy(
            table_any.at[pl.ds(first, chunk)], table_ref.at[pl.ds(first, chunk)],
            sems.at[first // chunk],
        )
        for first in range(0, pool, chunk)
    ]
    for copy in tables:
        copy.start()
    near_cols = pl.ds(pl.multiple_of(low * (width // 2), 128), width // 2)
    far_cols = pl.ds(pl.multiple_of((1 - low) * (width // 2), 128), width // 2)
    for x in range(blocks):
        theirs[x * feats : x * feats + cut, :] = early_ref[x, :cut, :]
        theirs[x * feats + cut : (x + 1) * feats, :] = late_ref[x]
    for first in range(0, pool, chunk):
        rows = slice(first, first + chunk)
        tables[first // chunk].wait()
        mine = own_ref[...].reshape(blocks * feats, pair)
        both = jnp.dot(table_ref[rows, near_cols], mine, preferred_element_type=F32)
        both = both + jnp.dot(table_ref[rows, far_cols], theirs[...], preferred_element_type=F32)
        grads = grads_ref[rows, :].astype(F32)
        hidden, gate_cot, up_cot = activate(
            both[:, :main], both[:, main : 2 * main], grads[:, :main]
        )
        found_ref[rows, :main] = hidden
        cots_ref[rows, :main] = gate_cot
        cots_ref[rows, main : 2 * main] = up_cot
        rest = both[:, 2 * main :]
        hidden, gate_cot, up_cot = activate(rest[:, :tail], rest[:, tail:], grads[:, main:])
        found_ref[rows, main:] = hidden
        cots_ref[rows, 2 * main : 2 * main + tail] = gate_cot
        cots_ref[rows, 2 * main + tail :] = up_cot
        for weights, cols in ((mine, near_cols), (theirs[...], far_cols)):
            partial = lax.dot_general(
                cots_ref[rows, :], weights, (((1,), (1,)), ((), ())), preferred_element_type=F32
            )
            for j in range(chunk // step):
                block = partial[j * step : (j + 1) * step].astype(BF16)
                ahead = lax.rem(first // step + j - me + 2 * chain, 2 * chain)
                right = ahead < chain
                slot = jnp.where(right, chain - 1 - ahead, ahead - chain)
                kept = right == (core == 0)

                @pl.when(kept)
                def _():
                    keep_ref[slot, :, cols] = block

                @pl.when(jnp.logical_not(kept))
                def _():
                    give_ref[slot, :, cols] = block


def forward(place, table, own, early, late, grads, ny, chunk):
    pool, width = table.shape
    _, _, pair = own.shape
    part = pair // 2
    main = part // 128 * 128
    step = pool // ny
    return pl.pallas_call(
        functools.partial(forward_kernel, chunk, main, part - main),
        out_shape=(
            jax.ShapeDtypeStruct((pool, part), BF16),
            jax.ShapeDtypeStruct((pool, pair), BF16),
            jax.ShapeDtypeStruct((ny // 2, step, width), BF16),
            jax.ShapeDtypeStruct((ny // 2, step, width), BF16),
            jax.ShapeDtypeStruct((pool, width), BF16),
        ),
        in_specs=[SMEM, ANY, VMEM, VMEM, VMEM, VMEM],
        out_specs=(VMEM, VMEM, VMEM, VMEM, VMEM),
        scratch_shapes=[
            pltpu.VMEM((width // 2, pair), BF16),
            pltpu.SemaphoreType.DMA((pool // chunk,)),
        ],
        compiler_params=params(36),
        cost_estimate=pl.CostEstimate(
            flops=4 * pool * width * pair, bytes_accessed=2 * (2 * pool * width + width * pair), transcendentals=0
        ),
    )(place, table, own, early, late, grads)


def gradient_kernel(nx, nl, nc, table_ref, cots_ref, out_any, total, ready, sems):
    width = table_ref.shape[1]
    span = width // nl
    piece = span // (nx * nc)
    block = nx * piece
    copies = []
    for l in range(nl):
        total[...] = lax.dot_general(
            table_ref[:, l * span : (l + 1) * span], cots_ref[...], (((0,), (0,)), ((), ())),
            preferred_element_type=F32,
        )
        for c in range(nc):
            found = [total[(x * nc + c) * piece : (x * nc + c + 1) * piece, :] for x in range(nx)]
            z = c * nl + l
            ready[z] = jnp.concatenate(found, axis=0).astype(BF16)
            copies.append(
                pltpu.make_async_copy(
                    ready.at[z], out_any.at[pl.ds(z * block, block)], sems.at[z]
                )
            )
            copies[-1].start()
    for copy in copies:
        copy.wait()


def gradient(table, cots, nx, nl, nc):
    pool, width = table.shape
    pair = cots.shape[1]
    return pl.pallas_call(
        functools.partial(gradient_kernel, nx, nl, nc),
        out_shape=jax.ShapeDtypeStruct((width, pair), BF16),
        in_specs=[VMEM, VMEM],
        out_specs=ANY,
        scratch_shapes=[
            pltpu.VMEM((width // nl, pair), F32),
            pltpu.VMEM((nl * nc, width // (nl * nc), pair), BF16),
            pltpu.SemaphoreType.DMA((nl * nc,)),
        ],
        compiler_params=params(32),
        cost_estimate=pl.CostEstimate(
            flops=2 * pool * width * pair, bytes_accessed=2 * (pool * width + width * pair), transcendentals=0
        ),
    )(table, cots)


def swap_over_x(pieces, nx):
    me = lax.axis_index("x")
    got = [lax.dynamic_index_in_dim(pieces, me, 0, keepdims=False)]
    for shift in range(1, nx):
        piece = lax.dynamic_index_in_dim(pieces, lax.rem(me + shift, nx), 0, keepdims=False)
        got.append(lax.ppermute(piece, "x", ring(nx, shift)))
    return got


def row_scale_of(token_vals):
    mean = jnp.mean(token_vals * token_vals, axis=1, keepdims=True)
    return lax.rsqrt(mean + 1e-06).astype(BF16).astype(F32)


def turned(value, outer, inner):
    size = value.shape[1] // (outer * inner)
    blocks = [(o * inner + i) * size for i in range(inner) for o in range(outer)]
    return jnp.concatenate([value[:, at : at + size] for at in blocks], axis=1)


def normalise_kernel(tokens_ref, gain_ref, out_ref):
    token_vals = tokens_ref[...].astype(F32)
    scaled = (token_vals * gain_ref[...]).astype(BF16).astype(F32)
    normed = turned(scaled * row_scale_of(token_vals), out_ref.shape[0], 2).astype(BF16)
    for i in range(out_ref.shape[0]):
        out_ref[i] = normed


def normalise(tokens, gain, copies):
    return pl.pallas_call(
        normalise_kernel,
        out_shape=jax.ShapeDtypeStruct((copies, *tokens.shape), BF16),
        in_specs=[VMEM, VMEM],
        out_specs=VMEM,
        compiler_params=params(8),
    )(tokens, gain)


def gather_kernel(nx, rows, wide, thin, place_ref, near_ref, far_ref, sums_ref, grad_ref, out_ref):
    mine = sums_ref[0 : near_ref.shape[0], :].astype(F32)
    total = near_ref[...].astype(F32) + jnp.where(place_ref[1] == 0, mine, far_ref[...].astype(F32))
    grad = grad_ref[...].astype(F32)
    piece = grad.shape[0] // nx
    pad = jnp.zeros((16 - rows, wide + thin), F32)
    for x in range(nx):
        mine = total[x * rows : (x + 1) * rows]
        for j in range(nx):
            start = nx * wide + j * thin
            both = jnp.concatenate(
                [mine[:, j * wide : (j + 1) * wide], mine[:, start : start + thin]], axis=1
            )
            out_ref[x, 16 * j : 16 * j + 16, :] = jnp.concatenate([both, pad], axis=0).astype(BF16)
        out_ref[x, 16 * nx :, :] = grad[x * piece : (x + 1) * piece].astype(BF16)


def finish_kernel(main, tail, wide, thin, got_ref, tokens_ref, gain_ref, input_ref, gate_ref, up_ref):
    nx = got_ref.shape[0]
    rows, width = tokens_ref.shape
    found = [
        sum(got_ref[x, 16 * j : 16 * j + 16, :].astype(F32) for x in range(nx))[:rows]
        for j in range(nx)
    ]
    token_vals = tokens_ref[...].astype(F32)
    scale = row_scale_of(token_vals)
    gain = gain_ref[...]
    scaled = (token_vals * gain).astype(BF16).astype(F32)
    inner_grad = jnp.concatenate([f[:, :wide] for f in found] + [f[:, wide:] for f in found], axis=1)
    inner_grad = turned(inner_grad, 2, nx) * scale
    inner = jnp.sum(scaled * inner_grad, axis=1, keepdims=True)
    factor = scale * scale / width
    input_ref[...] = (gain * inner_grad - factor * token_vals * inner).astype(BF16)
    for q in range(nx):
        grad = got_ref[q, 16 * nx :, :].astype(F32)
        start = nx * main + q * tail
        gate_ref[:, q * main : (q + 1) * main] = grad[:, :main]
        gate_ref[:, start : start + tail] = grad[:, 2 * main : 2 * main + tail]
        up_ref[:, q * main : (q + 1) * main] = grad[:, main : 2 * main]
        up_ref[:, start : start + tail] = grad[:, 2 * main + tail :]


def spread_kernel(main, tail, place_ref, got_ref, out_ref):
    nx, half, _ = got_ref.shape
    me = place_ref[2]
    for q in range(nx):
        source = lax.rem(me - q + nx, nx)
        start = nx * main + q * tail
        for h in range(2):
            rows = slice(h * half, (h + 1) * half)
            out_ref[rows, q * main : (q + 1) * main] = got_ref[source, :, h * main : (h + 1) * main]
            out_ref[rows, start : start + tail] = got_ref[
                source, :, 2 * main + h * tail : 2 * main + (h + 1) * tail
            ]


def make_step(nc, nx, nl, ny, nk):
    def per_device(tokens, norm_gain, gate_weight, up_weight, hidden_grad):
        rows, width = tokens.shape
        feats, units = gate_weight.shape
        main, tail = share_sizes(units, nx)
        wide, thin = share_sizes(width, nx)
        pair = 2 * (main + tail)
        own_tokens = hidden_grad.shape[0]
        pool = nx * own_tokens
        nz = nc * nl
        place = jnp.stack([lax.axis_index(name) for name in ("l", "k", "x", "y")]).astype(jnp.int32)
        gain = norm_gain.reshape(1, width)

        near = exchange(normalise(tokens, gain, nx), "x").reshape(nx * rows, width)
        table = lax.all_gather(near, ("y", "k"), axis=0, tiled=True)

        cut = feats // 2
        early = lax.ppermute(
            pack_weights(nx, gate_weight, up_weight, cut), ("c", "l", "k"), both_ways(nz)
        )
        own = exchange(pack_weights(nx, gate_weight, up_weight, feats), "x")
        early = exchange(pack_grads(nx, early, hidden_grad), "x")
        late = lax.ppermute(own[:, cut:], ("c", "l", "k"), both_ways(nz))
        grads = sort_grads(early, cut, own_tokens, rows)

        found, cots, keep, give, table = forward(
            place, table, own, early, late, grads, ny, pool // 2
        )
        taken = lax.ppermute(give, "k", [(0, 1), (1, 0)])
        grad = gradient(table, cots, nx, nl, nc)
        taken, grad = lax.optimization_barrier((taken, grad))
        grad = lax.psum_scatter(grad, ("c", "l"), scatter_dimension=0, tiled=True)

        def term(i):
            return keep[i].astype(F32) + taken[i].astype(F32)

        partial = term(0).astype(BF16)
        for i in range(1, ny // 2):
            partial = lax.ppermute(partial, ("y", "k"), both_ways(ny))
            partial = (partial.astype(F32) + term(i)).astype(BF16)
        step = partial.shape[0] // 2
        lower, upper = partial[:step], partial[step:]
        core = lax.axis_index("k")
        near = lax.ppermute(
            jnp.where(core == 0, upper, lower), ("y", "k"),
            [(2 * y, 2 * y + 1) for y in range(ny)]
            + [(2 * y + 1, 2 * ((y - 1) % ny)) for y in range(ny)],
        )
        far = lax.ppermute(
            upper, ("y", "k"), [(2 * y + 1, 2 * ((y - 1) % ny) + 1) for y in range(ny)]
        )

        hidden = jnp.stack(swap_over_x(sort_hidden(found, nx, rows), nx))
        hidden = pl.pallas_call(
            functools.partial(spread_kernel, main, tail),
            out_shape=jax.ShapeDtypeStruct((own_tokens, units), BF16),
            in_specs=[SMEM, VMEM],
            out_specs=VMEM,
            compiler_params=params(8),
        )(place, hidden)
        hidden, near, far = lax.optimization_barrier((hidden, near, far))
        last = pl.pallas_call(
            functools.partial(gather_kernel, nx, rows, wide, thin),
            out_shape=jax.ShapeDtypeStruct((nx, 16 * nx + feats // nc, pair), BF16),
            in_specs=[SMEM, VMEM, VMEM, VMEM, VMEM],
            out_specs=VMEM,
            compiler_params=params(24),
        )(place, near, far, partial, grad)
        last = exchange(last, "x")
        input_grad, gate_grad, up_grad = pl.pallas_call(
            functools.partial(finish_kernel, main, tail, wide, thin),
            out_shape=(
                jax.ShapeDtypeStruct((rows, width), BF16),
                jax.ShapeDtypeStruct((feats // nc, units), F32),
                jax.ShapeDtypeStruct((feats // nc, units), F32),
            ),
            in_specs=[VMEM, VMEM, VMEM],
            out_specs=(VMEM, VMEM, VMEM),
            compiler_params=params(16),
        )(last, tokens, gain)
        return (hidden, input_grad, gate_grad, up_grad)

    return per_device


def solution(mesh):
    fine = split_fsdp(mesh)
    return jax.shard_map(
        make_step(*fine.devices.shape),
        mesh=fine,
        in_specs=(
            P(("c", "x", "l", "y", "k"), None),
            P(),
            P(("x", "l"), ("y", "k")),
            P(("x", "l"), ("y", "k")),
            P(("c", "x", "l"), ("y", "k")),
        ),
        out_specs=(
            P(("c", "x", "l"), ("y", "k")),
            P(("c", "x", "l", "y", "k"), None),
            P(("x", "l", "c"), ("y", "k")),
            P(("x", "l", "c"), ("y", "k")),
        ),
        check_vma=False,
    )
```

```python
import functools

import jax
import jax.numpy as jnp
from jax import lax
from jax.experimental import pallas as pl
from jax.experimental.pallas import tpu as pltpu
from jax.sharding import Mesh
from jax.sharding import PartitionSpec as P

ROOT_TWO_PI = 0.7978845608028654
CUBIC = 0.044715
BF16 = jnp.bfloat16
F32 = jnp.float32
VMEM = pl.BlockSpec(memory_space=pltpu.VMEM)
SMEM = pl.BlockSpec(memory_space=pltpu.SMEM)
ANY = pl.BlockSpec(memory_space=pl.ANY)


def split_fsdp(mesh):
    cuts, fsdp, tensor = mesh.devices.shape
    return Mesh(
        mesh.devices.reshape(cuts, fsdp // 2, 2, tensor // 2, 2), ("c", "x", "l", "y", "k")
    )


def ring(size, shift):
    return [(i, (i + shift) % size) for i in range(size)]


def both_ways(size):
    return [(2 * i, 2 * ((i + 1) % size)) for i in range(size)] + [
        (2 * i + 1, 2 * ((i - 1) % size) + 1) for i in range(size)
    ]


def exchange(value, axis):
    return lax.all_to_all(value, axis, split_axis=0, concat_axis=0, tiled=True)


def params(mib):
    return pltpu.CompilerParams(vmem_limit_bytes=mib * 1024 * 1024)


def share_sizes(units, parts):
    part = units // parts
    main = part // 128 * 128
    return main, part - main


def put_pair(out_ref, q, rows, a, b, main, tail, parts):
    out_ref[q, rows, 0:main] = a[:, q * main : (q + 1) * main]
    out_ref[q, rows, main : 2 * main] = b[:, q * main : (q + 1) * main]
    start = parts * main + q * tail
    out_ref[q, rows, 2 * main : 2 * main + tail] = a[:, start : start + tail]
    out_ref[q, rows, 2 * main + tail : 2 * (main + tail)] = b[:, start : start + tail]


def pack_weights_kernel(main, tail, parts, gate_ref, up_ref, out_ref):
    rows = slice(0, out_ref.shape[1])
    for q in range(parts):
        put_pair(out_ref, q, rows, gate_ref.at[rows], up_ref.at[rows], main, tail, parts)


def pack_weights(parts, gate, up, rows):
    main, tail = share_sizes(gate.shape[1], parts)
    return pl.pallas_call(
        functools.partial(pack_weights_kernel, main, tail, parts),
        out_shape=jax.ShapeDtypeStruct((parts, rows, 2 * (main + tail)), BF16),
        in_specs=[VMEM, VMEM],
        out_specs=VMEM,
        compiler_params=params(16),
    )(gate, up)


def pack_grads_kernel(main, tail, parts, weights_ref, grad_ref, out_ref):
    cut = weights_ref.shape[1]
    half = grad_ref.shape[0] // 2
    out_ref[:, 0:cut, :] = weights_ref[...]
    for q in range(parts):
        put_pair(
            out_ref, q, slice(cut, cut + half),
            grad_ref.at[0:half], grad_ref.at[half : 2 * half], main, tail, parts,
        )


def pack_grads(parts, weights, grads):
    main, tail = share_sizes(grads.shape[1], parts)
    rows = weights.shape[1] + grads.shape[0] // 2 + 32
    return pl.pallas_call(
        functools.partial(pack_grads_kernel, main, tail, parts),
        out_shape=jax.ShapeDtypeStruct((parts, rows, 2 * (main + tail)), BF16),
        in_specs=[VMEM, VMEM],
        out_specs=VMEM,
        compiler_params=params(16),
    )(weights, grads)


def activate(gate, upward, cotangent):
    square = gate * gate
    tangent = jnp.tanh(ROOT_TWO_PI * (gate + CUBIC * square * gate))
    active = 0.5 * gate * (1.0 + tangent)
    slope = 0.5 * (1.0 + tangent) + 0.5 * gate * (1.0 - tangent * tangent) * ROOT_TWO_PI * (
        1.0 + 3.0 * CUBIC * square
    )
    hidden = (active * upward).astype(BF16)
    return hidden, (cotangent * upward * slope).astype(BF16), (cotangent * active).astype(BF16)


def split_index(value, size, top):
    factor = (1 << 20) // size + 1
    assert all(i * factor >> 20 == i // size for i in range(top))
    high = (value * factor) >> 20
    return high, value - high * size


def shuffle(pool, outer, inner, rows):
    index = lax.broadcasted_iota(jnp.int32, (pool, 1), 0)
    high, rest = split_index(index, inner * rows, pool)
    mid, low = split_index(rest, rows, inner * rows)
    source = mid * (outer * rows) + high * rows + low
    columns = lax.broadcasted_iota(jnp.int32, (pool, pool), 1)
    return (columns == source).astype(F32).astype(BF16)


SORTED = 4


def sort_grads_kernel(main, tail, cut, rows_each, raw_ref, out_ref):
    blocks = raw_ref.shape[0]
    size = SORTED * rows_each
    half = out_ref.shape[0] // (2 * blocks)
    order = shuffle(blocks * size, SORTED, blocks, rows_each)
    for g in range(2 * half // size):
        h, at = g * size // half, cut + g * size % half
        found = [raw_ref[x, at : at + size, :] for x in range(blocks)]
        found = jnp.concatenate(found, axis=0)
        rows = slice(g * blocks * size, (g + 1) * blocks * size)
        for lanes, first, width in (
            (slice(0, main), h * main, main), (slice(main, main + tail), 2 * main + h * tail, tail)
        ):
            out_ref[rows, lanes] = jnp.dot(
                order, found[:, first : first + width], preferred_element_type=F32
            ).astype(BF16)


def sort_grads(raw, cut, own_tokens, rows_each):
    blocks, _, pair = raw.shape
    main = pair // 2 // 128 * 128
    return pl.pallas_call(
        functools.partial(sort_grads_kernel, main, pair // 2 - main, cut, rows_each),
        out_shape=jax.ShapeDtypeStruct((blocks * own_tokens, pair // 2), BF16),
        in_specs=[VMEM],
        out_specs=VMEM,
        compiler_params=params(16),
    )(raw)


def sort_hidden_kernel(main, tail, rows_each, found_ref, out_ref):
    blocks, half, _ = out_ref.shape
    size = SORTED * rows_each
    order = shuffle(blocks * size, blocks, SORTED, rows_each)
    for g in range(2 * half // size):
        h, at = g * size // half, g * size % half
        rows = slice(g * blocks * size, (g + 1) * blocks * size)
        for lanes, first, width in (
            (slice(0, main), h * main, main), (slice(main, main + tail), 2 * main + h * tail, tail)
        ):
            got = jnp.dot(order, found_ref[rows, lanes], preferred_element_type=F32).astype(BF16)
            for x in range(blocks):
                out_ref[x, at : at + size, first : first + width] = got[x * size : (x + 1) * size]


def sort_hidden(found, blocks, rows_each):
    pool, part = found.shape
    main = part // 128 * 128
    return pl.pallas_call(
        functools.partial(sort_hidden_kernel, main, part - main, rows_each),
        out_shape=jax.ShapeDtypeStruct((blocks, pool // blocks // 2, 2 * part), BF16),
        in_specs=[VMEM],
        out_specs=VMEM,
        compiler_params=params(16),
    )(found)


def forward_kernel(
    chunk, main, tail, place_ref, table_ref, own_ref, early_ref, late_ref, grads_ref,
    found_ref, cots_ref, keep_ref, give_ref, matrix,
):
    blocks, feats, pair = own_ref.shape
    cut = feats - late_ref.shape[1]
    pool, width = table_ref.shape
    low, core, me = place_ref[0], place_ref[1], place_ref[3]
    chain, step, _ = keep_ref.shape
    near = low * (width // 2)
    far = (1 - low) * (width // 2)
    for x in range(blocks):
        for first, size, rows in (
            (near + x * feats, feats, own_ref[x]),
            (far + x * feats, cut, early_ref[x, :cut, :]),
            (far + x * feats + cut, feats - cut, late_ref[x]),
        ):
            matrix[pl.ds(pl.multiple_of(first, 16), size), :] = rows
    for first in range(0, pool, chunk):
        rows = slice(first, first + chunk)
        both = jnp.dot(table_ref[rows, :], matrix[...], preferred_element_type=F32)
        grads = grads_ref[rows, :].astype(F32)
        hidden, gate_cot, up_cot = activate(
            both[:, :main], both[:, main : 2 * main], grads[:, :main]
        )
        found_ref[rows, :main] = hidden
        cots_ref[rows, :main] = gate_cot
        cots_ref[rows, main : 2 * main] = up_cot
        rest = both[:, 2 * main :]
        hidden, gate_cot, up_cot = activate(rest[:, :tail], rest[:, tail:], grads[:, main:])
        found_ref[rows, main:] = hidden
        cots_ref[rows, 2 * main : 2 * main + tail] = gate_cot
        cots_ref[rows, 2 * main + tail :] = up_cot
        partial = lax.dot_general(
            cots_ref[rows, :], matrix[...], (((1,), (1,)), ((), ())), preferred_element_type=F32
        )
        for j in range(chunk // step):
            block = partial[j * step : (j + 1) * step].astype(BF16)
            ahead = lax.rem(first // step + j - me + 2 * chain, 2 * chain)
            right = ahead < chain
            slot = jnp.where(right, chain - 1 - ahead, ahead - chain)
            kept = right == (core == 0)

            @pl.when(kept)
            def _():
                keep_ref[slot] = block

            @pl.when(jnp.logical_not(kept))
            def _():
                give_ref[slot] = block


def forward(place, table, own, early, late, grads, ny, chunk):
    pool, width = table.shape
    _, _, pair = own.shape
    part = pair // 2
    main = part // 128 * 128
    step = pool // ny
    return pl.pallas_call(
        functools.partial(forward_kernel, chunk, main, part - main),
        out_shape=(
            jax.ShapeDtypeStruct((pool, part), BF16),
            jax.ShapeDtypeStruct((pool, pair), BF16),
            jax.ShapeDtypeStruct((ny // 2, step, width), BF16),
            jax.ShapeDtypeStruct((ny // 2, step, width), BF16),
        ),
        in_specs=[SMEM, VMEM, VMEM, VMEM, VMEM, VMEM],
        out_specs=(VMEM, VMEM, VMEM, VMEM),
        scratch_shapes=[pltpu.VMEM((width, pair), BF16)],
        compiler_params=params(32),
        cost_estimate=pl.CostEstimate(
            flops=4 * pool * width * pair, bytes_accessed=2 * (2 * pool * width + width * pair), transcendentals=0
        ),
    )(place, table, own, early, late, grads)


def gradient_kernel(nx, nl, nc, table_ref, cots_ref, out_any, total, ready, sems):
    width = table_ref.shape[1]
    span = width // nl
    piece = span // (nx * nc)
    block = nx * piece
    copies = []
    for l in range(nl):
        total[...] = lax.dot_general(
            table_ref[:, l * span : (l + 1) * span], cots_ref[...], (((0,), (0,)), ((), ())),
            preferred_element_type=F32,
        )
        for c in range(nc):
            found = [total[(x * nc + c) * piece : (x * nc + c + 1) * piece, :] for x in range(nx)]
            z = c * nl + l
            ready[z] = jnp.concatenate(found, axis=0).astype(BF16)
            copies.append(
                pltpu.make_async_copy(
                    ready.at[z], out_any.at[pl.ds(z * block, block)], sems.at[z]
                )
            )
            copies[-1].start()
    for copy in copies:
        copy.wait()


def gradient(table, cots, nx, nl, nc):
    pool, width = table.shape
    pair = cots.shape[1]
    return pl.pallas_call(
        functools.partial(gradient_kernel, nx, nl, nc),
        out_shape=jax.ShapeDtypeStruct((width, pair), BF16),
        in_specs=[VMEM, VMEM],
        out_specs=ANY,
        scratch_shapes=[
            pltpu.VMEM((width // nl, pair), F32),
            pltpu.VMEM((nl * nc, width // (nl * nc), pair), BF16),
            pltpu.SemaphoreType.DMA((nl * nc,)),
        ],
        compiler_params=params(32),
        cost_estimate=pl.CostEstimate(
            flops=2 * pool * width * pair, bytes_accessed=2 * (pool * width + width * pair), transcendentals=0
        ),
    )(table, cots)


def row_scale_of(token_vals):
    mean = jnp.mean(token_vals * token_vals, axis=1, keepdims=True)
    return lax.rsqrt(mean + 1e-06).astype(BF16).astype(F32)


def turned(value, outer, inner):
    size = value.shape[1] // (outer * inner)
    blocks = [(o * inner + i) * size for i in range(inner) for o in range(outer)]
    return jnp.concatenate([value[:, at : at + size] for at in blocks], axis=1)


def normalise_kernel(tokens_ref, gain_ref, out_ref):
    token_vals = tokens_ref[...].astype(F32)
    gain = gain_ref[...].reshape(1, tokens_ref.shape[1])
    scaled = (token_vals * gain).astype(BF16).astype(F32)
    normed = turned(scaled * row_scale_of(token_vals), out_ref.shape[0], 2).astype(BF16)
    for i in range(out_ref.shape[0]):
        out_ref[i] = normed


def normalise(tokens, gain, copies):
    return pl.pallas_call(
        normalise_kernel,
        out_shape=jax.ShapeDtypeStruct((copies, *tokens.shape), BF16),
        in_specs=[VMEM, VMEM],
        out_specs=VMEM,
        compiler_params=params(8),
    )(tokens, gain)


def gather_kernel(nx, rows, wide, thin, place_ref, near_ref, far_ref, sums_ref, grad_ref, out_ref):
    mine = sums_ref[0 : near_ref.shape[0], :].astype(F32)
    total = near_ref[...].astype(F32) + jnp.where(place_ref[1] == 0, mine, far_ref[...].astype(F32))
    grad = grad_ref[...].astype(F32)
    piece = grad.shape[0] // nx
    pad = jnp.zeros((16 - rows, wide + thin), F32)
    for x in range(nx):
        mine = total[x * rows : (x + 1) * rows]
        for j in range(nx):
            start = nx * wide + j * thin
            both = jnp.concatenate(
                [mine[:, j * wide : (j + 1) * wide], mine[:, start : start + thin]], axis=1
            )
            out_ref[x, 16 * j : 16 * j + 16, :] = jnp.concatenate([both, pad], axis=0).astype(BF16)
        out_ref[x, 16 * nx :, :] = grad[x * piece : (x + 1) * piece].astype(BF16)


def finish_kernel(main, tail, wide, thin, got_ref, tokens_ref, gain_ref, input_ref, gate_ref, up_ref):
    nx = got_ref.shape[0]
    rows, width = tokens_ref.shape
    found = [
        sum(got_ref[x, 16 * j : 16 * j + 16, :].astype(F32) for x in range(nx))[:rows]
        for j in range(nx)
    ]
    token_vals = tokens_ref[...].astype(F32)
    scale = row_scale_of(token_vals)
    gain = gain_ref[...].reshape(1, width)
    scaled = (token_vals * gain).astype(BF16).astype(F32)
    inner_grad = jnp.concatenate([f[:, :wide] for f in found] + [f[:, wide:] for f in found], axis=1)
    inner_grad = turned(inner_grad, 2, nx) * scale
    inner = jnp.sum(scaled * inner_grad, axis=1, keepdims=True)
    factor = scale * scale / width
    input_ref[...] = (gain * inner_grad - factor * token_vals * inner).astype(BF16)
    for q in range(nx):
        grad = got_ref[q, 16 * nx :, :].astype(F32)
        start = nx * main + q * tail
        gate_ref[:, q * main : (q + 1) * main] = grad[:, :main]
        gate_ref[:, start : start + tail] = grad[:, 2 * main : 2 * main + tail]
        up_ref[:, q * main : (q + 1) * main] = grad[:, main : 2 * main]
        up_ref[:, start : start + tail] = grad[:, 2 * main + tail :]


def spread_kernel(main, tail, got_ref, out_ref):
    nx, half, _ = got_ref.shape
    for q in range(nx):
        start = nx * main + q * tail
        for h in range(2):
            rows = slice(h * half, (h + 1) * half)
            out_ref[rows, q * main : (q + 1) * main] = got_ref[q, :, h * main : (h + 1) * main]
            out_ref[rows, start : start + tail] = got_ref[
                q, :, 2 * main + h * tail : 2 * main + (h + 1) * tail
            ]


def make_step(nc, nx, nl, ny, nk):
    def per_device(tokens, norm_gain, gate_weight, up_weight, hidden_grad):
        rows, width = tokens.shape
        feats, units = gate_weight.shape
        main, tail = share_sizes(units, nx)
        wide, thin = share_sizes(width, nx)
        pair = 2 * (main + tail)
        own_tokens = hidden_grad.shape[0]
        pool = nx * own_tokens
        nz = nc * nl
        place = jnp.stack([lax.axis_index(name) for name in ("l", "k", "x", "y")]).astype(jnp.int32)

        near = exchange(normalise(tokens, norm_gain, nx), "x").reshape(nx * rows, width)
        table = lax.all_gather(near, ("y", "k"), axis=0, tiled=True)

        cut = feats // 2
        early = lax.ppermute(
            pack_weights(nx, gate_weight, up_weight, cut), ("c", "l", "k"), both_ways(nz)
        )
        own = exchange(pack_weights(nx, gate_weight, up_weight, feats), "x")
        early = exchange(pack_grads(nx, early, hidden_grad), "x")
        late = lax.ppermute(own[:, cut:], ("c", "l", "k"), both_ways(nz))
        grads = sort_grads(early, cut, own_tokens, rows)

        found, cots, keep, give = forward(place, table, own, early, late, grads, ny, pool)
        taken = lax.ppermute(give, "k", [(0, 1), (1, 0)])
        grad = gradient(table, cots, nx, nl, nc)
        taken, grad = lax.optimization_barrier((taken, grad))
        grad = lax.psum_scatter(grad, ("c", "l"), scatter_dimension=0, tiled=True)

        def term(i):
            return keep[i].astype(F32) + taken[i].astype(F32)

        hidden = exchange(sort_hidden(found, nx, rows), "x")
        partial = term(0).astype(BF16)
        for i in range(1, ny // 2):
            partial = lax.ppermute(partial, ("y", "k"), both_ways(ny))
            if i == ny // 2 - 1:
                partial, hidden = lax.optimization_barrier((partial, hidden))
            partial = (partial.astype(F32) + term(i)).astype(BF16)
        step = partial.shape[0] // 2
        lower, upper = partial[:step], partial[step:]
        core = lax.axis_index("k")
        near = lax.ppermute(
            jnp.where(core == 0, upper, lower), ("y", "k"),
            [(2 * y, 2 * y + 1) for y in range(ny)]
            + [(2 * y + 1, 2 * ((y - 1) % ny)) for y in range(ny)],
        )
        far = lax.ppermute(
            upper, ("y", "k"), [(2 * y + 1, 2 * ((y - 1) % ny) + 1) for y in range(ny)]
        )

        hidden = pl.pallas_call(
            functools.partial(spread_kernel, main, tail),
            out_shape=jax.ShapeDtypeStruct((own_tokens, units), BF16),
            in_specs=[VMEM],
            out_specs=VMEM,
            compiler_params=params(8),
        )(hidden)
        hidden, near, far = lax.optimization_barrier((hidden, near, far))
        last = pl.pallas_call(
            functools.partial(gather_kernel, nx, rows, wide, thin),
            out_shape=jax.ShapeDtypeStruct((nx, 16 * nx + feats // nc, pair), BF16),
            in_specs=[SMEM, VMEM, VMEM, VMEM, VMEM],
            out_specs=VMEM,
            compiler_params=params(24),
        )(place, near, far, partial, grad)
        last = exchange(last, "x")
        input_grad, gate_grad, up_grad = pl.pallas_call(
            functools.partial(finish_kernel, main, tail, wide, thin),
            out_shape=(
                jax.ShapeDtypeStruct((rows, width), BF16),
                jax.ShapeDtypeStruct((feats // nc, units), F32),
                jax.ShapeDtypeStruct((feats // nc, units), F32),
            ),
            in_specs=[VMEM, VMEM, VMEM],
            out_specs=(VMEM, VMEM, VMEM),
            compiler_params=params(16),
        )(last, tokens, norm_gain)
        return (hidden, input_grad, gate_grad, up_grad)

    return per_device


def solution(mesh):
    fine = split_fsdp(mesh)
    return jax.shard_map(
        make_step(*fine.devices.shape),
        mesh=fine,
        in_specs=(
            P(("c", "x", "l", "y", "k"), None),
            P(),
            P(("x", "l"), ("y", "k")),
            P(("x", "l"), ("y", "k")),
            P(("c", "x", "l"), ("y", "k")),
        ),
        out_specs=(
            P(("c", "x", "l"), ("y", "k")),
            P(("c", "x", "l", "y", "k"), None),
            P(("x", "l", "c"), ("y", "k")),
            P(("x", "l", "c"), ("y", "k")),
        ),
        check_vma=False,
    )
```

```python
import functools

import jax
import jax.numpy as jnp
from jax import lax
from jax.experimental import pallas as pl
from jax.experimental.pallas import tpu as pltpu
from jax.sharding import Mesh
from jax.sharding import PartitionSpec as P

ROOT_TWO_PI = 0.7978845608028654
CUBIC = 0.044715
BF16 = jnp.bfloat16
F32 = jnp.float32
VMEM = pl.BlockSpec(memory_space=pltpu.VMEM)
SMEM = pl.BlockSpec(memory_space=pltpu.SMEM)
ANY = pl.BlockSpec(memory_space=pl.ANY)


def split_fsdp(mesh):
    cuts, fsdp, tensor = mesh.devices.shape
    return Mesh(
        mesh.devices.reshape(cuts, fsdp // 2, 2, tensor // 2, 2), ("c", "x", "l", "y", "k")
    )


def ring(size, shift):
    return [(i, (i + shift) % size) for i in range(size)]


def both_ways(size):
    return [(2 * i, 2 * ((i + 1) % size)) for i in range(size)] + [
        (2 * i + 1, 2 * ((i - 1) % size) + 1) for i in range(size)
    ]


def exchange(value, axis):
    return lax.all_to_all(value, axis, split_axis=0, concat_axis=0, tiled=True)


def params(mib):
    return pltpu.CompilerParams(vmem_limit_bytes=mib * 1024 * 1024)


def share_sizes(units, parts):
    part = units // parts
    main = part // 128 * 128
    return main, part - main


def put_pair(out_ref, q, rows, a, b, main, tail, parts):
    out_ref[q, rows, 0:main] = a[:, q * main : (q + 1) * main]
    out_ref[q, rows, main : 2 * main] = b[:, q * main : (q + 1) * main]
    start = parts * main + q * tail
    out_ref[q, rows, 2 * main : 2 * main + tail] = a[:, start : start + tail]
    out_ref[q, rows, 2 * main + tail : 2 * (main + tail)] = b[:, start : start + tail]


def pack_weights_kernel(main, tail, parts, gate_ref, up_ref, out_ref):
    rows = slice(0, out_ref.shape[1])
    for q in range(parts):
        put_pair(out_ref, q, rows, gate_ref.at[rows], up_ref.at[rows], main, tail, parts)


def pack_weights(parts, gate, up, rows):
    main, tail = share_sizes(gate.shape[1], parts)
    return pl.pallas_call(
        functools.partial(pack_weights_kernel, main, tail, parts),
        out_shape=jax.ShapeDtypeStruct((parts, rows, 2 * (main + tail)), BF16),
        in_specs=[VMEM, VMEM],
        out_specs=VMEM,
        compiler_params=params(16),
    )(gate, up)


def pack_grads_kernel(main, tail, parts, weights_ref, grad_ref, out_ref):
    cut = weights_ref.shape[1]
    half = grad_ref.shape[0] // 2
    out_ref[:, 0:cut, :] = weights_ref[...]
    for q in range(parts):
        put_pair(
            out_ref, q, slice(cut, cut + half),
            grad_ref.at[0:half], grad_ref.at[half : 2 * half], main, tail, parts,
        )


def pack_grads(parts, weights, grads):
    main, tail = share_sizes(grads.shape[1], parts)
    rows = weights.shape[1] + grads.shape[0] // 2 + 32
    return pl.pallas_call(
        functools.partial(pack_grads_kernel, main, tail, parts),
        out_shape=jax.ShapeDtypeStruct((parts, rows, 2 * (main + tail)), BF16),
        in_specs=[VMEM, VMEM],
        out_specs=VMEM,
        compiler_params=params(16),
    )(weights, grads)


def activate(gate, upward, cotangent):
    square = gate * gate
    tangent = jnp.tanh(ROOT_TWO_PI * (gate + CUBIC * square * gate))
    active = 0.5 * gate * (1.0 + tangent)
    slope = 0.5 * (1.0 + tangent) + 0.5 * gate * (1.0 - tangent * tangent) * ROOT_TWO_PI * (
        1.0 + 3.0 * CUBIC * square
    )
    hidden = (active * upward).astype(BF16)
    return hidden, (cotangent * upward * slope).astype(BF16), (cotangent * active).astype(BF16)


def split_index(value, size, top):
    factor = (1 << 20) // size + 1
    assert all(i * factor >> 20 == i // size for i in range(top))
    high = (value * factor) >> 20
    return high, value - high * size


def shuffle(pool, outer, inner, rows):
    index = lax.broadcasted_iota(jnp.int32, (pool, 1), 0)
    high, rest = split_index(index, inner * rows, pool)
    mid, low = split_index(rest, rows, inner * rows)
    source = mid * (outer * rows) + high * rows + low
    columns = lax.broadcasted_iota(jnp.int32, (pool, pool), 1)
    return (columns == source).astype(F32).astype(BF16)


SORTED = 4


def sort_grads_kernel(main, tail, cut, rows_each, raw_ref, out_ref):
    blocks = raw_ref.shape[0]
    size = SORTED * rows_each
    half = out_ref.shape[0] // (2 * blocks)
    order = shuffle(blocks * size, SORTED, blocks, rows_each)
    for g in range(2 * half // size):
        h, at = g * size // half, cut + g * size % half
        found = [raw_ref[x, at : at + size, :] for x in range(blocks)]
        found = jnp.concatenate(found, axis=0)
        rows = slice(g * blocks * size, (g + 1) * blocks * size)
        for lanes, first, width in (
            (slice(0, main), h * main, main), (slice(main, main + tail), 2 * main + h * tail, tail)
        ):
            out_ref[rows, lanes] = jnp.dot(
                order, found[:, first : first + width], preferred_element_type=F32
            ).astype(BF16)


def sort_grads(raw, cut, own_tokens, rows_each):
    blocks, _, pair = raw.shape
    main = pair // 2 // 128 * 128
    return pl.pallas_call(
        functools.partial(sort_grads_kernel, main, pair // 2 - main, cut, rows_each),
        out_shape=jax.ShapeDtypeStruct((blocks * own_tokens, pair // 2), BF16),
        in_specs=[VMEM],
        out_specs=VMEM,
        compiler_params=params(16),
    )(raw)


def sort_hidden_kernel(main, tail, rows_each, found_ref, out_ref):
    blocks, half, _ = out_ref.shape
    size = SORTED * rows_each
    order = shuffle(blocks * size, blocks, SORTED, rows_each)
    for g in range(2 * half // size):
        h, at = g * size // half, g * size % half
        rows = slice(g * blocks * size, (g + 1) * blocks * size)
        for lanes, first, width in (
            (slice(0, main), h * main, main), (slice(main, main + tail), 2 * main + h * tail, tail)
        ):
            got = jnp.dot(order, found_ref[rows, lanes], preferred_element_type=F32).astype(BF16)
            for x in range(blocks):
                out_ref[x, at : at + size, first : first + width] = got[x * size : (x + 1) * size]


def sort_hidden(found, blocks, rows_each):
    pool, part = found.shape
    main = part // 128 * 128
    return pl.pallas_call(
        functools.partial(sort_hidden_kernel, main, part - main, rows_each),
        out_shape=jax.ShapeDtypeStruct((blocks, pool // blocks // 2, 2 * part), BF16),
        in_specs=[VMEM],
        out_specs=VMEM,
        compiler_params=params(16),
    )(found)


def forward_kernel(
    chunk, main, tail, place_ref, table_ref, own_ref, early_ref, late_ref, grads_ref,
    found_ref, cots_ref, keep_ref, give_ref, matrix,
):
    blocks, feats, pair = own_ref.shape
    cut = feats - late_ref.shape[1]
    pool, width = table_ref.shape
    low, core, me = place_ref[0], place_ref[1], place_ref[3]
    _, chain, step, _ = keep_ref.shape
    near = low * (width // 2)
    far = (1 - low) * (width // 2)
    for x in range(blocks):
        for first, size, rows in (
            (near + x * feats, feats, own_ref[x]),
            (far + x * feats, cut, early_ref[x, :cut, :]),
            (far + x * feats + cut, feats - cut, late_ref[x]),
        ):
            matrix[pl.ds(pl.multiple_of(first, 16), size), :] = rows
    for first in range(0, pool, chunk):
        rows = slice(first, first + chunk)
        both = jnp.dot(table_ref[rows, :], matrix[...], preferred_element_type=F32)
        grads = grads_ref[rows, :].astype(F32)
        hidden, gate_cot, up_cot = activate(
            both[:, :main], both[:, main : 2 * main], grads[:, :main]
        )
        found_ref[rows, :main] = hidden
        cots_ref[rows, :main] = gate_cot
        cots_ref[rows, main : 2 * main] = up_cot
        rest = both[:, 2 * main :]
        hidden, gate_cot, up_cot = activate(rest[:, :tail], rest[:, tail:], grads[:, main:])
        found_ref[rows, main:] = hidden
        cots_ref[rows, 2 * main : 2 * main + tail] = gate_cot
        cots_ref[rows, 2 * main + tail :] = up_cot
        partial = lax.dot_general(
            cots_ref[rows, :], matrix[...], (((1,), (1,)), ((), ())), preferred_element_type=F32
        )
        for j in range(chunk // (2 * step)):
            even = partial[2 * j * step : (2 * j + 1) * step]
            odd = partial[(2 * j + 1) * step : (2 * j + 2) * step]
            ahead = lax.rem(first // (2 * step) + j - me + 2 * chain, 2 * chain)
            right = ahead < chain
            side = jnp.where(right, 0, 1)
            slot = jnp.where(right, chain - 1 - ahead, ahead - chain)
            straight = right == (core == 0)
            keep_ref[side, slot] = jnp.where(straight, even, odd).astype(BF16)
            give_ref[side, slot] = jnp.where(straight, odd, even).astype(BF16)


def forward(place, table, own, early, late, grads, ny, chunk):
    pool, width = table.shape
    _, _, pair = own.shape
    part = pair // 2
    main = part // 128 * 128
    step = pool // (2 * ny)
    return pl.pallas_call(
        functools.partial(forward_kernel, chunk, main, part - main),
        out_shape=(
            jax.ShapeDtypeStruct((pool, part), BF16),
            jax.ShapeDtypeStruct((pool, pair), BF16),
            jax.ShapeDtypeStruct((2, ny // 2, step, width), BF16),
            jax.ShapeDtypeStruct((2, ny // 2, step, width), BF16),
        ),
        in_specs=[SMEM, VMEM, VMEM, VMEM, VMEM, VMEM],
        out_specs=(VMEM, VMEM, VMEM, VMEM),
        scratch_shapes=[pltpu.VMEM((width, pair), BF16)],
        compiler_params=params(32),
        cost_estimate=pl.CostEstimate(
            flops=4 * pool * width * pair, bytes_accessed=2 * (2 * pool * width + width * pair), transcendentals=0
        ),
    )(place, table, own, early, late, grads)


def gradient_kernel(nx, nl, nc, table_ref, cots_ref, out_any, total, ready, sems):
    width = table_ref.shape[1]
    span = width // nl
    piece = span // (nx * nc)
    block = nx * piece
    copies = []
    for l in range(nl):
        total[...] = lax.dot_general(
            table_ref[:, l * span : (l + 1) * span], cots_ref[...], (((0,), (0,)), ((), ())),
            preferred_element_type=F32,
        )
        for c in range(nc):
            found = [total[(x * nc + c) * piece : (x * nc + c + 1) * piece, :] for x in range(nx)]
            z = c * nl + l
            ready[z] = jnp.concatenate(found, axis=0).astype(BF16)
            copies.append(
                pltpu.make_async_copy(
                    ready.at[z], out_any.at[pl.ds(z * block, block)], sems.at[z]
                )
            )
            copies[-1].start()
    for copy in copies:
        copy.wait()


def gradient(table, cots, nx, nl, nc):
    pool, width = table.shape
    pair = cots.shape[1]
    return pl.pallas_call(
        functools.partial(gradient_kernel, nx, nl, nc),
        out_shape=jax.ShapeDtypeStruct((width, pair), BF16),
        in_specs=[VMEM, VMEM],
        out_specs=ANY,
        scratch_shapes=[
            pltpu.VMEM((width // nl, pair), F32),
            pltpu.VMEM((nl * nc, width // (nl * nc), pair), BF16),
            pltpu.SemaphoreType.DMA((nl * nc,)),
        ],
        compiler_params=params(32),
        cost_estimate=pl.CostEstimate(
            flops=2 * pool * width * pair, bytes_accessed=2 * (pool * width + width * pair), transcendentals=0
        ),
    )(table, cots)


def row_scale_of(token_vals):
    mean = jnp.mean(token_vals * token_vals, axis=1, keepdims=True)
    return lax.rsqrt(mean + 1e-06).astype(BF16).astype(F32)


def turned(value, outer, inner):
    size = value.shape[1] // (outer * inner)
    blocks = [(o * inner + i) * size for i in range(inner) for o in range(outer)]
    return jnp.concatenate([value[:, at : at + size] for at in blocks], axis=1)


def normalise_kernel(tokens_ref, gain_ref, out_ref):
    token_vals = tokens_ref[...].astype(F32)
    gain = gain_ref[...].reshape(1, tokens_ref.shape[1])
    scaled = (token_vals * gain).astype(BF16).astype(F32)
    normed = turned(scaled * row_scale_of(token_vals), out_ref.shape[0], 2).astype(BF16)
    for i in range(out_ref.shape[0]):
        out_ref[i] = normed


def normalise(tokens, gain, copies):
    return pl.pallas_call(
        normalise_kernel,
        out_shape=jax.ShapeDtypeStruct((copies, *tokens.shape), BF16),
        in_specs=[VMEM, VMEM],
        out_specs=VMEM,
        compiler_params=params(8),
    )(tokens, gain)


def gather_kernel(nx, rows, wide, thin, right_ref, left_ref, grad_ref, out_ref):
    total = right_ref[...].astype(F32) + left_ref[...].astype(F32)
    grad = grad_ref[...].astype(F32)
    piece = grad.shape[0] // nx
    pad = jnp.zeros((16 - rows, wide + thin), F32)
    for x in range(nx):
        mine = total[x * rows : (x + 1) * rows]
        for j in range(nx):
            start = nx * wide + j * thin
            both = jnp.concatenate(
                [mine[:, j * wide : (j + 1) * wide], mine[:, start : start + thin]], axis=1
            )
            out_ref[x, 16 * j : 16 * j + 16, :] = jnp.concatenate([both, pad], axis=0).astype(BF16)
        out_ref[x, 16 * nx :, :] = grad[x * piece : (x + 1) * piece].astype(BF16)


def finish_kernel(main, tail, wide, thin, got_ref, tokens_ref, gain_ref, input_ref, gate_ref, up_ref):
    nx = got_ref.shape[0]
    rows, width = tokens_ref.shape
    found = [
        sum(got_ref[x, 16 * j : 16 * j + 16, :].astype(F32) for x in range(nx))[:rows]
        for j in range(nx)
    ]
    token_vals = tokens_ref[...].astype(F32)
    scale = row_scale_of(token_vals)
    gain = gain_ref[...].reshape(1, width)
    scaled = (token_vals * gain).astype(BF16).astype(F32)
    inner_grad = jnp.concatenate([f[:, :wide] for f in found] + [f[:, wide:] for f in found], axis=1)
    inner_grad = turned(inner_grad, 2, nx) * scale
    inner = jnp.sum(scaled * inner_grad, axis=1, keepdims=True)
    factor = scale * scale / width
    input_ref[...] = (gain * inner_grad - factor * token_vals * inner).astype(BF16)
    for q in range(nx):
        grad = got_ref[q, 16 * nx :, :].astype(F32)
        start = nx * main + q * tail
        gate_ref[:, q * main : (q + 1) * main] = grad[:, :main]
        gate_ref[:, start : start + tail] = grad[:, 2 * main : 2 * main + tail]
        up_ref[:, q * main : (q + 1) * main] = grad[:, main : 2 * main]
        up_ref[:, start : start + tail] = grad[:, 2 * main + tail :]


def spread_kernel(main, tail, got_ref, out_ref):
    nx, half, _ = got_ref.shape
    for q in range(nx):
        start = nx * main + q * tail
        for h in range(2):
            rows = slice(h * half, (h + 1) * half)
            out_ref[rows, q * main : (q + 1) * main] = got_ref[q, :, h * main : (h + 1) * main]
            out_ref[rows, start : start + tail] = got_ref[
                q, :, 2 * main + h * tail : 2 * main + (h + 1) * tail
            ]


def make_step(nc, nx, nl, ny, nk):
    def per_device(tokens, norm_gain, gate_weight, up_weight, hidden_grad):
        rows, width = tokens.shape
        feats, units = gate_weight.shape
        main, tail = share_sizes(units, nx)
        wide, thin = share_sizes(width, nx)
        pair = 2 * (main + tail)
        own_tokens = hidden_grad.shape[0]
        pool = nx * own_tokens
        nz = nc * nl
        place = jnp.stack([lax.axis_index(name) for name in ("l", "k", "x", "y")]).astype(jnp.int32)

        near = exchange(normalise(tokens, norm_gain, nx), "x").reshape(nx * rows, width)
        table = lax.all_gather(near, ("y", "k"), axis=0, tiled=True)

        cut = feats // 2
        early = lax.ppermute(
            pack_weights(nx, gate_weight, up_weight, cut), ("c", "l", "k"), both_ways(nz)
        )
        own = exchange(pack_weights(nx, gate_weight, up_weight, feats), "x")
        early = exchange(pack_grads(nx, early, hidden_grad), "x")
        late = lax.ppermute(own[:, cut:], ("c", "l", "k"), both_ways(nz))
        table, early = lax.optimization_barrier((table, early))
        grads = sort_grads(early, cut, own_tokens, rows)

        found, cots, keep, give = forward(place, table, own, early, late, grads, ny, pool)
        taken = lax.ppermute(give, "k", [(0, 1), (1, 0)])
        grad = gradient(table, cots, nx, nl, nc)
        taken, grad = lax.optimization_barrier((taken, grad))
        grad = lax.psum_scatter(grad, ("c", "l"), scatter_dimension=0, tiled=True)

        def term(side, i):
            return keep[side, i].astype(F32) + taken[side, i].astype(F32)

        hidden = exchange(sort_hidden(found, nx, rows), "x")
        right, left = term(0, 0).astype(BF16), term(1, 0).astype(BF16)
        for i in range(1, ny // 2):
            right = lax.ppermute(right, "y", ring(ny, 1))
            left = lax.ppermute(left, "y", ring(ny, -1))
            if i == ny // 2 - 1:
                right, hidden = lax.optimization_barrier((right, hidden))
            right = (right.astype(F32) + term(0, i)).astype(BF16)
            left = (left.astype(F32) + term(1, i)).astype(BF16)
        left = lax.ppermute(
            left, ("y", "k"),
            [(2 * y + k, 2 * ((y - 1) % ny) + 1 - k) for y in range(ny) for k in range(2)],
        )

        hidden = pl.pallas_call(
            functools.partial(spread_kernel, main, tail),
            out_shape=jax.ShapeDtypeStruct((own_tokens, units), BF16),
            in_specs=[VMEM],
            out_specs=VMEM,
            compiler_params=params(8),
        )(hidden)
        hidden, left = lax.optimization_barrier((hidden, left))
        last = pl.pallas_call(
            functools.partial(gather_kernel, nx, rows, wide, thin),
            out_shape=jax.ShapeDtypeStruct((nx, 16 * nx + feats // nc, pair), BF16),
            in_specs=[VMEM, VMEM, VMEM],
            out_specs=VMEM,
            compiler_params=params(24),
        )(right, left, grad)
        last = exchange(last, "x")
        input_grad, gate_grad, up_grad = pl.pallas_call(
            functools.partial(finish_kernel, main, tail, wide, thin),
            out_shape=(
                jax.ShapeDtypeStruct((rows, width), BF16),
                jax.ShapeDtypeStruct((feats // nc, units), F32),
                jax.ShapeDtypeStruct((feats // nc, units), F32),
            ),
            in_specs=[VMEM, VMEM, VMEM],
            out_specs=(VMEM, VMEM, VMEM),
            compiler_params=params(16),
        )(last, tokens, norm_gain)
        return (hidden, input_grad, gate_grad, up_grad)

    return per_device


def solution(mesh):
    fine = split_fsdp(mesh)
    return jax.shard_map(
        make_step(*fine.devices.shape),
        mesh=fine,
        in_specs=(
            P(("c", "x", "l", "y", "k"), None),
            P(),
            P(("x", "l"), ("y", "k")),
            P(("x", "l"), ("y", "k")),
            P(("c", "x", "l"), ("y", "k")),
        ),
        out_specs=(
            P(("c", "x", "l"), ("y", "k")),
            P(("c", "x", "l", "y", "k"), None),
            P(("x", "l", "c"), ("y", "k")),
            P(("x", "l", "c"), ("y", "k")),
        ),
        check_vma=False,
    )
```

```python
import functools

import jax
import jax.numpy as jnp
from jax import lax
from jax.experimental import pallas as pl
from jax.experimental.pallas import tpu as pltpu
from jax.sharding import Mesh
from jax.sharding import PartitionSpec as P

ROOT_TWO_PI = 0.7978845608028654
CUBIC = 0.044715
BF16 = jnp.bfloat16
F32 = jnp.float32
VMEM = pl.BlockSpec(memory_space=pltpu.VMEM)
SMEM = pl.BlockSpec(memory_space=pltpu.SMEM)
ANY = pl.BlockSpec(memory_space=pl.ANY)


def split_fsdp(mesh):
    cuts, fsdp, tensor = mesh.devices.shape
    return Mesh(
        mesh.devices.reshape(cuts, fsdp // 2, 2, tensor // 2, 2), ("c", "x", "l", "y", "k")
    )


def ring(size, shift):
    return [(i, (i + shift) % size) for i in range(size)]


def both_ways(size):
    return [(2 * i, 2 * ((i + 1) % size)) for i in range(size)] + [
        (2 * i + 1, 2 * ((i - 1) % size) + 1) for i in range(size)
    ]


def exchange(value, axis):
    return lax.all_to_all(value, axis, split_axis=0, concat_axis=0, tiled=True)


def params(mib):
    return pltpu.CompilerParams(vmem_limit_bytes=mib * 1024 * 1024)


def share_sizes(units, parts):
    part = units // parts
    main = part // 128 * 128
    return main, part - main


def put_pair(out_ref, at, rows, a, b, main, tail, parts, q):
    out_ref[at, rows, 0:main] = a[:, q * main : (q + 1) * main]
    out_ref[at, rows, main : 2 * main] = b[:, q * main : (q + 1) * main]
    start = parts * main + q * tail
    out_ref[at, rows, 2 * main : 2 * main + tail] = a[:, start : start + tail]
    out_ref[at, rows, 2 * main + tail : 2 * (main + tail)] = b[:, start : start + tail]


def pack_weights_kernel(main, tail, parts, gate_ref, up_ref, *out_refs):
    held, count, _ = out_refs[0].shape
    rows = slice(0, count)
    for q in range(parts):
        put_pair(
            out_refs[q // held], q % held, rows, gate_ref.at[rows], up_ref.at[rows], main, tail, parts, q
        )


def pack_weights(parts, gate, up, rows, pieces):
    main, tail = share_sizes(gate.shape[1], parts)
    return pl.pallas_call(
        functools.partial(pack_weights_kernel, main, tail, parts),
        out_shape=(jax.ShapeDtypeStruct((parts // pieces, rows, 2 * (main + tail)), BF16),) * pieces,
        in_specs=[VMEM, VMEM],
        out_specs=(VMEM,) * pieces,
        compiler_params=params(16),
    )(gate, up)


def pack_grads_kernel(main, tail, parts, lower_ref, upper_ref, grad_ref, out_ref):
    held, cut, _ = lower_ref.shape
    half = grad_ref.shape[0] // 2
    out_ref[:held, 0:cut, :] = lower_ref[...]
    out_ref[held:, 0:cut, :] = upper_ref[...]
    for q in range(parts):
        put_pair(
            out_ref, q, slice(cut, cut + half),
            grad_ref.at[0:half], grad_ref.at[half : 2 * half], main, tail, parts, q,
        )


def pack_grads(parts, lower, upper, grads):
    main, tail = share_sizes(grads.shape[1], parts)
    rows = lower.shape[1] + grads.shape[0] // 2 + 32
    return pl.pallas_call(
        functools.partial(pack_grads_kernel, main, tail, parts),
        out_shape=jax.ShapeDtypeStruct((parts, rows, 2 * (main + tail)), BF16),
        in_specs=[VMEM, VMEM, VMEM],
        out_specs=VMEM,
        compiler_params=params(16),
    )(lower, upper, grads)


def activate(gate, upward, cotangent):
    square = gate * gate
    tangent = jnp.tanh(ROOT_TWO_PI * (gate + CUBIC * square * gate))
    active = 0.5 * gate * (1.0 + tangent)
    slope = 0.5 * (1.0 + tangent) + 0.5 * gate * (1.0 - tangent * tangent) * ROOT_TWO_PI * (
        1.0 + 3.0 * CUBIC * square
    )
    hidden = (active * upward).astype(BF16)
    return hidden, (cotangent * upward * slope).astype(BF16), (cotangent * active).astype(BF16)


def split_index(value, size, top):
    factor = (1 << 20) // size + 1
    assert all(i * factor >> 20 == i // size for i in range(top))
    high = (value * factor) >> 20
    return high, value - high * size


def shuffle(pool, outer, inner, rows):
    index = lax.broadcasted_iota(jnp.int32, (pool, 1), 0)
    high, rest = split_index(index, inner * rows, pool)
    mid, low = split_index(rest, rows, inner * rows)
    source = mid * (outer * rows) + high * rows + low
    columns = lax.broadcasted_iota(jnp.int32, (pool, pool), 1)
    return (columns == source).astype(F32).astype(BF16)


SORTED = 4


def sort_grads_kernel(main, tail, cut, rows_each, raw_ref, out_ref):
    blocks = raw_ref.shape[0]
    size = SORTED * rows_each
    half = out_ref.shape[0] // (2 * blocks)
    order = shuffle(blocks * size, SORTED, blocks, rows_each)
    for g in range(2 * half // size):
        h, at = g * size // half, cut + g * size % half
        found = [raw_ref[x, at : at + size, :] for x in range(blocks)]
        found = jnp.concatenate(found, axis=0)
        rows = slice(g * blocks * size, (g + 1) * blocks * size)
        for lanes, first, width in (
            (slice(0, main), h * main, main), (slice(main, main + tail), 2 * main + h * tail, tail)
        ):
            out_ref[rows, lanes] = jnp.dot(
                order, found[:, first : first + width], preferred_element_type=F32
            ).astype(BF16)


def sort_grads(raw, cut, own_tokens, rows_each):
    blocks, _, pair = raw.shape
    main = pair // 2 // 128 * 128
    return pl.pallas_call(
        functools.partial(sort_grads_kernel, main, pair // 2 - main, cut, rows_each),
        out_shape=jax.ShapeDtypeStruct((blocks * own_tokens, pair // 2), BF16),
        in_specs=[VMEM],
        out_specs=VMEM,
        compiler_params=params(16),
    )(raw)


def sort_hidden_kernel(main, tail, rows_each, found_ref, out_ref):
    blocks, half, _ = out_ref.shape
    size = SORTED * rows_each
    order = shuffle(blocks * size, blocks, SORTED, rows_each)
    for g in range(2 * half // size):
        h, at = g * size // half, g * size % half
        rows = slice(g * blocks * size, (g + 1) * blocks * size)
        for lanes, first, width in (
            (slice(0, main), h * main, main), (slice(main, main + tail), 2 * main + h * tail, tail)
        ):
            got = jnp.dot(order, found_ref[rows, lanes], preferred_element_type=F32).astype(BF16)
            for x in range(blocks):
                out_ref[x, at : at + size, first : first + width] = got[x * size : (x + 1) * size]


def sort_hidden(found, blocks, rows_each):
    pool, part = found.shape
    main = part // 128 * 128
    return pl.pallas_call(
        functools.partial(sort_hidden_kernel, main, part - main, rows_each),
        out_shape=jax.ShapeDtypeStruct((blocks, pool // blocks // 2, 2 * part), BF16),
        in_specs=[VMEM],
        out_specs=VMEM,
        compiler_params=params(16),
    )(found)


def forward_kernel(
    chunk, main, tail, place_ref, table_ref, own_ref, early_ref, late_ref, grads_ref,
    found_ref, cots_ref, keep_ref, give_ref, matrix,
):
    blocks, feats, pair = own_ref.shape
    late = late_ref.shape[1]
    cut = feats - late
    pool, width = table_ref.shape
    low, core, me = place_ref[0], place_ref[1], place_ref[3]
    _, chain, step, _ = keep_ref.shape
    near = low * (width // 2)
    far = (1 - low) * (width // 2)
    for x in range(blocks):
        for first, size, rows in (
            (near + x * feats, feats, own_ref[x]),
            (far + x * feats, cut, early_ref[x, :cut, :]),
            (far + x * feats + cut, late, late_ref[x]),
        ):
            matrix[pl.ds(pl.multiple_of(first, 16), size), :] = rows
    for first in range(0, pool, chunk):
        rows = slice(first, first + chunk)
        both = jnp.dot(table_ref[rows, :], matrix[...], preferred_element_type=F32)
        grads = grads_ref[rows, :].astype(F32)
        hidden, gate_cot, up_cot = activate(
            both[:, :main], both[:, main : 2 * main], grads[:, :main]
        )
        found_ref[rows, :main] = hidden
        cots_ref[rows, :main] = gate_cot
        cots_ref[rows, main : 2 * main] = up_cot
        rest = both[:, 2 * main :]
        hidden, gate_cot, up_cot = activate(rest[:, :tail], rest[:, tail:], grads[:, main:])
        found_ref[rows, main:] = hidden
        cots_ref[rows, 2 * main : 2 * main + tail] = gate_cot
        cots_ref[rows, 2 * main + tail :] = up_cot
        partial = lax.dot_general(
            cots_ref[rows, :], matrix[...], (((1,), (1,)), ((), ())), preferred_element_type=F32
        )
        for j in range(chunk // (2 * step)):
            even = partial[2 * j * step : (2 * j + 1) * step]
            odd = partial[(2 * j + 1) * step : (2 * j + 2) * step]
            ahead = lax.rem(first // (2 * step) + j - me + 2 * chain, 2 * chain)
            right = ahead < chain
            side = jnp.where(right, 0, 1)
            slot = jnp.where(right, chain - 1 - ahead, ahead - chain)
            straight = right == (core == 0)
            keep_ref[side, slot] = jnp.where(straight, even, odd).astype(BF16)
            give_ref[side, slot] = jnp.where(straight, odd, even).astype(BF16)


def forward(place, table, own, early, late, grads, ny, chunk):
    pool, width = table.shape
    _, _, pair = own.shape
    part = pair // 2
    main = part // 128 * 128
    step = pool // (2 * ny)
    return pl.pallas_call(
        functools.partial(forward_kernel, chunk, main, part - main),
        out_shape=(
            jax.ShapeDtypeStruct((pool, part), BF16),
            jax.ShapeDtypeStruct((pool, pair), BF16),
            jax.ShapeDtypeStruct((2, ny // 2, step, width), BF16),
            jax.ShapeDtypeStruct((2, ny // 2, step, width), BF16),
        ),
        in_specs=[SMEM] + [VMEM] * 5,
        out_specs=(VMEM, VMEM, VMEM, VMEM),
        scratch_shapes=[pltpu.VMEM((width, pair), BF16)],
        compiler_params=params(32),
        cost_estimate=pl.CostEstimate(
            flops=4 * pool * width * pair, bytes_accessed=2 * (2 * pool * width + width * pair), transcendentals=0
        ),
    )(place, table, own, early, late, grads)


def gradient_kernel(nx, nl, nc, table_ref, cots_ref, out_any, total, ready, sems):
    width = table_ref.shape[1]
    span = width // nl
    piece = span // (nx * nc)
    block = nx * piece
    copies = []
    for l in range(nl):
        total[...] = lax.dot_general(
            table_ref[:, l * span : (l + 1) * span], cots_ref[...], (((0,), (0,)), ((), ())),
            preferred_element_type=F32,
        )
        for c in range(nc):
            found = [total[(x * nc + c) * piece : (x * nc + c + 1) * piece, :] for x in range(nx)]
            z = c * nl + l
            ready[z] = jnp.concatenate(found, axis=0).astype(BF16)
            copies.append(
                pltpu.make_async_copy(
                    ready.at[z], out_any.at[pl.ds(z * block, block)], sems.at[z]
                )
            )
            copies[-1].start()
    for copy in copies:
        copy.wait()


def gradient(table, cots, nx, nl, nc):
    pool, width = table.shape
    pair = cots.shape[1]
    return pl.pallas_call(
        functools.partial(gradient_kernel, nx, nl, nc),
        out_shape=jax.ShapeDtypeStruct((width, pair), BF16),
        in_specs=[VMEM, VMEM],
        out_specs=ANY,
        scratch_shapes=[
            pltpu.VMEM((width // nl, pair), F32),
            pltpu.VMEM((nl * nc, width // (nl * nc), pair), BF16),
            pltpu.SemaphoreType.DMA((nl * nc,)),
        ],
        compiler_params=params(52),
        cost_estimate=pl.CostEstimate(
            flops=2 * pool * width * pair, bytes_accessed=2 * (pool * width + width * pair), transcendentals=0
        ),
    )(table, cots)


def row_scale_of(token_vals):
    mean = jnp.mean(token_vals * token_vals, axis=1, keepdims=True)
    return lax.rsqrt(mean + 1e-06).astype(BF16).astype(F32)


def turned(value, outer, inner):
    size = value.shape[1] // (outer * inner)
    blocks = [(o * inner + i) * size for i in range(inner) for o in range(outer)]
    return jnp.concatenate([value[:, at : at + size] for at in blocks], axis=1)


def normalise_kernel(tokens_ref, gain_ref, out_ref):
    token_vals = tokens_ref[...].astype(F32)
    gain = gain_ref[...].reshape(1, tokens_ref.shape[1])
    scaled = (token_vals * gain).astype(BF16).astype(F32)
    normed = turned(scaled * row_scale_of(token_vals), out_ref.shape[0], 2).astype(BF16)
    for i in range(out_ref.shape[0]):
        out_ref[i] = normed


def normalise(tokens, gain, copies):
    return pl.pallas_call(
        normalise_kernel,
        out_shape=jax.ShapeDtypeStruct((copies, *tokens.shape), BF16),
        in_specs=[VMEM, VMEM],
        out_specs=VMEM,
        compiler_params=params(8),
    )(tokens, gain)


def add_terms_kernel(i, keep_ref, taken_ref, *refs):
    sums, outs = refs[:-2], refs[-2:]
    for side, out_ref in enumerate(outs):
        total = keep_ref[side, i].astype(F32) + taken_ref[side, i].astype(F32)
        if sums:
            total = total + sums[side][...].astype(F32)
        out_ref[...] = total.astype(BF16)


def add_terms(keep, taken, i, *sums):
    block = jax.ShapeDtypeStruct(keep.shape[2:], BF16)
    return pl.pallas_call(
        functools.partial(add_terms_kernel, i),
        out_shape=(block, block),
        in_specs=[VMEM] * (2 + len(sums)),
        out_specs=(VMEM, VMEM),
        compiler_params=params(12),
    )(keep, taken, *sums)


def gather_kernel(nx, rows, wide, thin, right_ref, left_ref, grad_ref, out_ref):
    total = right_ref[...].astype(F32) + left_ref[...].astype(F32)
    grad = grad_ref[...].astype(F32)
    piece = grad.shape[0] // nx
    for x in range(nx):
        mine = total[x * rows : (x + 1) * rows]
        found = []
        for j in range(nx):
            start = nx * wide + j * thin
            found.append(
                jnp.concatenate(
                    [mine[:, j * wide : (j + 1) * wide], mine[:, start : start + thin]], axis=1
                )
            )
        out_ref[x, : nx * rows, : wide + thin] = jnp.concatenate(found, axis=0).astype(BF16)
        out_ref[x, nx * rows :, : grad.shape[1]] = grad[x * piece : (x + 1) * piece].astype(BF16)


def finish_kernel(main, tail, wide, thin, got_ref, tokens_ref, gain_ref, input_ref, gate_ref, up_ref):
    nx = got_ref.shape[0]
    rows, width = tokens_ref.shape
    pair = 2 * (main + tail)
    total = sum(got_ref[x, : nx * rows, : wide + thin].astype(F32) for x in range(nx))
    found = [total[j * rows : (j + 1) * rows] for j in range(nx)]
    token_vals = tokens_ref[...].astype(F32)
    scale = row_scale_of(token_vals)
    gain = gain_ref[...].reshape(1, width)
    scaled = (token_vals * gain).astype(BF16).astype(F32)
    inner_grad = jnp.concatenate([f[:, :wide] for f in found] + [f[:, wide:] for f in found], axis=1)
    inner_grad = turned(inner_grad, 2, nx) * scale
    inner = jnp.sum(scaled * inner_grad, axis=1, keepdims=True)
    factor = scale * scale / width
    input_ref[...] = (gain * inner_grad - factor * token_vals * inner).astype(BF16)
    for q in range(nx):
        grad = got_ref[q, nx * rows :, :pair].astype(F32)
        start = nx * main + q * tail
        gate_ref[:, q * main : (q + 1) * main] = grad[:, :main]
        gate_ref[:, start : start + tail] = grad[:, 2 * main : 2 * main + tail]
        up_ref[:, q * main : (q + 1) * main] = grad[:, main : 2 * main]
        up_ref[:, start : start + tail] = grad[:, 2 * main + tail :]


def spread_kernel(main, tail, got_ref, out_ref):
    nx, half, _ = got_ref.shape
    for q in range(nx):
        start = nx * main + q * tail
        for h in range(2):
            rows = slice(h * half, (h + 1) * half)
            out_ref[rows, q * main : (q + 1) * main] = got_ref[q, :, h * main : (h + 1) * main]
            out_ref[rows, start : start + tail] = got_ref[
                q, :, 2 * main + h * tail : 2 * main + (h + 1) * tail
            ]


def make_step(nc, nx, nl, ny, nk):
    def per_device(tokens, norm_gain, gate_weight, up_weight, hidden_grad):
        rows, width = tokens.shape
        feats, units = gate_weight.shape
        main, tail = share_sizes(units, nx)
        wide, thin = share_sizes(width, nx)
        pair = 2 * (main + tail)
        own_tokens = hidden_grad.shape[0]
        pool = nx * own_tokens
        nz = nc * nl
        place = jnp.stack([lax.axis_index(name) for name in ("l", "k", "x", "y")]).astype(jnp.int32)

        near = exchange(normalise(tokens, norm_gain, nx), "x").reshape(nx * rows, width)
        table = lax.all_gather(near, ("y", "k"), axis=0, tiled=True)

        def from_other(lower, upper):
            lower = lax.ppermute(lower, ("c", "l"), ring(nz, 1))
            return lower, lax.ppermute(upper, ("c", "l"), ring(nz, -1))

        cut, held = feats // 2, nx // 2
        lower, upper = from_other(*pack_weights(nx, gate_weight, up_weight, cut, 2))
        own = exchange(pack_weights(nx, gate_weight, up_weight, feats, 1)[0], "x")
        early = exchange(pack_grads(nx, lower, upper, hidden_grad), "x")
        late = lax.ppermute(own[:, cut:], ("c", "l", "k"), both_ways(nz))
        table, early = lax.optimization_barrier((table, early))
        grads = sort_grads(early, cut, own_tokens, rows)

        found, cots, keep, give = forward(
            place, table, own, early, late, grads, ny, pool
        )
        taken = lax.ppermute(give, "k", [(0, 1), (1, 0)])
        grad = gradient(table, cots, nx, nl, nc)
        taken, grad = lax.optimization_barrier((taken, grad))
        grad = lax.psum_scatter(grad, ("c", "l"), scatter_dimension=0, tiled=True)

        hidden = exchange(sort_hidden(found, nx, rows), "x")
        right, left = add_terms(keep, taken, 0)
        for i in range(1, ny // 2):
            right = lax.ppermute(right, "y", ring(ny, 1))
            left = lax.ppermute(left, "y", ring(ny, -1))
            if i == ny // 2 - 1:
                right, hidden = lax.optimization_barrier((right, hidden))
            right, left = add_terms(keep, taken, i, right, left)
        left = lax.ppermute(
            left, ("y", "k"),
            [(2 * y + k, 2 * ((y - 1) % ny) + 1 - k) for y in range(ny) for k in range(2)],
        )

        hidden = pl.pallas_call(
            functools.partial(spread_kernel, main, tail),
            out_shape=jax.ShapeDtypeStruct((own_tokens, units), BF16),
            in_specs=[VMEM],
            out_specs=VMEM,
            compiler_params=params(8),
        )(hidden)
        hidden, left = lax.optimization_barrier((hidden, left))
        last = pl.pallas_call(
            functools.partial(gather_kernel, nx, rows, wide, thin),
            out_shape=jax.ShapeDtypeStruct((nx, nx * rows + feats // nc, -(-pair // 128) * 128), BF16),
            in_specs=[VMEM, VMEM, VMEM],
            out_specs=VMEM,
            compiler_params=params(24),
        )(right, left, grad)
        last = exchange(last, "x")
        input_grad, gate_grad, up_grad = pl.pallas_call(
            functools.partial(finish_kernel, main, tail, wide, thin),
            out_shape=(
                jax.ShapeDtypeStruct((rows, width), BF16),
                jax.ShapeDtypeStruct((feats // nc, units), F32),
                jax.ShapeDtypeStruct((feats // nc, units), F32),
            ),
            in_specs=[VMEM, VMEM, VMEM],
            out_specs=(VMEM, VMEM, VMEM),
            compiler_params=params(16),
        )(last, tokens, norm_gain)
        return (hidden, input_grad, gate_grad, up_grad)

    return per_device


def solution(mesh):
    fine = split_fsdp(mesh)
    return jax.shard_map(
        make_step(*fine.devices.shape),
        mesh=fine,
        in_specs=(
            P(("c", "x", "l", "y", "k"), None),
            P(),
            P(("x", "l"), ("y", "k")),
            P(("x", "l"), ("y", "k")),
            P(("c", "x", "l"), ("y", "k")),
        ),
        out_specs=(
            P(("c", "x", "l"), ("y", "k")),
            P(("c", "x", "l", "y", "k"), None),
            P(("x", "l", "c"), ("y", "k")),
            P(("x", "l", "c"), ("y", "k")),
        ),
        check_vma=False,
    )
```

```python
import functools

import jax
import jax.numpy as jnp
from jax import lax
from jax.experimental import pallas as pl
from jax.experimental.pallas import tpu as pltpu
from jax.sharding import Mesh
from jax.sharding import PartitionSpec as P

ROOT_TWO_PI = 0.7978845608028654
CUBIC = 0.044715
BF16 = jnp.bfloat16
F32 = jnp.float32
VMEM = pl.BlockSpec(memory_space=pltpu.VMEM)
SMEM = pl.BlockSpec(memory_space=pltpu.SMEM)
ANY = pl.BlockSpec(memory_space=pl.ANY)


def split_fsdp(mesh):
    cuts, fsdp, tensor = mesh.devices.shape
    return Mesh(
        mesh.devices.reshape(cuts, fsdp // 2, 2, tensor // 2, 2), ("c", "x", "l", "y", "k")
    )


def ring(size, shift):
    return [(i, (i + shift) % size) for i in range(size)]


def both_ways(size):
    return [(2 * i, 2 * ((i + 1) % size)) for i in range(size)] + [
        (2 * i + 1, 2 * ((i - 1) % size) + 1) for i in range(size)
    ]


def exchange(value, axis):
    return lax.all_to_all(value, axis, split_axis=0, concat_axis=0, tiled=True)


def params(mib):
    return pltpu.CompilerParams(vmem_limit_bytes=mib * 1024 * 1024)


def share_sizes(units, parts):
    part = units // parts
    main = part // 128 * 128
    return main, part - main


def put_pair(out_ref, q, rows, a, b, main, tail, parts):
    out_ref[q, rows, 0:main] = a[:, q * main : (q + 1) * main]
    out_ref[q, rows, main : 2 * main] = b[:, q * main : (q + 1) * main]
    start = parts * main + q * tail
    out_ref[q, rows, 2 * main : 2 * main + tail] = a[:, start : start + tail]
    out_ref[q, rows, 2 * main + tail : 2 * (main + tail)] = b[:, start : start + tail]


def pack_weights_kernel(main, tail, parts, gate_ref, up_ref, out_ref):
    rows = slice(0, out_ref.shape[1])
    for q in range(parts):
        put_pair(out_ref, q, rows, gate_ref.at[rows], up_ref.at[rows], main, tail, parts)


def pack_weights(parts, gate, up, rows):
    main, tail = share_sizes(gate.shape[1], parts)
    return pl.pallas_call(
        functools.partial(pack_weights_kernel, main, tail, parts),
        out_shape=jax.ShapeDtypeStruct((parts, rows, 2 * (main + tail)), BF16),
        in_specs=[VMEM, VMEM],
        out_specs=VMEM,
        compiler_params=params(16),
    )(gate, up)


def pack_grads_kernel(main, tail, parts, weights_ref, grad_ref, out_ref):
    cut = weights_ref.shape[1]
    half = grad_ref.shape[0] // 2
    out_ref[:, 0:cut, :] = weights_ref[...]
    for q in range(parts):
        put_pair(
            out_ref, q, slice(cut, cut + half),
            grad_ref.at[0:half], grad_ref.at[half : 2 * half], main, tail, parts,
        )


def pack_grads(parts, weights, grads):
    main, tail = share_sizes(grads.shape[1], parts)
    rows = weights.shape[1] + grads.shape[0] // 2 + 32
    return pl.pallas_call(
        functools.partial(pack_grads_kernel, main, tail, parts),
        out_shape=jax.ShapeDtypeStruct((parts, rows, 2 * (main + tail)), BF16),
        in_specs=[VMEM, VMEM],
        out_specs=VMEM,
        compiler_params=params(16),
    )(weights, grads)


def activate(gate, upward, cotangent):
    square = gate * gate
    tangent = jnp.tanh(ROOT_TWO_PI * (gate + CUBIC * square * gate))
    active = 0.5 * gate * (1.0 + tangent)
    slope = 0.5 * (1.0 + tangent) + 0.5 * gate * (1.0 - tangent * tangent) * ROOT_TWO_PI * (
        1.0 + 3.0 * CUBIC * square
    )
    hidden = (active * upward).astype(BF16)
    return hidden, (cotangent * upward * slope).astype(BF16), (cotangent * active).astype(BF16)


def split_index(value, size, top):
    factor = (1 << 20) // size + 1
    assert all(i * factor >> 20 == i // size for i in range(top))
    high = (value * factor) >> 20
    return high, value - high * size


def shuffle(pool, outer, inner, rows):
    index = lax.broadcasted_iota(jnp.int32, (pool, 1), 0)
    high, rest = split_index(index, inner * rows, pool)
    mid, low = split_index(rest, rows, inner * rows)
    source = mid * (outer * rows) + high * rows + low
    columns = lax.broadcasted_iota(jnp.int32, (pool, pool), 1)
    return (columns == source).astype(F32).astype(BF16)


SORTED = 4


def sort_grads_kernel(main, tail, cut, rows_each, raw_ref, out_ref):
    blocks = raw_ref.shape[0]
    size = SORTED * rows_each
    half = out_ref.shape[0] // (2 * blocks)
    order = shuffle(blocks * size, SORTED, blocks, rows_each)
    for g in range(2 * half // size):
        h, at = g * size // half, cut + g * size % half
        found = [raw_ref[x, at : at + size, :] for x in range(blocks)]
        found = jnp.concatenate(found, axis=0)
        rows = slice(g * blocks * size, (g + 1) * blocks * size)
        for lanes, first, width in (
            (slice(0, main), h * main, main), (slice(main, main + tail), 2 * main + h * tail, tail)
        ):
            out_ref[rows, lanes] = jnp.dot(
                order, found[:, first : first + width], preferred_element_type=F32
            ).astype(BF16)


def sort_grads(raw, cut, own_tokens, rows_each):
    blocks, _, pair = raw.shape
    main = pair // 2 // 128 * 128
    return pl.pallas_call(
        functools.partial(sort_grads_kernel, main, pair // 2 - main, cut, rows_each),
        out_shape=jax.ShapeDtypeStruct((blocks * own_tokens, pair // 2), BF16),
        in_specs=[VMEM],
        out_specs=VMEM,
        compiler_params=params(16),
    )(raw)


def sort_hidden_kernel(main, tail, rows_each, found_ref, out_ref):
    blocks, half, _ = out_ref.shape
    size = SORTED * rows_each
    order = shuffle(blocks * size, blocks, SORTED, rows_each)
    for g in range(2 * half // size):
        h, at = g * size // half, g * size % half
        rows = slice(g * blocks * size, (g + 1) * blocks * size)
        for lanes, first, width in (
            (slice(0, main), h * main, main), (slice(main, main + tail), 2 * main + h * tail, tail)
        ):
            got = jnp.dot(order, found_ref[rows, lanes], preferred_element_type=F32).astype(BF16)
            for x in range(blocks):
                out_ref[x, at : at + size, first : first + width] = got[x * size : (x + 1) * size]


def sort_hidden(found, blocks, rows_each):
    pool, part = found.shape
    main = part // 128 * 128
    return pl.pallas_call(
        functools.partial(sort_hidden_kernel, main, part - main, rows_each),
        out_shape=jax.ShapeDtypeStruct((blocks, pool // blocks // 2, 2 * part), BF16),
        in_specs=[VMEM],
        out_specs=VMEM,
        compiler_params=params(16),
    )(found)


def forward_kernel(
    chunk, main, tail, place_ref, table_ref, own_ref, early_ref, late_ref, grads_ref,
    found_ref, cots_ref, keep_ref, give_ref, matrix,
):
    blocks, feats, pair = own_ref.shape
    cut = feats - late_ref.shape[1]
    pool, width = table_ref.shape
    low, core, me = place_ref[0], place_ref[1], place_ref[3]
    chain, step, _ = keep_ref.shape
    near = low * (width // 2)
    far = (1 - low) * (width // 2)
    for x in range(blocks):
        for first, size, rows in (
            (near + x * feats, feats, own_ref[x]),
            (far + x * feats, cut, early_ref[x, :cut, :]),
            (far + x * feats + cut, feats - cut, late_ref[x]),
        ):
            matrix[pl.ds(pl.multiple_of(first, 16), size), :] = rows
    for first in range(0, pool, chunk):
        rows = slice(first, first + chunk)
        both = jnp.dot(table_ref[rows, :], matrix[...], preferred_element_type=F32)
        grads = grads_ref[rows, :].astype(F32)
        hidden, gate_cot, up_cot = activate(
            both[:, :main], both[:, main : 2 * main], grads[:, :main]
        )
        found_ref[rows, :main] = hidden
        cots_ref[rows, :main] = gate_cot
        cots_ref[rows, main : 2 * main] = up_cot
        rest = both[:, 2 * main :]
        hidden, gate_cot, up_cot = activate(rest[:, :tail], rest[:, tail:], grads[:, main:])
        found_ref[rows, main:] = hidden
        cots_ref[rows, 2 * main : 2 * main + tail] = gate_cot
        cots_ref[rows, 2 * main + tail :] = up_cot
        partial = lax.dot_general(
            cots_ref[rows, :], matrix[...], (((1,), (1,)), ((), ())), preferred_element_type=F32
        )
        for j in range(chunk // step):
            block = partial[j * step : (j + 1) * step].astype(BF16)
            ahead = lax.rem(first // step + j - me + 2 * chain, 2 * chain)
            right = ahead < chain
            slot = jnp.where(right, chain - 1 - ahead, ahead - chain)
            kept = right == (core == 0)

            @pl.when(kept)
            def _():
                keep_ref[slot] = block

            @pl.when(jnp.logical_not(kept))
            def _():
                give_ref[slot] = block


def forward(place, table, own, early, late, grads, ny, chunk):
    pool, width = table.shape
    _, _, pair = own.shape
    part = pair // 2
    main = part // 128 * 128
    step = pool // ny
    return pl.pallas_call(
        functools.partial(forward_kernel, chunk, main, part - main),
        out_shape=(
            jax.ShapeDtypeStruct((pool, part), BF16),
            jax.ShapeDtypeStruct((pool, pair), BF16),
            jax.ShapeDtypeStruct((ny // 2, step, width), BF16),
            jax.ShapeDtypeStruct((ny // 2, step, width), BF16),
        ),
        in_specs=[SMEM, VMEM, VMEM, VMEM, VMEM, VMEM],
        out_specs=(VMEM, VMEM, VMEM, VMEM),
        scratch_shapes=[pltpu.VMEM((width, pair), BF16)],
        compiler_params=params(32),
        cost_estimate=pl.CostEstimate(
            flops=4 * pool * width * pair, bytes_accessed=2 * (2 * pool * width + width * pair), transcendentals=0
        ),
    )(place, table, own, early, late, grads)


def gradient_kernel(nx, nl, nc, table_ref, cots_ref, out_any, total, ready, sems):
    width = table_ref.shape[1]
    span = width // nl
    piece = span // (nx * nc)
    block = nx * piece
    copies = []
    for l in range(nl):
        total[...] = lax.dot_general(
            table_ref[:, l * span : (l + 1) * span], cots_ref[...], (((0,), (0,)), ((), ())),
            preferred_element_type=F32,
        )
        for c in range(nc):
            found = [total[(x * nc + c) * piece : (x * nc + c + 1) * piece, :] for x in range(nx)]
            z = c * nl + l
            ready[z] = jnp.concatenate(found, axis=0).astype(BF16)
            copies.append(
                pltpu.make_async_copy(
                    ready.at[z], out_any.at[pl.ds(z * block, block)], sems.at[z]
                )
            )
            copies[-1].start()
    for copy in copies:
        copy.wait()


def gradient(table, cots, nx, nl, nc):
    pool, width = table.shape
    pair = cots.shape[1]
    return pl.pallas_call(
        functools.partial(gradient_kernel, nx, nl, nc),
        out_shape=jax.ShapeDtypeStruct((width, pair), BF16),
        in_specs=[VMEM, VMEM],
        out_specs=ANY,
        scratch_shapes=[
            pltpu.VMEM((width // nl, pair), F32),
            pltpu.VMEM((nl * nc, width // (nl * nc), pair), BF16),
            pltpu.SemaphoreType.DMA((nl * nc,)),
        ],
        compiler_params=params(32),
        cost_estimate=pl.CostEstimate(
            flops=2 * pool * width * pair, bytes_accessed=2 * (pool * width + width * pair), transcendentals=0
        ),
    )(table, cots)


def row_scale_of(token_vals):
    mean = jnp.mean(token_vals * token_vals, axis=1, keepdims=True)
    return lax.rsqrt(mean + 1e-06).astype(BF16).astype(F32)


def turned(value, outer, inner):
    size = value.shape[1] // (outer * inner)
    blocks = [(o * inner + i) * size for i in range(inner) for o in range(outer)]
    return jnp.concatenate([value[:, at : at + size] for at in blocks], axis=1)


def normalise_kernel(tokens_ref, gain_ref, out_ref):
    token_vals = tokens_ref[...].astype(F32)
    gain = gain_ref[...].reshape(1, tokens_ref.shape[1])
    scaled = (token_vals * gain).astype(BF16).astype(F32)
    normed = turned(scaled * row_scale_of(token_vals), out_ref.shape[0], 2).astype(BF16)
    for i in range(out_ref.shape[0]):
        out_ref[i] = normed


def normalise(tokens, gain, copies):
    return pl.pallas_call(
        normalise_kernel,
        out_shape=jax.ShapeDtypeStruct((copies, *tokens.shape), BF16),
        in_specs=[VMEM, VMEM],
        out_specs=VMEM,
        compiler_params=params(8),
    )(tokens, gain)


def gather_kernel(nx, rows, wide, thin, place_ref, near_ref, far_ref, sums_ref, grad_ref, out_ref):
    mine = sums_ref[0 : near_ref.shape[0], :].astype(F32)
    total = near_ref[...].astype(F32) + jnp.where(place_ref[1] == 0, mine, far_ref[...].astype(F32))
    grad = grad_ref[...].astype(F32)
    piece = grad.shape[0] // nx
    for x in range(nx):
        mine = total[x * rows : (x + 1) * rows]
        found = []
        for j in range(nx):
            start = nx * wide + j * thin
            found.append(
                jnp.concatenate(
                    [mine[:, j * wide : (j + 1) * wide], mine[:, start : start + thin]], axis=1
                )
            )
        out_ref[x, : nx * rows, : wide + thin] = jnp.concatenate(found, axis=0).astype(BF16)
        out_ref[x, nx * rows :, : grad.shape[1]] = grad[x * piece : (x + 1) * piece].astype(BF16)


def finish_kernel(main, tail, wide, thin, got_ref, tokens_ref, gain_ref, input_ref, gate_ref, up_ref):
    nx = got_ref.shape[0]
    rows, width = tokens_ref.shape
    pair = 2 * (main + tail)
    total = sum(got_ref[x, : nx * rows, : wide + thin].astype(F32) for x in range(nx))
    found = [total[j * rows : (j + 1) * rows] for j in range(nx)]
    token_vals = tokens_ref[...].astype(F32)
    scale = row_scale_of(token_vals)
    gain = gain_ref[...].reshape(1, width)
    scaled = (token_vals * gain).astype(BF16).astype(F32)
    inner_grad = jnp.concatenate([f[:, :wide] for f in found] + [f[:, wide:] for f in found], axis=1)
    inner_grad = turned(inner_grad, 2, nx) * scale
    inner = jnp.sum(scaled * inner_grad, axis=1, keepdims=True)
    factor = scale * scale / width
    input_ref[...] = (gain * inner_grad - factor * token_vals * inner).astype(BF16)
    for q in range(nx):
        grad = got_ref[q, nx * rows :, :pair].astype(F32)
        start = nx * main + q * tail
        gate_ref[:, q * main : (q + 1) * main] = grad[:, :main]
        gate_ref[:, start : start + tail] = grad[:, 2 * main : 2 * main + tail]
        up_ref[:, q * main : (q + 1) * main] = grad[:, main : 2 * main]
        up_ref[:, start : start + tail] = grad[:, 2 * main + tail :]


def spread_kernel(main, tail, got_ref, out_ref):
    nx, half, _ = got_ref.shape
    for q in range(nx):
        start = nx * main + q * tail
        for h in range(2):
            rows = slice(h * half, (h + 1) * half)
            out_ref[rows, q * main : (q + 1) * main] = got_ref[q, :, h * main : (h + 1) * main]
            out_ref[rows, start : start + tail] = got_ref[
                q, :, 2 * main + h * tail : 2 * main + (h + 1) * tail
            ]


def make_step(nc, nx, nl, ny, nk):
    def per_device(tokens, norm_gain, gate_weight, up_weight, hidden_grad):
        rows, width = tokens.shape
        feats, units = gate_weight.shape
        main, tail = share_sizes(units, nx)
        wide, thin = share_sizes(width, nx)
        pair = 2 * (main + tail)
        own_tokens = hidden_grad.shape[0]
        pool = nx * own_tokens
        nz = nc * nl
        place = jnp.stack([lax.axis_index(name) for name in ("l", "k", "x", "y")]).astype(jnp.int32)

        near = exchange(normalise(tokens, norm_gain, nx), "x").reshape(nx * rows, width)
        table = lax.all_gather(near, ("y", "k"), axis=0, tiled=True)

        cut = feats // 2
        early = lax.ppermute(
            pack_weights(nx, gate_weight, up_weight, cut), ("c", "l", "k"), both_ways(nz)
        )
        own = exchange(pack_weights(nx, gate_weight, up_weight, feats), "x")
        early = exchange(pack_grads(nx, early, hidden_grad), "x")
        late = lax.ppermute(own[:, cut:], ("c", "l", "k"), both_ways(nz))
        table, early = lax.optimization_barrier((table, early))
        grads = sort_grads(early, cut, own_tokens, rows)

        found, cots, keep, give = forward(place, table, own, early, late, grads, ny, pool)
        taken = lax.ppermute(give, "k", [(0, 1), (1, 0)])
        grad = gradient(table, cots, nx, nl, nc)
        taken, grad = lax.optimization_barrier((taken, grad))
        grad = lax.psum_scatter(grad, ("c", "l"), scatter_dimension=0, tiled=True)

        def term(i):
            return keep[i].astype(F32) + taken[i].astype(F32)

        hidden = exchange(sort_hidden(found, nx, rows), "x")
        partial = term(0).astype(BF16)
        for i in range(1, ny // 2):
            partial = lax.ppermute(partial, ("y", "k"), both_ways(ny))
            partial = (partial.astype(F32) + term(i)).astype(BF16)
        partial, hidden = lax.optimization_barrier((partial, hidden))
        step = partial.shape[0] // 2
        lower, upper = partial[:step], partial[step:]
        core = lax.axis_index("k")
        near = lax.ppermute(
            jnp.where(core == 0, upper, lower), ("y", "k"),
            [(2 * y, 2 * y + 1) for y in range(ny)]
            + [(2 * y + 1, 2 * ((y - 1) % ny)) for y in range(ny)],
        )
        far = lax.ppermute(
            upper, ("y", "k"), [(2 * y + 1, 2 * ((y - 1) % ny) + 1) for y in range(ny)]
        )

        hidden = pl.pallas_call(
            functools.partial(spread_kernel, main, tail),
            out_shape=jax.ShapeDtypeStruct((own_tokens, units), BF16),
            in_specs=[VMEM],
            out_specs=VMEM,
            compiler_params=params(8),
        )(hidden)
        hidden, near, far = lax.optimization_barrier((hidden, near, far))
        last = pl.pallas_call(
            functools.partial(gather_kernel, nx, rows, wide, thin),
            out_shape=jax.ShapeDtypeStruct((nx, nx * rows + feats // nc, -(-pair // 128) * 128), BF16),
            in_specs=[SMEM, VMEM, VMEM, VMEM, VMEM],
            out_specs=VMEM,
            compiler_params=params(24),
        )(place, near, far, partial, grad)
        last = exchange(last, "x")
        input_grad, gate_grad, up_grad = pl.pallas_call(
            functools.partial(finish_kernel, main, tail, wide, thin),
            out_shape=(
                jax.ShapeDtypeStruct((rows, width), BF16),
                jax.ShapeDtypeStruct((feats // nc, units), F32),
                jax.ShapeDtypeStruct((feats // nc, units), F32),
            ),
            in_specs=[VMEM, VMEM, VMEM],
            out_specs=(VMEM, VMEM, VMEM),
            compiler_params=params(16),
        )(last, tokens, norm_gain)
        return (hidden, input_grad, gate_grad, up_grad)

    return per_device


def solution(mesh):
    fine = split_fsdp(mesh)
    return jax.shard_map(
        make_step(*fine.devices.shape),
        mesh=fine,
        in_specs=(
            P(("c", "x", "l", "y", "k"), None),
            P(),
            P(("x", "l"), ("y", "k")),
            P(("x", "l"), ("y", "k")),
            P(("c", "x", "l"), ("y", "k")),
        ),
        out_specs=(
            P(("c", "x", "l"), ("y", "k")),
            P(("c", "x", "l", "y", "k"), None),
            P(("x", "l", "c"), ("y", "k")),
            P(("x", "l", "c"), ("y", "k")),
        ),
        check_vma=False,
    )
```

```python
import functools

import jax
import jax.numpy as jnp
from jax import lax
from jax.experimental import pallas as pl
from jax.experimental.pallas import tpu as pltpu
from jax.sharding import Mesh
from jax.sharding import PartitionSpec as P

ROOT_TWO_PI = 0.7978845608028654
CUBIC = 0.044715
BF16 = jnp.bfloat16
F32 = jnp.float32
VMEM = pl.BlockSpec(memory_space=pltpu.VMEM)
SMEM = pl.BlockSpec(memory_space=pltpu.SMEM)
ANY = pl.BlockSpec(memory_space=pl.ANY)


def split_fsdp(mesh):
    cuts, fsdp, tensor = mesh.devices.shape
    return Mesh(
        mesh.devices.reshape(cuts, fsdp // 2, 2, tensor // 2, 2), ("c", "x", "l", "y", "k")
    )


def ring(size, shift):
    return [(i, (i + shift) % size) for i in range(size)]


def both_ways(size):
    return [(2 * i, 2 * ((i + 1) % size)) for i in range(size)] + [
        (2 * i + 1, 2 * ((i - 1) % size) + 1) for i in range(size)
    ]


def exchange(value, axis):
    return lax.all_to_all(value, axis, split_axis=0, concat_axis=0, tiled=True)


def params(mib):
    return pltpu.CompilerParams(vmem_limit_bytes=mib * 1024 * 1024)


def share_sizes(units, parts):
    part = units // parts
    main = part // 128 * 128
    return main, part - main


def put_pair(out_ref, q, rows, a, b, main, tail, parts):
    out_ref[q, rows, 0:main] = a[:, q * main : (q + 1) * main]
    out_ref[q, rows, main : 2 * main] = b[:, q * main : (q + 1) * main]
    start = parts * main + q * tail
    out_ref[q, rows, 2 * main : 2 * main + tail] = a[:, start : start + tail]
    out_ref[q, rows, 2 * main + tail : 2 * (main + tail)] = b[:, start : start + tail]


def pack_weights_kernel(main, tail, parts, gate_ref, up_ref, out_ref):
    rows = slice(0, out_ref.shape[1])
    for q in range(parts):
        put_pair(out_ref, q, rows, gate_ref.at[rows], up_ref.at[rows], main, tail, parts)


def pack_weights(parts, gate, up, rows):
    main, tail = share_sizes(gate.shape[1], parts)
    return pl.pallas_call(
        functools.partial(pack_weights_kernel, main, tail, parts),
        out_shape=jax.ShapeDtypeStruct((parts, rows, 2 * (main + tail)), BF16),
        in_specs=[VMEM, VMEM],
        out_specs=VMEM,
        compiler_params=params(16),
    )(gate, up)


def pack_grads_kernel(main, tail, parts, weights_ref, grad_ref, out_ref):
    cut = weights_ref.shape[1]
    half = grad_ref.shape[0] // 2
    out_ref[:, 0:cut, :] = weights_ref[...]
    for q in range(parts):
        put_pair(
            out_ref, q, slice(cut, cut + half),
            grad_ref.at[0:half], grad_ref.at[half : 2 * half], main, tail, parts,
        )


def pack_grads(parts, weights, grads):
    main, tail = share_sizes(grads.shape[1], parts)
    rows = weights.shape[1] + grads.shape[0] // 2 + 32
    return pl.pallas_call(
        functools.partial(pack_grads_kernel, main, tail, parts),
        out_shape=jax.ShapeDtypeStruct((parts, rows, 2 * (main + tail)), BF16),
        in_specs=[VMEM, VMEM],
        out_specs=VMEM,
        compiler_params=params(16),
    )(weights, grads)


def activate(gate, upward, cotangent):
    square = gate * gate
    tangent = jnp.tanh(ROOT_TWO_PI * (gate + CUBIC * square * gate))
    active = 0.5 * gate * (1.0 + tangent)
    slope = 0.5 * (1.0 + tangent) + 0.5 * gate * (1.0 - tangent * tangent) * ROOT_TWO_PI * (
        1.0 + 3.0 * CUBIC * square
    )
    hidden = (active * upward).astype(BF16)
    return hidden, (cotangent * upward * slope).astype(BF16), (cotangent * active).astype(BF16)


def split_index(value, size, top):
    factor = (1 << 20) // size + 1
    assert all(i * factor >> 20 == i // size for i in range(top))
    high = (value * factor) >> 20
    return high, value - high * size


def shuffle(pool, outer, inner, rows):
    index = lax.broadcasted_iota(jnp.int32, (pool, 1), 0)
    high, rest = split_index(index, inner * rows, pool)
    mid, low = split_index(rest, rows, inner * rows)
    source = mid * (outer * rows) + high * rows + low
    columns = lax.broadcasted_iota(jnp.int32, (pool, pool), 1)
    return (columns == source).astype(F32).astype(BF16)


SORTED = 4


def sort_grads_kernel(main, tail, cut, rows_each, raw_ref, out_ref):
    blocks = raw_ref.shape[0]
    size = SORTED * rows_each
    half = out_ref.shape[0] // (2 * blocks)
    order = shuffle(blocks * size, SORTED, blocks, rows_each)
    for g in range(2 * half // size):
        h, at = g * size // half, cut + g * size % half
        found = [raw_ref[x, at : at + size, :] for x in range(blocks)]
        found = jnp.concatenate(found, axis=0)
        rows = slice(g * blocks * size, (g + 1) * blocks * size)
        for lanes, first, width in (
            (slice(0, main), h * main, main), (slice(main, main + tail), 2 * main + h * tail, tail)
        ):
            out_ref[rows, lanes] = jnp.dot(
                order, found[:, first : first + width], preferred_element_type=F32
            ).astype(BF16)


def sort_grads(raw, cut, own_tokens, rows_each):
    blocks, _, pair = raw.shape
    main = pair // 2 // 128 * 128
    return pl.pallas_call(
        functools.partial(sort_grads_kernel, main, pair // 2 - main, cut, rows_each),
        out_shape=jax.ShapeDtypeStruct((blocks * own_tokens, pair // 2), BF16),
        in_specs=[VMEM],
        out_specs=VMEM,
        compiler_params=params(16),
    )(raw)


def sort_hidden_kernel(main, tail, rows_each, place_ref, found_ref, *refs):
    outs, got_ref = refs[:-1], refs[-1]
    blocks = len(outs)
    half = outs[0].shape[0]
    me = place_ref[2]
    size = SORTED * rows_each
    order = shuffle(blocks * size, blocks, SORTED, rows_each)
    for g in range(2 * half // size):
        h, at = g * size // half, g * size % half
        rows = slice(g * blocks * size, (g + 1) * blocks * size)
        got = jnp.dot(order, found_ref[rows, :], preferred_element_type=F32)
        got_ref[...] = got.astype(BF16)
        for s, out_ref in enumerate(outs):
            x = lax.rem(me + s, blocks)
            block = got_ref[pl.ds(pl.multiple_of(x * size, 16), size), :]
            out_ref[at : at + size, h * main : (h + 1) * main] = block[:, :main]
            first = 2 * main + h * tail
            out_ref[at : at + size, first : first + tail] = block[:, main:]


def sort_hidden(place, found, blocks, rows_each):
    pool, part = found.shape
    main = part // 128 * 128
    out = jax.ShapeDtypeStruct((pool // blocks // 2, 2 * part), BF16)
    return pl.pallas_call(
        functools.partial(sort_hidden_kernel, main, part - main, rows_each),
        out_shape=(out,) * blocks,
        in_specs=[SMEM, VMEM],
        out_specs=(VMEM,) * blocks,
        scratch_shapes=[pltpu.VMEM((blocks * SORTED * rows_each, part), BF16)],
        compiler_params=params(16),
    )(place, found)


def forward_kernel(
    chunk, main, tail, place_ref, table_ref, own_ref, early_ref, late_ref, grads_ref,
    found_ref, cots_ref, keep_ref, give_ref, matrix,
):
    blocks, feats, pair = own_ref.shape
    cut = feats - late_ref.shape[1]
    pool, width = table_ref.shape
    low, core, me = place_ref[0], place_ref[1], place_ref[3]
    chain, step, _ = keep_ref.shape
    near = low * (width // 2)
    far = (1 - low) * (width // 2)
    for x in range(blocks):
        for first, size, rows in (
            (near + x * feats, feats, own_ref[x]),
            (far + x * feats, cut, early_ref[x, :cut, :]),
            (far + x * feats + cut, feats - cut, late_ref[x]),
        ):
            matrix[pl.ds(pl.multiple_of(first, 16), size), :] = rows
    for first in range(0, pool, chunk):
        rows = slice(first, first + chunk)
        both = jnp.dot(table_ref[rows, :], matrix[...], preferred_element_type=F32)
        grads = grads_ref[rows, :].astype(F32)
        hidden, gate_cot, up_cot = activate(
            both[:, :main], both[:, main : 2 * main], grads[:, :main]
        )
        found_ref[rows, :main] = hidden
        cots_ref[rows, :main] = gate_cot
        cots_ref[rows, main : 2 * main] = up_cot
        rest = both[:, 2 * main :]
        hidden, gate_cot, up_cot = activate(rest[:, :tail], rest[:, tail:], grads[:, main:])
        found_ref[rows, main:] = hidden
        cots_ref[rows, 2 * main : 2 * main + tail] = gate_cot
        cots_ref[rows, 2 * main + tail :] = up_cot
        partial = lax.dot_general(
            cots_ref[rows, :], matrix[...], (((1,), (1,)), ((), ())), preferred_element_type=F32
        )
        for j in range(chunk // step):
            block = partial[j * step : (j + 1) * step].astype(BF16)
            ahead = lax.rem(first // step + j - me + 2 * chain, 2 * chain)
            right = ahead < chain
            slot = jnp.where(right, chain - 1 - ahead, ahead - chain)
            kept = right == (core == 0)

            @pl.when(kept)
            def _():
                keep_ref[slot] = block

            @pl.when(jnp.logical_not(kept))
            def _():
                give_ref[slot] = block


def forward(place, table, own, early, late, grads, ny, chunk):
    pool, width = table.shape
    _, _, pair = own.shape
    part = pair // 2
    main = part // 128 * 128
    step = pool // ny
    return pl.pallas_call(
        functools.partial(forward_kernel, chunk, main, part - main),
        out_shape=(
            jax.ShapeDtypeStruct((pool, part), BF16),
            jax.ShapeDtypeStruct((pool, pair), BF16),
            jax.ShapeDtypeStruct((ny // 2, step, width), BF16),
            jax.ShapeDtypeStruct((ny // 2, step, width), BF16),
        ),
        in_specs=[SMEM, VMEM, VMEM, VMEM, VMEM, VMEM],
        out_specs=(VMEM, VMEM, VMEM, VMEM),
        scratch_shapes=[pltpu.VMEM((width, pair), BF16)],
        compiler_params=params(32),
        cost_estimate=pl.CostEstimate(
            flops=4 * pool * width * pair, bytes_accessed=2 * (2 * pool * width + width * pair), transcendentals=0
        ),
    )(place, table, own, early, late, grads)


def gradient_kernel(nx, nl, nc, table_ref, cots_ref, out_any, total, ready, sems):
    width = table_ref.shape[1]
    span = width // nl
    piece = span // (nx * nc)
    block = nx * piece
    copies = []
    for l in range(nl):
        total[...] = lax.dot_general(
            table_ref[:, l * span : (l + 1) * span], cots_ref[...], (((0,), (0,)), ((), ())),
            preferred_element_type=F32,
        )
        for c in range(nc):
            found = [total[(x * nc + c) * piece : (x * nc + c + 1) * piece, :] for x in range(nx)]
            z = c * nl + l
            ready[z] = jnp.concatenate(found, axis=0).astype(BF16)
            copies.append(
                pltpu.make_async_copy(
                    ready.at[z], out_any.at[pl.ds(z * block, block)], sems.at[z]
                )
            )
            copies[-1].start()
    for copy in copies:
        copy.wait()


def gradient(table, cots, nx, nl, nc):
    pool, width = table.shape
    pair = cots.shape[1]
    return pl.pallas_call(
        functools.partial(gradient_kernel, nx, nl, nc),
        out_shape=jax.ShapeDtypeStruct((width, pair), BF16),
        in_specs=[VMEM, VMEM],
        out_specs=ANY,
        scratch_shapes=[
            pltpu.VMEM((width // nl, pair), F32),
            pltpu.VMEM((nl * nc, width // (nl * nc), pair), BF16),
            pltpu.SemaphoreType.DMA((nl * nc,)),
        ],
        compiler_params=params(32),
        cost_estimate=pl.CostEstimate(
            flops=2 * pool * width * pair, bytes_accessed=2 * (pool * width + width * pair), transcendentals=0
        ),
    )(table, cots)


def row_scale_of(token_vals):
    mean = jnp.mean(token_vals * token_vals, axis=1, keepdims=True)
    return lax.rsqrt(mean + 1e-06).astype(BF16).astype(F32)


def turned(value, outer, inner):
    size = value.shape[1] // (outer * inner)
    blocks = [(o * inner + i) * size for i in range(inner) for o in range(outer)]
    return jnp.concatenate([value[:, at : at + size] for at in blocks], axis=1)


def normalise_kernel(tokens_ref, gain_ref, out_ref):
    token_vals = tokens_ref[...].astype(F32)
    gain = gain_ref[...].reshape(1, tokens_ref.shape[1])
    scaled = (token_vals * gain).astype(BF16).astype(F32)
    normed = turned(scaled * row_scale_of(token_vals), out_ref.shape[0], 2).astype(BF16)
    for i in range(out_ref.shape[0]):
        out_ref[i] = normed


def normalise(tokens, gain, copies):
    return pl.pallas_call(
        normalise_kernel,
        out_shape=jax.ShapeDtypeStruct((copies, *tokens.shape), BF16),
        in_specs=[VMEM, VMEM],
        out_specs=VMEM,
        compiler_params=params(8),
    )(tokens, gain)


def gather_kernel(nx, rows, wide, thin, place_ref, near_ref, far_ref, sums_ref, grad_ref, out_ref):
    mine = sums_ref[0 : near_ref.shape[0], :].astype(F32)
    total = near_ref[...].astype(F32) + jnp.where(place_ref[1] == 0, mine, far_ref[...].astype(F32))
    grad = grad_ref[...].astype(F32)
    piece = grad.shape[0] // nx
    for x in range(nx):
        mine = total[x * rows : (x + 1) * rows]
        found = []
        for j in range(nx):
            start = nx * wide + j * thin
            found.append(
                jnp.concatenate(
                    [mine[:, j * wide : (j + 1) * wide], mine[:, start : start + thin]], axis=1
                )
            )
        out_ref[x, : nx * rows, : wide + thin] = jnp.concatenate(found, axis=0).astype(BF16)
        out_ref[x, nx * rows :, : grad.shape[1]] = grad[x * piece : (x + 1) * piece].astype(BF16)


def finish_kernel(main, tail, wide, thin, got_ref, tokens_ref, gain_ref, input_ref, gate_ref, up_ref):
    nx = got_ref.shape[0]
    rows, width = tokens_ref.shape
    pair = 2 * (main + tail)
    total = sum(got_ref[x, : nx * rows, : wide + thin].astype(F32) for x in range(nx))
    found = [total[j * rows : (j + 1) * rows] for j in range(nx)]
    token_vals = tokens_ref[...].astype(F32)
    scale = row_scale_of(token_vals)
    gain = gain_ref[...].reshape(1, width)
    scaled = (token_vals * gain).astype(BF16).astype(F32)
    inner_grad = jnp.concatenate([f[:, :wide] for f in found] + [f[:, wide:] for f in found], axis=1)
    inner_grad = turned(inner_grad, 2, nx) * scale
    inner = jnp.sum(scaled * inner_grad, axis=1, keepdims=True)
    factor = scale * scale / width
    input_ref[...] = (gain * inner_grad - factor * token_vals * inner).astype(BF16)
    for q in range(nx):
        grad = got_ref[q, nx * rows :, :pair].astype(F32)
        start = nx * main + q * tail
        gate_ref[:, q * main : (q + 1) * main] = grad[:, :main]
        gate_ref[:, start : start + tail] = grad[:, 2 * main : 2 * main + tail]
        up_ref[:, q * main : (q + 1) * main] = grad[:, main : 2 * main]
        up_ref[:, start : start + tail] = grad[:, 2 * main + tail :]


def spread_kernel(main, tail, place_ref, *refs):
    sources, out_ref, got_ref = refs[:-2], refs[-2], refs[-1]
    nx, half, _ = got_ref.shape
    for s, source in enumerate(sources):
        got_ref[lax.rem(place_ref[2] - s + nx, nx)] = source[...]
    for q in range(nx):
        start = nx * main + q * tail
        for h in range(2):
            rows = slice(h * half, (h + 1) * half)
            out_ref[rows, q * main : (q + 1) * main] = got_ref[q, :, h * main : (h + 1) * main]
            out_ref[rows, start : start + tail] = got_ref[
                q, :, 2 * main + h * tail : 2 * main + (h + 1) * tail
            ]


def make_step(nc, nx, nl, ny, nk):
    def per_device(tokens, norm_gain, gate_weight, up_weight, hidden_grad):
        rows, width = tokens.shape
        feats, units = gate_weight.shape
        main, tail = share_sizes(units, nx)
        wide, thin = share_sizes(width, nx)
        pair = 2 * (main + tail)
        own_tokens = hidden_grad.shape[0]
        pool = nx * own_tokens
        nz = nc * nl
        place = jnp.stack([lax.axis_index(name) for name in ("l", "k", "x", "y")]).astype(jnp.int32)

        near = exchange(normalise(tokens, norm_gain, nx), "x").reshape(nx * rows, width)
        table = lax.all_gather(near, ("y", "k"), axis=0, tiled=True)

        cut = feats // 2
        early = lax.ppermute(
            pack_weights(nx, gate_weight, up_weight, cut), ("c", "l", "k"), both_ways(nz)
        )
        own = exchange(pack_weights(nx, gate_weight, up_weight, feats), "x")
        early = exchange(pack_grads(nx, early, hidden_grad), "x")
        late = lax.ppermute(own[:, cut:], ("c", "l", "k"), both_ways(nz))
        table, early = lax.optimization_barrier((table, early))
        grads = sort_grads(early, cut, own_tokens, rows)

        found, cots, keep, give = forward(place, table, own, early, late, grads, ny, pool)
        taken = lax.ppermute(give, "k", [(0, 1), (1, 0)])
        grad = gradient(table, cots, nx, nl, nc)
        taken, grad = lax.optimization_barrier((taken, grad))
        grad = lax.psum_scatter(grad, ("c", "l"), scatter_dimension=0, tiled=True)

        def term(i):
            return keep[i].astype(F32) + taken[i].astype(F32)

        hidden = list(sort_hidden(place, found, nx, rows))
        partial = term(0).astype(BF16)
        for i in range(1, ny // 2):
            partial = lax.ppermute(partial, ("y", "k"), both_ways(ny))
            if i < nx:
                hidden[i] = lax.ppermute(hidden[i], "x", ring(nx, i))
                partial, hidden[i] = lax.optimization_barrier((partial, hidden[i]))
            partial = (partial.astype(F32) + term(i)).astype(BF16)
        for i in range(ny // 2, nx):
            hidden[i] = lax.ppermute(hidden[i], "x", ring(nx, i))
        step = partial.shape[0] // 2
        lower, upper = partial[:step], partial[step:]
        core = lax.axis_index("k")
        near = lax.ppermute(
            jnp.where(core == 0, upper, lower), ("y", "k"),
            [(2 * y, 2 * y + 1) for y in range(ny)]
            + [(2 * y + 1, 2 * ((y - 1) % ny)) for y in range(ny)],
        )
        far = lax.ppermute(
            upper, ("y", "k"), [(2 * y + 1, 2 * ((y - 1) % ny) + 1) for y in range(ny)]
        )

        hidden = pl.pallas_call(
            functools.partial(spread_kernel, main, tail),
            out_shape=jax.ShapeDtypeStruct((own_tokens, units), BF16),
            in_specs=[SMEM] + [VMEM] * nx,
            out_specs=VMEM,
            scratch_shapes=[pltpu.VMEM((nx, own_tokens // 2, pair), BF16)],
            compiler_params=params(8),
        )(place, *hidden)
        hidden, near, far = lax.optimization_barrier((hidden, near, far))
        last = pl.pallas_call(
            functools.partial(gather_kernel, nx, rows, wide, thin),
            out_shape=jax.ShapeDtypeStruct((nx, nx * rows + feats // nc, -(-pair // 128) * 128), BF16),
            in_specs=[SMEM, VMEM, VMEM, VMEM, VMEM],
            out_specs=VMEM,
            compiler_params=params(24),
        )(place, near, far, partial, grad)
        last = exchange(last, "x")
        input_grad, gate_grad, up_grad = pl.pallas_call(
            functools.partial(finish_kernel, main, tail, wide, thin),
            out_shape=(
                jax.ShapeDtypeStruct((rows, width), BF16),
                jax.ShapeDtypeStruct((feats // nc, units), F32),
                jax.ShapeDtypeStruct((feats // nc, units), F32),
            ),
            in_specs=[VMEM, VMEM, VMEM],
            out_specs=(VMEM, VMEM, VMEM),
            compiler_params=params(16),
        )(last, tokens, norm_gain)
        return (hidden, input_grad, gate_grad, up_grad)

    return per_device


def solution(mesh):
    fine = split_fsdp(mesh)
    return jax.shard_map(
        make_step(*fine.devices.shape),
        mesh=fine,
        in_specs=(
            P(("c", "x", "l", "y", "k"), None),
            P(),
            P(("x", "l"), ("y", "k")),
            P(("x", "l"), ("y", "k")),
            P(("c", "x", "l"), ("y", "k")),
        ),
        out_specs=(
            P(("c", "x", "l"), ("y", "k")),
            P(("c", "x", "l", "y", "k"), None),
            P(("x", "l", "c"), ("y", "k")),
            P(("x", "l", "c"), ("y", "k")),
        ),
        check_vma=False,
    )
```

```python
import functools

import jax
import jax.numpy as jnp
from jax import lax
from jax.experimental import pallas as pl
from jax.experimental.pallas import tpu as pltpu
from jax.sharding import Mesh
from jax.sharding import PartitionSpec as P

ROOT_TWO_PI = 0.7978845608028654
CUBIC = 0.044715
BF16 = jnp.bfloat16
F32 = jnp.float32
VMEM = pl.BlockSpec(memory_space=pltpu.VMEM)
SMEM = pl.BlockSpec(memory_space=pltpu.SMEM)
ANY = pl.BlockSpec(memory_space=pl.ANY)


def split_fsdp(mesh):
    cuts, fsdp, tensor = mesh.devices.shape
    return Mesh(
        mesh.devices.reshape(cuts, fsdp // 2, 2, tensor // 2, 2), ("c", "x", "l", "y", "k")
    )


def ring(size, shift):
    return [(i, (i + shift) % size) for i in range(size)]


def both_ways(size):
    return [(2 * i, 2 * ((i + 1) % size)) for i in range(size)] + [
        (2 * i + 1, 2 * ((i - 1) % size) + 1) for i in range(size)
    ]


def exchange(value, axis):
    return lax.all_to_all(value, axis, split_axis=0, concat_axis=0, tiled=True)


def params(mib):
    return pltpu.CompilerParams(vmem_limit_bytes=mib * 1024 * 1024)


def share_sizes(units, parts):
    part = units // parts
    main = part // 128 * 128
    return main, part - main


def put_pair(out_ref, q, rows, a, b, main, tail, parts):
    out_ref[q, rows, 0:main] = a[:, q * main : (q + 1) * main]
    out_ref[q, rows, main : 2 * main] = b[:, q * main : (q + 1) * main]
    start = parts * main + q * tail
    out_ref[q, rows, 2 * main : 2 * main + tail] = a[:, start : start + tail]
    out_ref[q, rows, 2 * main + tail : 2 * (main + tail)] = b[:, start : start + tail]


def pack_weights_kernel(main, tail, parts, gate_ref, up_ref, out_ref):
    rows = slice(0, out_ref.shape[1])
    for q in range(parts):
        put_pair(out_ref, q, rows, gate_ref.at[rows], up_ref.at[rows], main, tail, parts)


def pack_weights(parts, gate, up, rows):
    main, tail = share_sizes(gate.shape[1], parts)
    return pl.pallas_call(
        functools.partial(pack_weights_kernel, main, tail, parts),
        out_shape=jax.ShapeDtypeStruct((parts, rows, 2 * (main + tail)), BF16),
        in_specs=[VMEM, VMEM],
        out_specs=VMEM,
        compiler_params=params(16),
    )(gate, up)


def pack_grads_kernel(main, tail, parts, weights_ref, grad_ref, out_ref):
    cut = weights_ref.shape[1]
    half = grad_ref.shape[0] // 2
    out_ref[:, 0:cut, :] = weights_ref[...]
    for q in range(parts):
        put_pair(
            out_ref, q, slice(cut, cut + half),
            grad_ref.at[0:half], grad_ref.at[half : 2 * half], main, tail, parts,
        )


def pack_grads(parts, weights, grads):
    main, tail = share_sizes(grads.shape[1], parts)
    rows = weights.shape[1] + grads.shape[0] // 2 + 32
    return pl.pallas_call(
        functools.partial(pack_grads_kernel, main, tail, parts),
        out_shape=jax.ShapeDtypeStruct((parts, rows, 2 * (main + tail)), BF16),
        in_specs=[VMEM, VMEM],
        out_specs=VMEM,
        compiler_params=params(16),
    )(weights, grads)


def activate(gate, upward, cotangent):
    square = gate * gate
    tangent = jnp.tanh(ROOT_TWO_PI * (gate + CUBIC * square * gate))
    active = 0.5 * gate * (1.0 + tangent)
    slope = 0.5 * (1.0 + tangent) + 0.5 * gate * (1.0 - tangent * tangent) * ROOT_TWO_PI * (
        1.0 + 3.0 * CUBIC * square
    )
    hidden = (active * upward).astype(BF16)
    return hidden, (cotangent * upward * slope).astype(BF16), (cotangent * active).astype(BF16)


def split_index(value, size, top):
    factor = (1 << 20) // size + 1
    assert all(i * factor >> 20 == i // size for i in range(top))
    high = (value * factor) >> 20
    return high, value - high * size


def shuffle(pool, outer, inner, rows):
    index = lax.broadcasted_iota(jnp.int32, (pool, 1), 0)
    high, rest = split_index(index, inner * rows, pool)
    mid, low = split_index(rest, rows, inner * rows)
    source = mid * (outer * rows) + high * rows + low
    columns = lax.broadcasted_iota(jnp.int32, (pool, pool), 1)
    return (columns == source).astype(F32).astype(BF16)


SORTED = 4


def sort_grads_kernel(main, tail, cut, rows_each, raw_ref, out_ref):
    blocks = raw_ref.shape[0]
    size = SORTED * rows_each
    half = out_ref.shape[0] // (2 * blocks)
    order = shuffle(blocks * size, SORTED, blocks, rows_each)
    for g in range(2 * half // size):
        h, at = g * size // half, cut + g * size % half
        found = [raw_ref[x, at : at + size, :] for x in range(blocks)]
        found = jnp.concatenate(found, axis=0)
        rows = slice(g * blocks * size, (g + 1) * blocks * size)
        for lanes, first, width in (
            (slice(0, main), h * main, main), (slice(main, main + tail), 2 * main + h * tail, tail)
        ):
            out_ref[rows, lanes] = jnp.dot(
                order, found[:, first : first + width], preferred_element_type=F32
            ).astype(BF16)


def sort_grads(raw, cut, own_tokens, rows_each):
    blocks, _, pair = raw.shape
    main = pair // 2 // 128 * 128
    return pl.pallas_call(
        functools.partial(sort_grads_kernel, main, pair // 2 - main, cut, rows_each),
        out_shape=jax.ShapeDtypeStruct((blocks * own_tokens, pair // 2), BF16),
        in_specs=[VMEM],
        out_specs=VMEM,
        compiler_params=params(16),
    )(raw)


def sort_hidden_kernel(main, tail, rows_each, place_ref, found_ref, *refs):
    outs, got_ref = refs[:-1], refs[-1]
    blocks = len(outs)
    half = outs[0].shape[0]
    me = place_ref[2]
    size = SORTED * rows_each
    order = shuffle(blocks * size, blocks, SORTED, rows_each)
    for g in range(2 * half // size):
        h, at = g * size // half, g * size % half
        rows = slice(g * blocks * size, (g + 1) * blocks * size)
        got = jnp.dot(order, found_ref[rows, :], preferred_element_type=F32)
        got_ref[...] = got.astype(BF16)
        for s, out_ref in enumerate(outs):
            x = lax.rem(me + s, blocks)
            block = got_ref[pl.ds(pl.multiple_of(x * size, 16), size), :]
            out_ref[at : at + size, h * main : (h + 1) * main] = block[:, :main]
            first = 2 * main + h * tail
            out_ref[at : at + size, first : first + tail] = block[:, main:]


def sort_hidden(place, found, blocks, rows_each):
    pool, part = found.shape
    main = part // 128 * 128
    out = jax.ShapeDtypeStruct((pool // blocks // 2, 2 * part), BF16)
    return pl.pallas_call(
        functools.partial(sort_hidden_kernel, main, part - main, rows_each),
        out_shape=(out,) * blocks,
        in_specs=[SMEM, VMEM],
        out_specs=(VMEM,) * blocks,
        scratch_shapes=[pltpu.VMEM((blocks * SORTED * rows_each, part), BF16)],
        compiler_params=params(16),
    )(place, found)


def forward_kernel(
    chunk, main, tail, place_ref, table_any, own_ref, early_ref, late_ref, grads_ref,
    found_ref, cots_ref, keep_ref, give_ref, table_ref, matrix, sem,
):
    blocks, feats, pair = own_ref.shape
    cut = feats - late_ref.shape[1]
    pool, width = table_ref.shape
    low, core, me = place_ref[0], place_ref[1], place_ref[3]
    chain, step, _ = keep_ref.shape
    fetch = pltpu.make_async_copy(table_any, table_ref, sem)
    fetch.start()
    near = low * (width // 2)
    far = (1 - low) * (width // 2)
    for x in range(blocks):
        for first, size, rows in (
            (near + x * feats, feats, own_ref[x]),
            (far + x * feats, cut, early_ref[x, :cut, :]),
            (far + x * feats + cut, feats - cut, late_ref[x]),
        ):
            matrix[pl.ds(pl.multiple_of(first, 16), size), :] = rows
    fetch.wait()
    for first in range(0, pool, chunk):
        rows = slice(first, first + chunk)
        both = jnp.dot(table_ref[rows, :], matrix[...], preferred_element_type=F32)
        grads = grads_ref[rows, :].astype(F32)
        hidden, gate_cot, up_cot = activate(
            both[:, :main], both[:, main : 2 * main], grads[:, :main]
        )
        found_ref[rows, :main] = hidden
        cots_ref[rows, :main] = gate_cot
        cots_ref[rows, main : 2 * main] = up_cot
        rest = both[:, 2 * main :]
        hidden, gate_cot, up_cot = activate(rest[:, :tail], rest[:, tail:], grads[:, main:])
        found_ref[rows, main:] = hidden
        cots_ref[rows, 2 * main : 2 * main + tail] = gate_cot
        cots_ref[rows, 2 * main + tail :] = up_cot
        partial = lax.dot_general(
            cots_ref[rows, :], matrix[...], (((1,), (1,)), ((), ())), preferred_element_type=F32
        )
        for j in range(chunk // step):
            block = partial[j * step : (j + 1) * step].astype(BF16)
            ahead = lax.rem(first // step + j - me + 2 * chain, 2 * chain)
            right = ahead < chain
            slot = jnp.where(right, chain - 1 - ahead, ahead - chain)
            kept = right == (core == 0)

            @pl.when(kept)
            def _():
                keep_ref[slot] = block

            @pl.when(jnp.logical_not(kept))
            def _():
                give_ref[slot] = block


def forward(place, table, own, early, late, grads, ny, chunk):
    pool, width = table.shape
    _, _, pair = own.shape
    part = pair // 2
    main = part // 128 * 128
    step = pool // ny
    return pl.pallas_call(
        functools.partial(forward_kernel, chunk, main, part - main),
        out_shape=(
            jax.ShapeDtypeStruct((pool, part), BF16),
            jax.ShapeDtypeStruct((pool, pair), BF16),
            jax.ShapeDtypeStruct((ny // 2, step, width), BF16),
            jax.ShapeDtypeStruct((ny // 2, step, width), BF16),
        ),
        in_specs=[SMEM, ANY, VMEM, VMEM, VMEM, VMEM],
        out_specs=(VMEM, VMEM, VMEM, VMEM),
        scratch_shapes=[
            pltpu.VMEM((pool, width), BF16),
            pltpu.VMEM((width, pair), BF16),
            pltpu.SemaphoreType.DMA,
        ],
        compiler_params=params(44),
        cost_estimate=pl.CostEstimate(
            flops=4 * pool * width * pair, bytes_accessed=2 * (2 * pool * width + width * pair), transcendentals=0
        ),
    )(place, table, own, early, late, grads)


def gradient_kernel(nx, nl, nc, table_ref, cots_ref, out_any, total, ready, sems):
    width = table_ref.shape[1]
    span = width // nl
    piece = span // (nx * nc)
    block = nx * piece
    copies = []
    for l in range(nl):
        total[...] = lax.dot_general(
            table_ref[:, l * span : (l + 1) * span], cots_ref[...], (((0,), (0,)), ((), ())),
            preferred_element_type=F32,
        )
        for c in range(nc):
            found = [total[(x * nc + c) * piece : (x * nc + c + 1) * piece, :] for x in range(nx)]
            z = c * nl + l
            ready[z] = jnp.concatenate(found, axis=0).astype(BF16)
            copies.append(
                pltpu.make_async_copy(
                    ready.at[z], out_any.at[pl.ds(z * block, block)], sems.at[z]
                )
            )
            copies[-1].start()
    for copy in copies:
        copy.wait()


def gradient(table, cots, nx, nl, nc):
    pool, width = table.shape
    pair = cots.shape[1]
    return pl.pallas_call(
        functools.partial(gradient_kernel, nx, nl, nc),
        out_shape=jax.ShapeDtypeStruct((width, pair), BF16),
        in_specs=[VMEM, VMEM],
        out_specs=ANY,
        scratch_shapes=[
            pltpu.VMEM((width // nl, pair), F32),
            pltpu.VMEM((nl * nc, width // (nl * nc), pair), BF16),
            pltpu.SemaphoreType.DMA((nl * nc,)),
        ],
        compiler_params=params(32),
        cost_estimate=pl.CostEstimate(
            flops=2 * pool * width * pair, bytes_accessed=2 * (pool * width + width * pair), transcendentals=0
        ),
    )(table, cots)


def row_scale_of(token_vals):
    mean = jnp.mean(token_vals * token_vals, axis=1, keepdims=True)
    return lax.rsqrt(mean + 1e-06).astype(BF16).astype(F32)


def turned(value, outer, inner):
    size = value.shape[1] // (outer * inner)
    blocks = [(o * inner + i) * size for i in range(inner) for o in range(outer)]
    return jnp.concatenate([value[:, at : at + size] for at in blocks], axis=1)


def normalise_kernel(tokens_ref, gain_ref, out_ref):
    token_vals = tokens_ref[...].astype(F32)
    gain = gain_ref[...].reshape(1, tokens_ref.shape[1])
    scaled = (token_vals * gain).astype(BF16).astype(F32)
    normed = turned(scaled * row_scale_of(token_vals), out_ref.shape[0], 2).astype(BF16)
    for i in range(out_ref.shape[0]):
        out_ref[i] = normed


def normalise(tokens, gain, copies):
    return pl.pallas_call(
        normalise_kernel,
        out_shape=jax.ShapeDtypeStruct((copies, *tokens.shape), BF16),
        in_specs=[VMEM, VMEM],
        out_specs=VMEM,
        compiler_params=params(8),
    )(tokens, gain)


def gather_kernel(nx, rows, wide, thin, place_ref, near_ref, far_ref, sums_ref, grad_ref, out_ref):
    mine = sums_ref[0 : near_ref.shape[0], :].astype(F32)
    total = near_ref[...].astype(F32) + jnp.where(place_ref[1] == 0, mine, far_ref[...].astype(F32))
    grad = grad_ref[...].astype(F32)
    piece = grad.shape[0] // nx
    for x in range(nx):
        mine = total[x * rows : (x + 1) * rows]
        found = []
        for j in range(nx):
            start = nx * wide + j * thin
            found.append(
                jnp.concatenate(
                    [mine[:, j * wide : (j + 1) * wide], mine[:, start : start + thin]], axis=1
                )
            )
        out_ref[x, : nx * rows, : wide + thin] = jnp.concatenate(found, axis=0).astype(BF16)
        out_ref[x, nx * rows :, : grad.shape[1]] = grad[x * piece : (x + 1) * piece].astype(BF16)


def finish_kernel(main, tail, wide, thin, got_ref, tokens_ref, gain_ref, input_ref, gate_ref, up_ref):
    nx = got_ref.shape[0]
    rows, width = tokens_ref.shape
    pair = 2 * (main + tail)
    total = sum(got_ref[x, : nx * rows, : wide + thin].astype(F32) for x in range(nx))
    found = [total[j * rows : (j + 1) * rows] for j in range(nx)]
    token_vals = tokens_ref[...].astype(F32)
    scale = row_scale_of(token_vals)
    gain = gain_ref[...].reshape(1, width)
    scaled = (token_vals * gain).astype(BF16).astype(F32)
    inner_grad = jnp.concatenate([f[:, :wide] for f in found] + [f[:, wide:] for f in found], axis=1)
    inner_grad = turned(inner_grad, 2, nx) * scale
    inner = jnp.sum(scaled * inner_grad, axis=1, keepdims=True)
    factor = scale * scale / width
    input_ref[...] = (gain * inner_grad - factor * token_vals * inner).astype(BF16)
    for q in range(nx):
        grad = got_ref[q, nx * rows :, :pair].astype(F32)
        start = nx * main + q * tail
        gate_ref[:, q * main : (q + 1) * main] = grad[:, :main]
        gate_ref[:, start : start + tail] = grad[:, 2 * main : 2 * main + tail]
        up_ref[:, q * main : (q + 1) * main] = grad[:, main : 2 * main]
        up_ref[:, start : start + tail] = grad[:, 2 * main + tail :]


def spread_kernel(main, tail, place_ref, *refs):
    sources, out_ref, got_ref = refs[:-2], refs[-2], refs[-1]
    nx, half, _ = got_ref.shape
    for s, source in enumerate(sources):
        got_ref[lax.rem(place_ref[2] - s + nx, nx)] = source[...]
    for q in range(nx):
        start = nx * main + q * tail
        for h in range(2):
            rows = slice(h * half, (h + 1) * half)
            out_ref[rows, q * main : (q + 1) * main] = got_ref[q, :, h * main : (h + 1) * main]
            out_ref[rows, start : start + tail] = got_ref[
                q, :, 2 * main + h * tail : 2 * main + (h + 1) * tail
            ]


def make_step(nc, nx, nl, ny, nk):
    def per_device(tokens, norm_gain, gate_weight, up_weight, hidden_grad):
        rows, width = tokens.shape
        feats, units = gate_weight.shape
        main, tail = share_sizes(units, nx)
        wide, thin = share_sizes(width, nx)
        pair = 2 * (main + tail)
        own_tokens = hidden_grad.shape[0]
        pool = nx * own_tokens
        nz = nc * nl
        place = jnp.stack([lax.axis_index(name) for name in ("l", "k", "x", "y")]).astype(jnp.int32)

        near = exchange(normalise(tokens, norm_gain, nx), "x").reshape(nx * rows, width)
        table = lax.all_gather(near, ("y", "k"), axis=0, tiled=True)

        cut = feats // 2
        early = lax.ppermute(
            pack_weights(nx, gate_weight, up_weight, cut), ("c", "l", "k"), both_ways(nz)
        )
        own = exchange(pack_weights(nx, gate_weight, up_weight, feats), "x")
        early = exchange(pack_grads(nx, early, hidden_grad), "x")
        late = lax.ppermute(own[:, cut:], ("c", "l", "k"), both_ways(nz))
        table, early, late = lax.optimization_barrier((table, early, late))
        grads = sort_grads(early, cut, own_tokens, rows)

        found, cots, keep, give = forward(place, table, own, early, late, grads, ny, pool)
        taken = lax.ppermute(give, "k", [(0, 1), (1, 0)])
        grad = gradient(table, cots, nx, nl, nc)
        taken, grad = lax.optimization_barrier((taken, grad))
        grad = lax.psum_scatter(grad, ("c", "l"), scatter_dimension=0, tiled=True)

        def term(i):
            return keep[i].astype(F32) + taken[i].astype(F32)

        hidden = list(sort_hidden(place, found, nx, rows))
        partial = term(0).astype(BF16)
        for i in range(1, ny // 2):
            partial = lax.ppermute(partial, ("y", "k"), both_ways(ny))
            if i < nx:
                hidden[i] = lax.ppermute(hidden[i], "x", ring(nx, i))
                partial, hidden[i] = lax.optimization_barrier((partial, hidden[i]))
            partial = (partial.astype(F32) + term(i)).astype(BF16)
        for i in range(ny // 2, nx):
            hidden[i] = lax.ppermute(hidden[i], "x", ring(nx, i))
        step = partial.shape[0] // 2
        lower, upper = partial[:step], partial[step:]
        core = lax.axis_index("k")
        near = lax.ppermute(
            jnp.where(core == 0, upper, lower), ("y", "k"),
            [(2 * y, 2 * y + 1) for y in range(ny)]
            + [(2 * y + 1, 2 * ((y - 1) % ny)) for y in range(ny)],
        )
        far = lax.ppermute(
            upper, ("y", "k"), [(2 * y + 1, 2 * ((y - 1) % ny) + 1) for y in range(ny)]
        )

        hidden = pl.pallas_call(
            functools.partial(spread_kernel, main, tail),
            out_shape=jax.ShapeDtypeStruct((own_tokens, units), BF16),
            in_specs=[SMEM] + [VMEM] * nx,
            out_specs=VMEM,
            scratch_shapes=[pltpu.VMEM((nx, own_tokens // 2, pair), BF16)],
            compiler_params=params(8),
        )(place, *hidden)
        hidden, near, far = lax.optimization_barrier((hidden, near, far))
        last = pl.pallas_call(
            functools.partial(gather_kernel, nx, rows, wide, thin),
            out_shape=jax.ShapeDtypeStruct((nx, nx * rows + feats // nc, -(-pair // 128) * 128), BF16),
            in_specs=[SMEM, VMEM, VMEM, VMEM, VMEM],
            out_specs=VMEM,
            compiler_params=params(24),
        )(place, near, far, partial, grad)
        last = exchange(last, "x")
        input_grad, gate_grad, up_grad = pl.pallas_call(
            functools.partial(finish_kernel, main, tail, wide, thin),
            out_shape=(
                jax.ShapeDtypeStruct((rows, width), BF16),
                jax.ShapeDtypeStruct((feats // nc, units), F32),
                jax.ShapeDtypeStruct((feats // nc, units), F32),
            ),
            in_specs=[VMEM, VMEM, VMEM],
            out_specs=(VMEM, VMEM, VMEM),
            compiler_params=params(16),
        )(last, tokens, norm_gain)
        return (hidden, input_grad, gate_grad, up_grad)

    return per_device


def solution(mesh):
    fine = split_fsdp(mesh)
    return jax.shard_map(
        make_step(*fine.devices.shape),
        mesh=fine,
        in_specs=(
            P(("c", "x", "l", "y", "k"), None),
            P(),
            P(("x", "l"), ("y", "k")),
            P(("x", "l"), ("y", "k")),
            P(("c", "x", "l"), ("y", "k")),
        ),
        out_specs=(
            P(("c", "x", "l"), ("y", "k")),
            P(("c", "x", "l", "y", "k"), None),
            P(("x", "l", "c"), ("y", "k")),
            P(("x", "l", "c"), ("y", "k")),
        ),
        check_vma=False,
    )
```

```python
import functools

import jax
import jax.numpy as jnp
from jax import lax
from jax.experimental import pallas as pl
from jax.experimental.pallas import tpu as pltpu
from jax.sharding import Mesh
from jax.sharding import PartitionSpec as P

ROOT_TWO_PI = 0.7978845608028654
CUBIC = 0.044715
BF16 = jnp.bfloat16
F32 = jnp.float32
VMEM = pl.BlockSpec(memory_space=pltpu.VMEM)
SMEM = pl.BlockSpec(memory_space=pltpu.SMEM)
ANY = pl.BlockSpec(memory_space=pl.ANY)


def split_fsdp(mesh):
    cuts, fsdp, tensor = mesh.devices.shape
    return Mesh(
        mesh.devices.reshape(cuts, fsdp // 2, 2, tensor // 2, 2), ("c", "x", "l", "y", "k")
    )


def ring(size, shift):
    return [(i, (i + shift) % size) for i in range(size)]


def both_ways(size):
    return [(2 * i, 2 * ((i + 1) % size)) for i in range(size)] + [
        (2 * i + 1, 2 * ((i - 1) % size) + 1) for i in range(size)
    ]


def exchange(value, axis):
    return lax.all_to_all(value, axis, split_axis=0, concat_axis=0, tiled=True)


def params(mib):
    return pltpu.CompilerParams(vmem_limit_bytes=mib * 1024 * 1024)


def share_sizes(units, parts):
    part = units // parts
    main = part // 128 * 128
    return main, part - main


def put_pair(out_ref, q, rows, a, b, main, tail, parts):
    out_ref[q, rows, 0:main] = a[:, q * main : (q + 1) * main]
    out_ref[q, rows, main : 2 * main] = b[:, q * main : (q + 1) * main]
    start = parts * main + q * tail
    out_ref[q, rows, 2 * main : 2 * main + tail] = a[:, start : start + tail]
    out_ref[q, rows, 2 * main + tail : 2 * (main + tail)] = b[:, start : start + tail]


def pack_weights_kernel(main, tail, parts, gate_ref, up_ref, out_ref):
    rows = slice(0, out_ref.shape[1])
    for q in range(parts):
        put_pair(out_ref, q, rows, gate_ref.at[rows], up_ref.at[rows], main, tail, parts)


def pack_weights(parts, gate, up, rows):
    main, tail = share_sizes(gate.shape[1], parts)
    return pl.pallas_call(
        functools.partial(pack_weights_kernel, main, tail, parts),
        out_shape=jax.ShapeDtypeStruct((parts, rows, 2 * (main + tail)), BF16),
        in_specs=[VMEM, VMEM],
        out_specs=VMEM,
        compiler_params=params(16),
    )(gate, up)


def pack_grads_kernel(main, tail, parts, weights_ref, grad_ref, out_ref):
    cut = weights_ref.shape[1]
    half = grad_ref.shape[0] // 2
    out_ref[:, 0:cut, :] = weights_ref[...]
    for q in range(parts):
        put_pair(
            out_ref, q, slice(cut, cut + half),
            grad_ref.at[0:half], grad_ref.at[half : 2 * half], main, tail, parts,
        )


def pack_grads(parts, weights, grads):
    main, tail = share_sizes(grads.shape[1], parts)
    rows = weights.shape[1] + grads.shape[0] // 2 + 32
    return pl.pallas_call(
        functools.partial(pack_grads_kernel, main, tail, parts),
        out_shape=jax.ShapeDtypeStruct((parts, rows, 2 * (main + tail)), BF16),
        in_specs=[VMEM, VMEM],
        out_specs=VMEM,
        compiler_params=params(16),
    )(weights, grads)


def activate(gate, upward, cotangent):
    square = gate * gate
    tangent = jnp.tanh(ROOT_TWO_PI * (gate + CUBIC * square * gate))
    active = 0.5 * gate * (1.0 + tangent)
    slope = 0.5 * (1.0 + tangent) + 0.5 * gate * (1.0 - tangent * tangent) * ROOT_TWO_PI * (
        1.0 + 3.0 * CUBIC * square
    )
    hidden = (active * upward).astype(BF16)
    return hidden, (cotangent * upward * slope).astype(BF16), (cotangent * active).astype(BF16)


def split_index(value, size, top):
    factor = (1 << 20) // size + 1
    assert all(i * factor >> 20 == i // size for i in range(top))
    high = (value * factor) >> 20
    return high, value - high * size


def shuffle(pool, outer, inner, rows):
    index = lax.broadcasted_iota(jnp.int32, (pool, 1), 0)
    high, rest = split_index(index, inner * rows, pool)
    mid, low = split_index(rest, rows, inner * rows)
    source = mid * (outer * rows) + high * rows + low
    columns = lax.broadcasted_iota(jnp.int32, (pool, pool), 1)
    return (columns == source).astype(F32).astype(BF16)


SORTED = 4


def sort_grads_kernel(main, tail, cut, rows_each, raw_ref, out_ref):
    blocks = raw_ref.shape[0]
    size = SORTED * rows_each
    half = out_ref.shape[0] // (2 * blocks)
    order = shuffle(blocks * size, SORTED, blocks, rows_each)
    for g in range(2 * half // size):
        h, at = g * size // half, cut + g * size % half
        found = [raw_ref[x, at : at + size, :] for x in range(blocks)]
        found = jnp.concatenate(found, axis=0)
        rows = slice(g * blocks * size, (g + 1) * blocks * size)
        for lanes, first, width in (
            (slice(0, main), h * main, main), (slice(main, main + tail), 2 * main + h * tail, tail)
        ):
            out_ref[rows, lanes] = jnp.dot(
                order, found[:, first : first + width], preferred_element_type=F32
            ).astype(BF16)


def sort_grads(raw, cut, own_tokens, rows_each):
    blocks, _, pair = raw.shape
    main = pair // 2 // 128 * 128
    return pl.pallas_call(
        functools.partial(sort_grads_kernel, main, pair // 2 - main, cut, rows_each),
        out_shape=jax.ShapeDtypeStruct((blocks * own_tokens, pair // 2), BF16),
        in_specs=[VMEM],
        out_specs=VMEM,
        compiler_params=params(16),
    )(raw)


def sort_hidden_kernel(main, tail, rows_each, place_ref, found_ref, *refs):
    outs, got_ref = refs[:-1], refs[-1]
    blocks = len(outs)
    half = outs[0].shape[0]
    me = place_ref[2]
    size = SORTED * rows_each
    order = shuffle(blocks * size, blocks, SORTED, rows_each)
    for g in range(2 * half // size):
        h, at = g * size // half, g * size % half
        rows = slice(g * blocks * size, (g + 1) * blocks * size)
        got = jnp.dot(order, found_ref[rows, :], preferred_element_type=F32)
        got_ref[...] = got.astype(BF16)
        for s, out_ref in enumerate(outs):
            x = lax.rem(me + s, blocks)
            block = got_ref[pl.ds(pl.multiple_of(x * size, 16), size), :]
            out_ref[at : at + size, h * main : (h + 1) * main] = block[:, :main]
            first = 2 * main + h * tail
            out_ref[at : at + size, first : first + tail] = block[:, main:]


def sort_hidden(place, found, blocks, rows_each):
    pool, part = found.shape
    main = part // 128 * 128
    out = jax.ShapeDtypeStruct((pool // blocks // 2, 2 * part), BF16)
    return pl.pallas_call(
        functools.partial(sort_hidden_kernel, main, part - main, rows_each),
        out_shape=(out,) * blocks,
        in_specs=[SMEM, VMEM],
        out_specs=(VMEM,) * blocks,
        scratch_shapes=[pltpu.VMEM((blocks * SORTED * rows_each, part), BF16)],
        compiler_params=params(16),
    )(place, found)


def forward_kernel(
    chunk, main, tail, place_ref, table_any, own_ref, early_ref, late_ref, grads_ref,
    found_ref, cots_ref, keep_ref, give_ref, table_ref, matrix, sems,
):
    blocks, feats, pair = own_ref.shape
    cut = feats - late_ref.shape[1]
    pool, width = table_ref.shape
    low, core, me = place_ref[0], place_ref[1], place_ref[3]
    chain, step, _ = keep_ref.shape
    tables = []
    for first in range(0, pool, chunk):
        rows = pl.ds(first, chunk)
        tables.append(
            pltpu.make_async_copy(table_any.at[rows], table_ref.at[rows], sems.at[first // chunk])
        )
        tables[-1].start()
    near = low * (width // 2)
    far = (1 - low) * (width // 2)
    for x in range(blocks):
        for first, size, rows in (
            (near + x * feats, feats, own_ref[x]),
            (far + x * feats, cut, early_ref[x, :cut, :]),
            (far + x * feats + cut, feats - cut, late_ref[x]),
        ):
            matrix[pl.ds(pl.multiple_of(first, 16), size), :] = rows
    for first in range(0, pool, chunk):
        rows = slice(first, first + chunk)
        tables[first // chunk].wait()
        both = jnp.dot(table_ref[rows, :], matrix[...], preferred_element_type=F32)
        grads = grads_ref[rows, :].astype(F32)
        hidden, gate_cot, up_cot = activate(
            both[:, :main], both[:, main : 2 * main], grads[:, :main]
        )
        found_ref[rows, :main] = hidden
        cots_ref[rows, :main] = gate_cot
        cots_ref[rows, main : 2 * main] = up_cot
        rest = both[:, 2 * main :]
        hidden, gate_cot, up_cot = activate(rest[:, :tail], rest[:, tail:], grads[:, main:])
        found_ref[rows, main:] = hidden
        cots_ref[rows, 2 * main : 2 * main + tail] = gate_cot
        cots_ref[rows, 2 * main + tail :] = up_cot
        partial = lax.dot_general(
            cots_ref[rows, :], matrix[...], (((1,), (1,)), ((), ())), preferred_element_type=F32
        )
        for j in range(chunk // step):
            block = partial[j * step : (j + 1) * step].astype(BF16)
            ahead = lax.rem(first // step + j - me + 2 * chain, 2 * chain)
            right = ahead < chain
            slot = jnp.where(right, chain - 1 - ahead, ahead - chain)
            kept = right == (core == 0)

            @pl.when(kept)
            def _():
                keep_ref[slot] = block

            @pl.when(jnp.logical_not(kept))
            def _():
                give_ref[slot] = block


def forward(place, table, own, early, late, grads, ny, chunk):
    pool, width = table.shape
    _, _, pair = own.shape
    part = pair // 2
    main = part // 128 * 128
    step = pool // ny
    return pl.pallas_call(
        functools.partial(forward_kernel, chunk, main, part - main),
        out_shape=(
            jax.ShapeDtypeStruct((pool, part), BF16),
            jax.ShapeDtypeStruct((pool, pair), BF16),
            jax.ShapeDtypeStruct((ny // 2, step, width), BF16),
            jax.ShapeDtypeStruct((ny // 2, step, width), BF16),
        ),
        in_specs=[SMEM, ANY, VMEM, VMEM, VMEM, VMEM],
        out_specs=(VMEM, VMEM, VMEM, VMEM),
        scratch_shapes=[
            pltpu.VMEM((pool, width), BF16),
            pltpu.VMEM((width, pair), BF16),
            pltpu.SemaphoreType.DMA((pool // chunk,)),
        ],
        compiler_params=params(44),
        cost_estimate=pl.CostEstimate(
            flops=4 * pool * width * pair, bytes_accessed=2 * (2 * pool * width + width * pair), transcendentals=0
        ),
    )(place, table, own, early, late, grads)


def gradient_kernel(nx, nl, nc, table_ref, cots_ref, out_any, total, ready, sems):
    width = table_ref.shape[1]
    span = width // nl
    piece = span // (nx * nc)
    block = nx * piece
    copies = []
    for l in range(nl):
        total[...] = lax.dot_general(
            table_ref[:, l * span : (l + 1) * span], cots_ref[...], (((0,), (0,)), ((), ())),
            preferred_element_type=F32,
        )
        for c in range(nc):
            found = [total[(x * nc + c) * piece : (x * nc + c + 1) * piece, :] for x in range(nx)]
            z = c * nl + l
            ready[z] = jnp.concatenate(found, axis=0).astype(BF16)
            copies.append(
                pltpu.make_async_copy(
                    ready.at[z], out_any.at[pl.ds(z * block, block)], sems.at[z]
                )
            )
            copies[-1].start()
    for copy in copies:
        copy.wait()


def gradient(table, cots, nx, nl, nc):
    pool, width = table.shape
    pair = cots.shape[1]
    return pl.pallas_call(
        functools.partial(gradient_kernel, nx, nl, nc),
        out_shape=jax.ShapeDtypeStruct((width, pair), BF16),
        in_specs=[VMEM, VMEM],
        out_specs=ANY,
        scratch_shapes=[
            pltpu.VMEM((width // nl, pair), F32),
            pltpu.VMEM((nl * nc, width // (nl * nc), pair), BF16),
            pltpu.SemaphoreType.DMA((nl * nc,)),
        ],
        compiler_params=params(32),
        cost_estimate=pl.CostEstimate(
            flops=2 * pool * width * pair, bytes_accessed=2 * (pool * width + width * pair), transcendentals=0
        ),
    )(table, cots)


def row_scale_of(token_vals):
    mean = jnp.mean(token_vals * token_vals, axis=1, keepdims=True)
    return lax.rsqrt(mean + 1e-06).astype(BF16).astype(F32)


def turned(value, outer, inner):
    size = value.shape[1] // (outer * inner)
    blocks = [(o * inner + i) * size for i in range(inner) for o in range(outer)]
    return jnp.concatenate([value[:, at : at + size] for at in blocks], axis=1)


def normalise_kernel(tokens_ref, gain_ref, out_ref):
    token_vals = tokens_ref[...].astype(F32)
    gain = gain_ref[...].reshape(1, tokens_ref.shape[1])
    scaled = (token_vals * gain).astype(BF16).astype(F32)
    normed = turned(scaled * row_scale_of(token_vals), out_ref.shape[0], 2).astype(BF16)
    for i in range(out_ref.shape[0]):
        out_ref[i] = normed


def normalise(tokens, gain, copies):
    return pl.pallas_call(
        normalise_kernel,
        out_shape=jax.ShapeDtypeStruct((copies, *tokens.shape), BF16),
        in_specs=[VMEM, VMEM],
        out_specs=VMEM,
        compiler_params=params(8),
    )(tokens, gain)


def gather_kernel(nx, rows, wide, thin, place_ref, near_ref, far_ref, sums_ref, grad_ref, out_ref):
    mine = sums_ref[0 : near_ref.shape[0], :].astype(F32)
    total = near_ref[...].astype(F32) + jnp.where(place_ref[1] == 0, mine, far_ref[...].astype(F32))
    grad = grad_ref[...].astype(F32)
    piece = grad.shape[0] // nx
    for x in range(nx):
        mine = total[x * rows : (x + 1) * rows]
        found = []
        for j in range(nx):
            start = nx * wide + j * thin
            found.append(
                jnp.concatenate(
                    [mine[:, j * wide : (j + 1) * wide], mine[:, start : start + thin]], axis=1
                )
            )
        out_ref[x, : nx * rows, : wide + thin] = jnp.concatenate(found, axis=0).astype(BF16)
        out_ref[x, nx * rows :, : grad.shape[1]] = grad[x * piece : (x + 1) * piece].astype(BF16)


def finish_kernel(main, tail, wide, thin, got_ref, tokens_ref, gain_ref, input_ref, gate_ref, up_ref):
    nx = got_ref.shape[0]
    rows, width = tokens_ref.shape
    pair = 2 * (main + tail)
    total = sum(got_ref[x, : nx * rows, : wide + thin].astype(F32) for x in range(nx))
    found = [total[j * rows : (j + 1) * rows] for j in range(nx)]
    token_vals = tokens_ref[...].astype(F32)
    scale = row_scale_of(token_vals)
    gain = gain_ref[...].reshape(1, width)
    scaled = (token_vals * gain).astype(BF16).astype(F32)
    inner_grad = jnp.concatenate([f[:, :wide] for f in found] + [f[:, wide:] for f in found], axis=1)
    inner_grad = turned(inner_grad, 2, nx) * scale
    inner = jnp.sum(scaled * inner_grad, axis=1, keepdims=True)
    factor = scale * scale / width
    input_ref[...] = (gain * inner_grad - factor * token_vals * inner).astype(BF16)
    for q in range(nx):
        grad = got_ref[q, nx * rows :, :pair].astype(F32)
        start = nx * main + q * tail
        gate_ref[:, q * main : (q + 1) * main] = grad[:, :main]
        gate_ref[:, start : start + tail] = grad[:, 2 * main : 2 * main + tail]
        up_ref[:, q * main : (q + 1) * main] = grad[:, main : 2 * main]
        up_ref[:, start : start + tail] = grad[:, 2 * main + tail :]


def spread_kernel(main, tail, place_ref, *refs):
    sources, out_ref, got_ref = refs[:-2], refs[-2], refs[-1]
    nx, half, _ = got_ref.shape
    for s, source in enumerate(sources):
        got_ref[lax.rem(place_ref[2] - s + nx, nx)] = source[...]
    for q in range(nx):
        start = nx * main + q * tail
        for h in range(2):
            rows = slice(h * half, (h + 1) * half)
            out_ref[rows, q * main : (q + 1) * main] = got_ref[q, :, h * main : (h + 1) * main]
            out_ref[rows, start : start + tail] = got_ref[
                q, :, 2 * main + h * tail : 2 * main + (h + 1) * tail
            ]


def make_step(nc, nx, nl, ny, nk):
    def per_device(tokens, norm_gain, gate_weight, up_weight, hidden_grad):
        rows, width = tokens.shape
        feats, units = gate_weight.shape
        main, tail = share_sizes(units, nx)
        wide, thin = share_sizes(width, nx)
        pair = 2 * (main + tail)
        own_tokens = hidden_grad.shape[0]
        pool = nx * own_tokens
        nz = nc * nl
        place = jnp.stack([lax.axis_index(name) for name in ("l", "k", "x", "y")]).astype(jnp.int32)

        near = exchange(normalise(tokens, norm_gain, nx), "x").reshape(nx * rows, width)
        table = lax.all_gather(near, ("y", "k"), axis=0, tiled=True)

        cut = feats // 2
        early = lax.ppermute(
            pack_weights(nx, gate_weight, up_weight, cut), ("c", "l", "k"), both_ways(nz)
        )
        own = exchange(pack_weights(nx, gate_weight, up_weight, feats), "x")
        early = exchange(pack_grads(nx, early, hidden_grad), "x")
        late = lax.ppermute(own[:, cut:], ("c", "l", "k"), both_ways(nz))
        table, early, late = lax.optimization_barrier((table, early, late))
        grads = sort_grads(early, cut, own_tokens, rows)

        found, cots, keep, give = forward(place, table, own, early, late, grads, ny, pool // 2)
        taken = lax.ppermute(give, "k", [(0, 1), (1, 0)])
        grad = gradient(table, cots, nx, nl, nc)
        taken, grad = lax.optimization_barrier((taken, grad))
        grad = lax.psum_scatter(grad, ("c", "l"), scatter_dimension=0, tiled=True)

        def term(i):
            return keep[i].astype(F32) + taken[i].astype(F32)

        hidden = list(sort_hidden(place, found, nx, rows))
        partial = term(0).astype(BF16)
        for i in range(1, ny // 2):
            partial = lax.ppermute(partial, ("y", "k"), both_ways(ny))
            if i < nx:
                hidden[i] = lax.ppermute(hidden[i], "x", ring(nx, i))
                partial, hidden[i] = lax.optimization_barrier((partial, hidden[i]))
            partial = (partial.astype(F32) + term(i)).astype(BF16)
        for i in range(ny // 2, nx):
            hidden[i] = lax.ppermute(hidden[i], "x", ring(nx, i))
        step = partial.shape[0] // 2
        lower, upper = partial[:step], partial[step:]
        core = lax.axis_index("k")
        near = lax.ppermute(
            jnp.where(core == 0, upper, lower), ("y", "k"),
            [(2 * y, 2 * y + 1) for y in range(ny)]
            + [(2 * y + 1, 2 * ((y - 1) % ny)) for y in range(ny)],
        )
        far = lax.ppermute(
            upper, ("y", "k"), [(2 * y + 1, 2 * ((y - 1) % ny) + 1) for y in range(ny)]
        )

        hidden = pl.pallas_call(
            functools.partial(spread_kernel, main, tail),
            out_shape=jax.ShapeDtypeStruct((own_tokens, units), BF16),
            in_specs=[SMEM] + [VMEM] * nx,
            out_specs=VMEM,
            scratch_shapes=[pltpu.VMEM((nx, own_tokens // 2, pair), BF16)],
            compiler_params=params(8),
        )(place, *hidden)
        hidden, near, far = lax.optimization_barrier((hidden, near, far))
        last = pl.pallas_call(
            functools.partial(gather_kernel, nx, rows, wide, thin),
            out_shape=jax.ShapeDtypeStruct((nx, nx * rows + feats // nc, -(-pair // 128) * 128), BF16),
            in_specs=[SMEM, VMEM, VMEM, VMEM, VMEM],
            out_specs=VMEM,
            compiler_params=params(24),
        )(place, near, far, partial, grad)
        last = exchange(last, "x")
        input_grad, gate_grad, up_grad = pl.pallas_call(
            functools.partial(finish_kernel, main, tail, wide, thin),
            out_shape=(
                jax.ShapeDtypeStruct((rows, width), BF16),
                jax.ShapeDtypeStruct((feats // nc, units), F32),
                jax.ShapeDtypeStruct((feats // nc, units), F32),
            ),
            in_specs=[VMEM, VMEM, VMEM],
            out_specs=(VMEM, VMEM, VMEM),
            compiler_params=params(16),
        )(last, tokens, norm_gain)
        return (hidden, input_grad, gate_grad, up_grad)

    return per_device


def solution(mesh):
    fine = split_fsdp(mesh)
    return jax.shard_map(
        make_step(*fine.devices.shape),
        mesh=fine,
        in_specs=(
            P(("c", "x", "l", "y", "k"), None),
            P(),
            P(("x", "l"), ("y", "k")),
            P(("x", "l"), ("y", "k")),
            P(("c", "x", "l"), ("y", "k")),
        ),
        out_specs=(
            P(("c", "x", "l"), ("y", "k")),
            P(("c", "x", "l", "y", "k"), None),
            P(("x", "l", "c"), ("y", "k")),
            P(("x", "l", "c"), ("y", "k")),
        ),
        check_vma=False,
    )
```
